128 devices in a mesh: stream: 4 (over z), tile: 32 (over y, x, core).
Axes of the slice: x: 4, y: 4, z: 4, core: 2. Of those that a mesh axis runs over, the one named last changes fastest.
Arguments:
- enthalpy: float32 [64, 64, 4096], P('stream', None, 'tile'), may hold values from -6 to 6
- velocity: float32 [64, 64, 4096], P('stream', None, 'tile'), may hold values from 0.05 to 0.35
- diffusivity: float32 [64, 64, 4096], P('stream', None, 'tile'), may hold values from 0.02 to 0.1
- wall_flux: float32 [64, 4096], P('stream', 'tile'), may hold values from 0.05 to 0.5
- profiles: float32 [64, 2097152], P(None, ('stream', 'tile')), may hold values from -6 to 6
- counts: int32 [128], P(('stream', 'tile')), may hold values from 1 to 16384, as said below
- owners: int32 [2097152], P(('stream', 'tile')), may hold values from 0 to 196607, as said below
- cells: int32 [2097152], P(('stream', 'tile')), may hold values from 0 to 131071, as said below
- radial_step: float32 [64, 64], replicated, may hold values from -1 to 1
- far_weights: float32 [64], replicated, may hold values from 0.05 to 0.3
- flux_weights: float32 [64], replicated, may hold values from -0.75 to 0.75
Outputs:
- new_enthalpy: float32 [64, 64, 4096], P('stream', None, 'tile')
- new_profiles: float32 [64, 786432], P(None, ('stream', 'tile'))
The draws below stay inside these ranges and needn't reach their ends.
Inputs may be any that keep to these rules, and one draw needn't show every extreme that they name: A tile's live bubbles fill its first counts slots; the counts of one group sum to 196608. `owners`: over the live slots of one group the entries are distinct and cover all 196608 balanced slots; entry // 6144 is the tile index of the device that holds the balanced slot, entry % 6144 the slot there. No tile has more than 512 live bubbles whose entries lie on one device. Entries of slots that are not live are arbitrary. `cells`: the cell's index (x * 64 + w) * 128 + s inside the home tile.
All inputs are finite; a program needn't handle non-finite values.
Results may differ from the reference program's by a relative error of at most 0.0001.
Values sent between devices are 32-bit elements; how exact they have to be, the bound alone decides.
No kernel may reach another device: no remote copies, remote signals or barrier semaphores. Data moves between devices by JAX's collectives and lax.ppermute only.
A program may use at most 128 MiB of HBM per device.

```python
import math
import jax
import jax.numpy as jnp
from jax import lax

P_SIZE = 64
NW = 64
SUB = 16
CX = 16
CS = 128
CAP = 16384
OWN = 6144
NX = 64
NS = 4096
BUB = 2097152
N_STREAM = 4
N_TILE = 32


def group_layout(key):
    busy_tiles = N_TILE // 8
    other_tiles = N_TILE - busy_tiles
    spread = N_TILE * CAP // 4 - other_tiles

    def one_group(group_key):
        order_key, weight_key = jax.random.split(group_key)
        order = jax.random.permutation(order_key, N_TILE)
        weights = jax.random.randint(weight_key, (other_tiles,), 2, 5)
        running = jnp.cumsum(weights)
        upper = spread * running // running[-1]
        lower = jnp.concatenate([jnp.zeros((1,), jnp.int32), upper[:-1]])
        tile_sizes = jnp.concatenate([jnp.full((busy_tiles,), CAP, jnp.int32), (1 + upper - lower).astype(jnp.int32)])
        return jnp.zeros((N_TILE,), jnp.int32).at[order].set(tile_sizes)
    tile_counts = jax.vmap(one_group)(jax.random.split(key, N_STREAM))
    prefix = jnp.cumsum(tile_counts, axis=1) - tile_counts
    slot_index = jnp.arange(CAP, dtype=jnp.int32)
    is_live = slot_index[None, None, :] < tile_counts[:, :, None]
    order_rank = jnp.where(is_live, prefix[:, :, None] + slot_index[None, None, :], 0)
    holder = order_rank % N_TILE
    position = order_rank // N_TILE
    perm_keys = jax.random.split(jax.random.fold_in(key, 101), N_STREAM * N_TILE)
    shuffles = jax.vmap(lambda perm_key: jax.random.permutation(perm_key, OWN))(perm_keys).reshape(N_STREAM, N_TILE, OWN)
    group_index = jnp.arange(N_STREAM, dtype=jnp.int32)[:, None, None]
    chosen = shuffles[group_index, holder, position]
    return (tile_counts, is_live, holder * OWN + chosen)


def draw_counts(key, part):
    tile_counts, is_live, owner_slots = group_layout(key)
    return tile_counts.reshape(-1)


def draw_owners(key, part):
    tile_counts, is_live, owner_slots = group_layout(key)
    key = jax.random.fold_in(key, 2)
    filler = jax.random.randint(key, owner_slots.shape, 0, N_TILE * OWN)
    return jnp.where(is_live, owner_slots, filler).reshape(-1)


def draw_cells(key, part):
    key = jax.random.fold_in(key, 3)
    first_key, second_key, third_key, fourth_key = jax.random.split(key, 4)
    total_slots = N_STREAM * N_TILE * CAP
    along = jax.random.randint(first_key, (total_slots,), 0, CX)
    depth = jnp.minimum(jax.random.randint(second_key, (total_slots,), 0, NW), jax.random.randint(third_key, (total_slots,), 0, NW))
    across = jax.random.randint(fourth_key, (total_slots,), 0, CS)
    index_cells = (along * NW + depth) * CS + across
    return index_cells.at[0].set(CX * NW * CS - 1).at[1].set(0)


def draw_radial_step(key, part):
    key = jax.random.fold_in(key, 4)
    diag_key, off_key = jax.random.split(key)
    diagonal = jax.random.uniform(diag_key, (P_SIZE,), jnp.float32, 0.3, 0.5)
    offdiag = jax.random.normal(off_key, (P_SIZE, P_SIZE), jnp.float32) * (0.2 / math.sqrt(P_SIZE))
    on_diagonal = jnp.arange(P_SIZE)[:, None] == jnp.arange(P_SIZE)[None, :]
    return jnp.clip(jnp.where(on_diagonal, diagonal[:, None], offdiag), -1.0, 1.0)


def steps_of(stream_key, shape, cuts, smallest, high):
    loudness, own = 1.0, jax.random.fold_in(stream_key, 6)
    for axis_at, parts in cuts:
        draws = jnp.exp(jax.random.uniform(jax.random.fold_in(own, axis_at), (parts,), jnp.float32, smallest / len(cuts), high / len(cuts)))
        loudness = loudness * jnp.repeat(draws, shape[axis_at] // parts).reshape([-1 if axis == axis_at else 1 for axis in range(len(shape))])
    return loudness


def normal_values(stream_key, shape, width, reach, pieces=(), kind=jnp.bfloat16):
    level = steps_of(stream_key, shape, pieces, -0.22, 0.18) if pieces else 1.0
    values = jax.random.normal(stream_key, shape, jnp.float32) * width * level
    return jnp.minimum(jnp.maximum(values, -reach), reach).astype(kind)


def setup_inputs(seed: int = 0) -> dict:
    arg_keys = jax.random.split(jax.random.key(seed), 12)
    return {
        "enthalpy": normal_values(arg_keys[0], (NX, NW, NS), 1.0, 6.0, ((0, 4), (2, 32)), jnp.float32),
        "velocity": jnp.clip(0.05 + 0.29999999 * jax.random.uniform(arg_keys[1], (NX, NW, NS), jnp.float32) ** steps_of(arg_keys[1], (NX, NW, NS), ((0, 4), (2, 32)), -0.2, 0.2), 0.05, 0.35),
        "diffusivity": jnp.clip(jnp.exp(math.log(0.1) - 1.609438 * jax.random.uniform(arg_keys[2], (NX, NW, NS), jnp.float32) ** steps_of(arg_keys[2], (NX, NW, NS), ((0, 4), (2, 32)), -0.2, 0.2)), 0.02, 0.1),
        "wall_flux": jnp.clip(jnp.exp(math.log(0.5) - 2.3025851 * jax.random.uniform(arg_keys[3], (NX, NS), jnp.float32) ** steps_of(arg_keys[3], (NX, NS), ((0, 4), (1, 32)), -0.2, 0.2)), 0.05, 0.5),
        "profiles": normal_values(arg_keys[4], (P_SIZE, BUB), 1.0, 6.0, ((1, 128),), jnp.float32),
        "counts": draw_counts(jax.random.fold_in(arg_keys[11], 71), 0),
        "owners": draw_owners(jax.random.fold_in(arg_keys[11], 71), 0),
        "cells": draw_cells(jax.random.fold_in(arg_keys[11], 71), 0),
        "radial_step": draw_radial_step(jax.random.fold_in(arg_keys[11], 71), 0),
        "far_weights": jnp.clip(jnp.exp(jax.random.uniform(arg_keys[9], (P_SIZE,), jnp.float32, math.log(0.05), math.log(0.3))), 0.05, 0.3),
        "flux_weights": normal_values(arg_keys[10], (P_SIZE,), P_SIZE ** -0.5, 0.75, (), jnp.float32),
    }


latent_share = 0.5


def advance(radial_step, far_weights, flux_weights, profile_state, far_temp):
    def substep(substep_index, carried):
        current, heat_rate = carried
        current = jnp.dot(radial_step, current, precision=lax.Precision.HIGHEST, preferred_element_type=jnp.float32) + far_weights[:, None] * far_temp[None, :] + 0.25 * jnp.tanh(current)
        heat_rate = heat_rate + jnp.dot(flux_weights, current, precision=lax.Precision.HIGHEST, preferred_element_type=jnp.float32)
        return current, heat_rate

    start_heat = jnp.zeros(far_temp.shape, jnp.float32)
    current, heat_rate = lax.fori_loop(0, SUB, substep, (profile_state, start_heat))
    return current, heat_rate / SUB


def stencil(enthalpy, x_lower, x_upper, s_lower, s_upper, velocity, diffusivity, wall_flux):
    wall_low = jnp.concatenate([enthalpy[:, :1], enthalpy[:, :-1]], axis=1)
    wall_high = jnp.concatenate([enthalpy[:, 1:], enthalpy[:, -1:]], axis=1)
    laplace = (x_lower + x_upper) + (wall_low + wall_high) + (s_lower + s_upper) - 6.0 * enthalpy
    stepped = enthalpy + diffusivity * laplace - velocity * (enthalpy - x_lower)
    return stepped.at[:, 0, :].add(wall_flux)


def reference(enthalpy, velocity, diffusivity, wall_flux, profiles, counts, owners, cells, radial_step, far_weights, flux_weights):
    slot_count = N_STREAM * N_TILE * CAP
    bubble = jnp.arange(slot_count, dtype=jnp.int32)
    device = bubble // CAP
    is_live = (bubble % CAP) < counts[device]
    stream_index = device // N_TILE
    tile_index = device % N_TILE
    cell_x = stream_index * CX + cells // (NW * CS)
    cell_w = (cells // CS) % NW
    cell_s = tile_index * CS + cells % CS
    far_all = enthalpy[cell_x, cell_w, cell_s]
    balanced = N_TILE * OWN
    target = jnp.where(is_live, stream_index * balanced + owners, N_STREAM * balanced).astype(jnp.int32)
    source = jnp.zeros((N_STREAM * balanced,), jnp.int32).at[target].set(bubble, mode="drop")
    final_state, heat_rate = advance(radial_step, far_weights, flux_weights, profiles[:, source], far_all[source])
    heat_home = jnp.zeros((slot_count,), jnp.float32).at[source].set(heat_rate)
    padded = jnp.pad(enthalpy, ((1, 1), (0, 0), (0, 0)))
    x_lower = padded[:-2]
    x_upper = padded[2:]
    s_lower = jnp.concatenate([enthalpy[..., -1:], enthalpy[..., :-1]], axis=2)
    s_upper = jnp.concatenate([enthalpy[..., 1:], enthalpy[..., :1]], axis=2)
    stepped = stencil(enthalpy, x_lower, x_upper, s_lower, s_upper, velocity, diffusivity, wall_flux)
    new_enthalpy = stepped.at[cell_x, cell_w, cell_s].add(latent_share * heat_home)
    return new_enthalpy, final_state
```

```python
import jax
import jax.numpy as jnp
from jax import lax
from jax.experimental import pallas as pl
from jax.experimental.pallas import tpu as pltpu
from jax.sharding import PartitionSpec as P

SUB = 16
PTS = 64
NT = 32
CAP = 16384
OWN = 6144
MSG = 512
HALF = MSG // 2
BLK = 256
NBLK = CAP // BLK
STRIDE = MSG + 16
ROWS = 1024
OWN2 = OWN // 2

F32, BF16, I32 = jnp.float32, jnp.bfloat16, jnp.int32
NTD = (((1,), (1,)), ((), ()))


def iota(shape, dim):
    return lax.broadcasted_iota(I32, shape, dim)


def split(x):
    high = x.astype(BF16)
    return high, (x - high.astype(F32)).astype(BF16)


def dot(a, b):
    return jnp.dot(a, b, preferred_element_type=F32)


def dot_nt(a, b):
    return lax.dot_general(a, b, NTD, preferred_element_type=F32)


def route_kernel(
    count_ref, owners_ref, cells_ref, prof_ref,
    rows_ref, meta_ref, lanes_ref,
    pos_s, m0_s, m1_s, m2_s, m3_s, m4_s, sorted_a, sorted_b, bucket, tab_v, tab_s, sem,
):
    count = count_ref[0]
    slot = iota((NBLK, BLK), 0) * BLK + iota((NBLK, BLK), 1)
    owners = owners_ref[...]
    dest = jnp.floor((owners.astype(F32) + 0.5) * (1.0 / OWN)).astype(I32)
    within = owners - dest * OWN
    live = slot < count
    dest = jnp.where(live, dest, NT)
    cells = cells_ref[...]
    m0_s[...] = (cells & 127).astype(F32)
    m1_s[...] = ((cells >> 7) & 255).astype(F32)
    m2_s[...] = (cells >> 15).astype(F32)
    m3_s[...] = (within & 255).astype(F32)
    m4_s[...] = (within >> 8).astype(F32)

    sub, lane = iota((BLK, BLK), 0), iota((BLK, BLK), 1)
    one, nil = jnp.ones((), F32), jnp.zeros((), F32)
    before = jnp.where(sub < lane, one, nil).astype(BF16)
    same_block = (sub >> 5) == (lane >> 5)
    same_dest = (sub & 31) == (lane & 31)
    seg_left = jnp.where(same_block & (lane < sub), one, nil).astype(BF16)
    seg_right = jnp.where(same_block & (sub < lane), one, nil).astype(BF16)
    base_right = jnp.where(same_dest & ((sub >> 5) < (lane >> 5)), one, nil).astype(BF16)
    all_right = jnp.where(same_dest, one, nil).astype(BF16)
    ones_a = jnp.ones((8, BLK), BF16)
    ones_b = jnp.ones((BLK, 128), BF16)
    run = jnp.zeros((8, BLK), F32)
    for c in range(8):
        part = dest[8 * c : 8 * c + 8]
        hot = jnp.where(part[:, None, :] == iota((8, NT, BLK), 1), one, nil).reshape(BLK, BLK)
        hot_b = hot.astype(BF16)
        prefix = dot(hot_b, before)
        amount = dot(hot_b, ones_b)
        seg = dot(seg_left, amount.astype(BF16))
        seg2 = jnp.concatenate([seg, seg], axis=1)
        pos = jnp.sum((hot * (prefix + seg2)).reshape(8, NT, BLK), axis=1)
        pos_s[8 * c : 8 * c + 8] = jnp.where(live[8 * c : 8 * c + 8], pos, 511.0)
        amount_l = dot_nt(ones_a, hot_b)
        amount_lb = amount_l.astype(BF16)
        src = dot(amount_lb, seg_right)
        base = dot(amount_lb, base_right) + run
        run = run + dot(amount_lb, all_right)
        most = amount_l
        for shift in (1, 2, 4, 8, 16):
            most = jnp.maximum(most, pltpu.roll(most, BLK - shift, 1))
        first = iota((8, BLK), 1) & 31
        row8 = iota((8, BLK), 0)
        packed = jnp.where(row8 == 0, src, nil)
        packed = jnp.where(row8 == 1, base + (first * STRIDE).astype(F32), packed)
        packed = jnp.where(row8 == 2, amount_l, packed)
        packed = jnp.where(row8 == 3, most, packed)
        tab_v[8 * c : 8 * c + 8] = packed.astype(I32)
    copy = pltpu.make_async_copy(tab_v, tab_s, sem)
    copy.start()
    total = run

    zero8 = jnp.zeros((STRIDE, 128), F32)

    @pl.loop(0, NT)
    def _(d):
        bucket[pl.ds(pl.multiple_of(d * STRIDE, 8), STRIDE)] = zero8

    copy.wait()

    meta_rest = jnp.zeros((56, BLK), BF16)
    low_rest = jnp.zeros((64, BLK), BF16)
    row8 = iota((8, BLK), 0)

    def sort_block(j, out):
        x = prof_ref[:, pl.ds(pl.multiple_of(j * BLK, BLK), BLK)]
        high, low = split(x)
        meta = jnp.zeros((8, BLK), F32)
        for k, ref in enumerate((m0_s, m1_s, m2_s, m3_s, m4_s)):
            meta = jnp.where(row8 == k, ref[pl.ds(j, 1), :], meta)
        data = jnp.concatenate([high, meta.astype(BF16), meta_rest, low, low_rest], axis=0)
        place = pos_s[pl.ds(j, 1), :].astype(I32)
        perm = jnp.where(place == sub, one, nil).astype(BF16)
        got = dot_nt(perm, data)
        out[0:BLK] = got[:, :128] + got[:, 128:]

    def copy_block(j, inp):
        chunk = (j >> 3) * 8
        at = (j & 7) * NT
        most = tab_s[chunk + 3, at]

        @pl.when(most <= 8)
        def _():
            for d in range(NT):
                src = tab_s[chunk, at + d]
                dst = tab_s[chunk + 1, at + d]
                bucket[pl.ds(dst, 8)] = inp[pl.ds(src, 8)]

        @pl.when((most > 8) & (most <= 16))
        def _():
            for d in range(NT):
                src = tab_s[chunk, at + d]
                dst = tab_s[chunk + 1, at + d]
                bucket[pl.ds(dst, 16)] = inp[pl.ds(src, 16)]

        @pl.when(most > 16)
        def _():
            @pl.loop(0, NT)
            def _(d):
                src = tab_s[chunk, at + d]
                dst = tab_s[chunk + 1, at + d]

                @pl.loop(0, (tab_s[chunk + 2, at + d] + 7) >> 3)
                def _(k):
                    bucket[pl.ds(dst + 8 * k, 8)] = inp[pl.ds(src + 8 * k, 8)]

    sorted_a[BLK:] = jnp.zeros((16, 128), F32)
    sorted_b[BLK:] = jnp.zeros((16, 128), F32)
    pairs = (count + 2 * BLK - 1) // (2 * BLK)
    sort_block(0, sorted_a)

    @pl.loop(0, pairs)
    def _(p):
        sort_block(2 * p + 1, sorted_b)
        copy_block(2 * p, sorted_a)
        sort_block(jnp.minimum(2 * p + 2, NBLK - 1), sorted_a)
        copy_block(2 * p + 1, sorted_b)

    low_lanes = iota((HALF, 128), 1) < 64
    r8, l8 = iota((8, 128), 0), iota((8, 128), 1)
    pick = jnp.where((r8 == 0) & (l8 == 64), one, nil)
    pick = jnp.where((r8 == 1) & (l8 == 65), one, pick)
    pick = jnp.where((r8 == 1) & (l8 == 66), 256.0 * one, pick)
    pick = jnp.where((r8 == 2) & (l8 == 67), one, pick)
    pick = jnp.where((r8 == 2) & (l8 == 68), 256.0 * one, pick)
    pick = pick.astype(BF16)
    rank = iota((8, MSG), 1)
    rank_row = iota((8, MSG), 0)
    lane_dest = iota((8, BLK), 1)

    @pl.loop(0, NT)
    def _(d):
        at = pl.multiple_of(d * STRIDE, 8)
        lo = bucket[pl.ds(at, HALF)]
        hi = bucket[pl.ds(pl.multiple_of(at + HALF, 8), HALF)]
        rows_ref[d] = jnp.where(low_lanes, lo, pltpu.roll(hi, 64, 1))
        meta_ref[d] = jnp.where(low_lanes, pltpu.roll(lo, 64, 1), hi).astype(BF16)
        both = jnp.concatenate([lo, hi], axis=0).astype(BF16)
        nums = dot_nt(pick, both)
        mine = jnp.max(jnp.where(lane_dest == d, total, nil), axis=1, keepdims=True)
        valid = rank.astype(F32) < mine
        nums = jnp.where((rank_row == 2) & ~valid, float(OWN), nums)
        nums = jnp.where(rank_row == 3, jnp.where(valid, one, nil), nums)
        lanes_ref[d] = nums


def route(counts, owners, cells, profiles):
    vmem = pl.BlockSpec(memory_space=pltpu.VMEM)
    return pl.pallas_call(
        route_kernel,
        out_shape=(
            jax.ShapeDtypeStruct((NT, HALF, 128), F32),
            jax.ShapeDtypeStruct((NT, HALF, 128), BF16),
            jax.ShapeDtypeStruct((NT, 8, MSG), F32),
        ),
        in_specs=[pl.BlockSpec(memory_space=pltpu.SMEM), vmem, vmem, vmem],
        out_specs=(vmem, vmem, vmem),
        scratch_shapes=[pltpu.VMEM((NBLK, BLK), F32)] * 6
        + [pltpu.VMEM((BLK + 16, 128), F32)] * 2
        + [
            pltpu.VMEM((NT * STRIDE, 128), F32),
            pltpu.VMEM((64, BLK), I32),
            pltpu.SMEM((64, BLK), I32),
            pltpu.SemaphoreType.DMA,
        ],
        compiler_params=pltpu.CompilerParams(vmem_limit_bytes=40 * 2**20),
        name="route",
    )(counts, owners.reshape(NBLK, BLK), cells.reshape(NBLK, BLK), profiles)


def far_kernel(meta_ref, cells_ref, fw_ref, far_ref, add_ref):
    table = cells_ref[...]
    t0, t1 = split(table)
    table2 = jnp.concatenate([t0, t1], axis=1)
    one, nil = jnp.ones((), F32), jnp.zeros((), F32)
    fw = fw_ref[...]
    fw0, fw1 = split(fw)
    shape = (128, 128)
    sub, lane = iota(shape, 0), iota(shape, 1)
    ones8 = jnp.ones((8, 256), BF16)
    cell_lane = iota((HALF, 128), 1)

    def half(h):
        first = 64 if h else 0
        meta = meta_ref[0]
        s128 = jnp.where(sub == first, one, nil)
        r128 = jnp.where(sub == first + 1, one, nil) + jnp.where(sub == first + 2, 256.0 * one, nil)
        pick = jnp.concatenate([s128, r128], axis=1).astype(BF16)
        got = dot(meta, pick)
        s_b = got[:, :128].astype(I32)
        r_b = got[:, 128:].astype(I32)
        hot = jnp.concatenate(
            [jnp.where(r_b == cell_lane + 128 * k, one, nil).astype(BF16) for k in range(ROWS // 128)],
            axis=1,
        )
        val = dot(hot, table2)
        val = val[:, :128] + val[:, 128:]
        v0, v1 = split(jnp.where(s_b == cell_lane, val, nil))
        v = jnp.concatenate([v0, v1], axis=1)
        far = dot_nt(ones8, v)
        mask = (lane >= 64) if h else (lane < 64)
        w0 = jnp.where(mask, fw0.astype(F32), nil).astype(BF16)
        w1 = jnp.where(mask, fw1.astype(F32), nil).astype(BF16)
        return far, v, w0, w1

    far_a, va, a0, a1 = half(0)
    far_b, vb, b0, b1 = half(1)
    far_ref[0] = jnp.concatenate([far_a, far_b], axis=1)
    w = jnp.concatenate([jnp.concatenate([a0, a1], axis=1)] * 2, axis=0)
    u = jnp.concatenate([jnp.concatenate([b0, b1], axis=1)] * 2, axis=0)
    got = dot(va, w) + dot(vb, u)
    add_ref[0] = got[:, :128] + got[:, 128:]


def far_gather(meta, table, fw):
    return pl.pallas_call(
        far_kernel,
        grid=(NT,),
        out_shape=(
            jax.ShapeDtypeStruct((NT, 8, MSG), F32),
            jax.ShapeDtypeStruct((NT, HALF, 128), F32),
        ),
        in_specs=[
            pl.BlockSpec((1, HALF, 128), lambda d: (d, 0, 0)),
            pl.BlockSpec((ROWS, 128), lambda d: (0, 0)),
            pl.BlockSpec((1, 128), lambda d: (0, 0)),
        ],
        out_specs=(
            pl.BlockSpec((1, 8, MSG), lambda d: (d, 0, 0)),
            pl.BlockSpec((1, HALF, 128), lambda d: (d, 0, 0)),
        ),
        compiler_params=pltpu.CompilerParams(vmem_limit_bytes=24 * 2**20),
        cost_estimate=pl.CostEstimate(flops=16384 * 1024 * 512, bytes_accessed=8 << 20, transcendentals=0),
        name="far_gather",
    )(meta, table, fw)


def step_weights(radial_step):
    zero = jnp.zeros((PTS, PTS), F32)
    w = jnp.concatenate(
        [
            jnp.concatenate([radial_step.T, zero], axis=1),
            jnp.concatenate([zero, radial_step.T], axis=1),
        ],
        axis=0,
    )
    high = lax.reduce_precision(w, 8, 7)
    w0, w1 = high.astype(BF16), (w - high).astype(BF16)
    row = jnp.concatenate([w0, w1], axis=1)
    return jnp.concatenate([row, row], axis=0)


def flux_rows(flux_weights):
    zero = jnp.zeros((PTS,), F32)
    f = jnp.stack(
        [jnp.concatenate([flux_weights, zero]), jnp.concatenate([zero, flux_weights])]
        + [jnp.zeros((128,), F32)] * 6
    )
    return f / SUB


def substep(state, add, weights):
    s0, s1 = split(state)
    got = dot(jnp.concatenate([s0, s1], axis=1), weights)
    return (got[:, :128] + got[:, 128:]) + (add + 0.25 * jnp.tanh(state))


def heat_kernel(rows_ref, add_ref, weights_ref, flux_ref, heat_ref):
    weights = weights_ref[...]
    state = rows_ref[0]
    total = jnp.zeros_like(state)
    for _ in range(SUB):
        state = substep(state, add_ref[0], weights)
        total = total + state
    t0, t1 = split(total)
    f0, f1 = split(flux_ref[...])
    heat_ref[0] = dot_nt(f0, t0) + dot_nt(f0, t1) + dot_nt(f1, t0)


def home_heat(rows, add, weights, flux):
    return pl.pallas_call(
        heat_kernel,
        grid=(NT,),
        out_shape=jax.ShapeDtypeStruct((NT, 8, HALF), F32),
        in_specs=[
            pl.BlockSpec((1, HALF, 128), lambda d: (d, 0, 0)),
            pl.BlockSpec((1, HALF, 128), lambda d: (d, 0, 0)),
            pl.BlockSpec((256, 256), lambda d: (0, 0)),
            pl.BlockSpec((8, 128), lambda d: (0, 0)),
        ],
        out_specs=pl.BlockSpec((1, 8, HALF), lambda d: (d, 0, 0)),
        compiler_params=pltpu.CompilerParams(vmem_limit_bytes=24 * 2**20),
        cost_estimate=pl.CostEstimate(
            flops=SUB * 8192 * 256 * 512, bytes_accessed=8 << 20, transcendentals=SUB << 20
        ),
        name="home_heat",
    )(rows, add, weights, flux)


def deposit_kernel(lanes_ref, heat_ref, stepped_ref, out_ref, acc):
    d = pl.program_id(0)

    @pl.when(d == 0)
    def _():
        acc[...] = jnp.zeros_like(acc)

    one, nil = jnp.ones((), F32), jnp.zeros((), F32)
    nums = lanes_ref[0]
    s, r, valid = nums[0:1].astype(I32), nums[1:2].astype(I32), nums[3:4]
    heat = jnp.concatenate([heat_ref[0, 0:1], heat_ref[0, 1:2]], axis=1)
    heat = jnp.where(valid > 0.5, 0.5 * heat, nil)
    spread = jnp.where(s == iota((128, MSG), 0), heat, nil)
    h0, h1 = split(spread)
    hot = jnp.where(r == iota((ROWS, MSG), 0), one, nil).astype(BF16)
    acc[...] += dot_nt(hot, jnp.concatenate([h0, h1], axis=0))

    @pl.when(d == NT - 1)
    def _():
        out_ref[...] = stepped_ref[...] + acc[:, :128] + acc[:, 128:]


def deposit(lanes, heat, stepped):
    return pl.pallas_call(
        deposit_kernel,
        grid=(NT,),
        out_shape=jax.ShapeDtypeStruct((ROWS, 128), F32),
        in_specs=[
            pl.BlockSpec((1, 8, MSG), lambda d: (d, 0, 0)),
            pl.BlockSpec((1, 8, HALF), lambda d: (d, 0, 0)),
            pl.BlockSpec((ROWS, 128), lambda d: (0, 0)),
        ],
        out_specs=pl.BlockSpec((ROWS, 128), lambda d: (0, 0)),
        scratch_shapes=[pltpu.VMEM((ROWS, 256), F32)],
        compiler_params=pltpu.CompilerParams(vmem_limit_bytes=24 * 2**20),
        cost_estimate=pl.CostEstimate(flops=16384 * 1024 * 512, bytes_accessed=2 << 20, transcendentals=0),
        name="deposit",
    )(lanes, heat, stepped)


def settle_kernel(amount_ref, slot_ref, rows_ref, far_ref, fw_ref, weights_ref, out_ref, stage, low_s, high_s):
    low_lanes = iota((HALF, 128), 1) < 64
    pick = jnp.where(iota((8, 128), 0) == 0, 1.0, 0.0).astype(F32)
    tn = (((0,), (0,)), ((), ()))

    @pl.loop(0, NT)
    def _(t):
        rows = rows_ref[t]
        far = far_ref[t]
        f0, f1 = split(far)
        col = lax.dot_general(f0, pick.astype(BF16), tn, preferred_element_type=F32)
        col = col + lax.dot_general(f1, pick.astype(BF16), tn, preferred_element_type=F32)
        low_s[...] = jnp.where(low_lanes, rows, col[:HALF])
        high_s[...] = jnp.where(low_lanes, pltpu.roll(rows, 64, 1), col[HALF:])
        amount = amount_ref[t]

        @pl.loop(0, (jnp.minimum(amount, HALF) + 7) >> 3)
        def _(k):
            at = pl.multiple_of(8 * k, 8)
            for i in range(8):
                stage[pl.ds(slot_ref[t, at + i], 1)] = low_s[pl.ds(at + i, 1)]

        @pl.loop(0, (jnp.maximum(amount - HALF, 0) + 7) >> 3)
        def _(k):
            at = pl.multiple_of(8 * k, 8)
            for i in range(8):
                stage[pl.ds(slot_ref[t, HALF + at + i], 1)] = high_s[pl.ds(at + i, 1)]

    weights = weights_ref[...]
    fw = fw_ref[...]

    @pl.loop(0, OWN2 // HALF)
    def _(c):
        at = pl.multiple_of(c * HALF, HALF)
        a = stage[pl.ds(at, HALF)]
        b = stage[pl.ds(pl.multiple_of(at + OWN2, HALF), HALF)]
        state = jnp.where(low_lanes, a, pltpu.roll(b, 64, 1))
        add = fw * jnp.where(low_lanes, pltpu.roll(a, 64, 1), b)
        for _ in range(SUB):
            state = substep(state, add, weights)
        for k in range(HALF // 128):
            turned = state[128 * k : 128 * k + 128].T
            out_ref[:, pl.ds(pl.multiple_of(at + 128 * k, 128), 128)] = turned[:64]
            out_ref[:, pl.ds(pl.multiple_of(at + OWN2 + 128 * k, 128), 128)] = turned[64:]


def settle(amount, slots, rows, far, fw, weights):
    vmem, smem = pl.BlockSpec(memory_space=pltpu.VMEM), pl.BlockSpec(memory_space=pltpu.SMEM)
    return pl.pallas_call(
        settle_kernel,
        out_shape=jax.ShapeDtypeStruct((PTS, OWN), F32),
        in_specs=[smem, smem, vmem, vmem, vmem, vmem],
        out_specs=vmem,
        scratch_shapes=[
            pltpu.VMEM((OWN + 8, 128), F32),
            pltpu.VMEM((HALF, 128), F32),
            pltpu.VMEM((HALF, 128), F32),
        ],
        compiler_params=pltpu.CompilerParams(vmem_limit_bytes=32 * 2**20),
        name="settle",
    )(amount, slots, rows, far, fw, weights)


def halo(cells):
    n_x, n_s = lax.axis_size("stream"), lax.axis_size("tile")
    up_x = [(i, i + 1) for i in range(n_x - 1)]
    down_x = [(i + 1, i) for i in range(n_x - 1)]
    up_s = [(i, (i + 1) % n_s) for i in range(n_s)]
    down_s = [((i + 1) % n_s, i) for i in range(n_s)]
    before_x = lax.ppermute(cells[-1:], "stream", up_x)
    after_x = lax.ppermute(cells[:1], "stream", down_x)
    before_s = lax.ppermute(cells[:, :, -1], "tile", up_s)[:, :, None]
    after_s = lax.ppermute(cells[:, :, 0], "tile", down_s)[:, :, None]
    return (
        jnp.concatenate([before_x, cells[:-1]], axis=0),
        jnp.concatenate([cells[1:], after_x], axis=0),
        jnp.concatenate([before_s, cells[..., :-1]], axis=2),
        jnp.concatenate([cells[..., 1:], after_s], axis=2),
    )


def stencil(enthalpy, x_lower, x_upper, s_lower, s_upper, velocity, diffusivity, wall_flux):
    wall_low = jnp.concatenate([enthalpy[:, :1], enthalpy[:, :-1]], axis=1)
    wall_high = jnp.concatenate([enthalpy[:, 1:], enthalpy[:, -1:]], axis=1)
    laplace = x_lower + x_upper + (wall_low + wall_high) + (s_lower + s_upper) - 6.0 * enthalpy
    stepped = enthalpy + diffusivity * laplace - velocity * (enthalpy - x_lower)
    at_wall = lax.broadcasted_iota(I32, stepped.shape, 1) == 0
    return stepped + jnp.where(at_wall, wall_flux[:, None, :], 0.0)


def on_device(
    enthalpy, velocity, diffusivity, wall_flux, profiles, counts, owners, cells,
    radial_step, far_weights, flux_weights,
):
    weights = step_weights(radial_step)
    fw = jnp.concatenate([far_weights, far_weights])[None, :]
    flux = flux_rows(flux_weights)
    rows, meta, lanes = route(counts, owners, cells, profiles)
    got_rows = lax.all_to_all(rows, "tile", split_axis=0, concat_axis=0, tiled=True)
    far, add = far_gather(meta, enthalpy.reshape(ROWS, 128), fw)
    side = jnp.concatenate(
        [lanes[:, 2].reshape(NT, 4, 128), far[:, 0].reshape(NT, 4, 128)], axis=1
    )
    got_side = lax.all_to_all(side, "tile", split_axis=0, concat_axis=0, tiled=True)
    heat = home_heat(rows, add, weights, flux)
    stepped = stencil(enthalpy, *halo(enthalpy), velocity, diffusivity, wall_flux)
    new_enthalpy = deposit(lanes, heat, stepped.reshape(ROWS, 128)).reshape(enthalpy.shape)
    slots = got_side[:, :4].reshape(NT, MSG).astype(I32)
    amount = jnp.sum((slots < OWN).astype(I32), axis=1)
    got_far = jnp.broadcast_to(got_side[:, 4:].reshape(NT, 1, MSG), (NT, 8, MSG))
    new_profiles = settle(amount, slots, got_rows, got_far, fw, weights)
    return new_enthalpy, new_profiles


def solution(mesh):
    return jax.shard_map(
        on_device,
        mesh=mesh,
        in_specs=(
            P("stream", None, "tile"),
            P("stream", None, "tile"),
            P("stream", None, "tile"),
            P("stream", "tile"),
            P(None, ("stream", "tile")),
            P(("stream", "tile")),
            P(("stream", "tile")),
            P(("stream", "tile")),
            P(),
            P(),
            P(),
        ),
        out_specs=(P("stream", None, "tile"), P(None, ("stream", "tile"))),
        check_vma=False,
    )
```

```python
import jax
import jax.numpy as jnp
from jax import lax
from jax.experimental import pallas as pl
from jax.experimental.pallas import tpu as pltpu
from jax.sharding import PartitionSpec as P

SUB = 16
PTS = 64
NT = 32
CAP = 16384
OWN = 6144
MSG = 512
HALF = MSG // 2
LOAD = HALF + 8
BLK = 256
NBLK = CAP // BLK
STRIDE = MSG + 16
ROWS = 1024
OWN2 = OWN // 2

F32, BF16, I32 = jnp.float32, jnp.bfloat16, jnp.int32
NTD = (((1,), (1,)), ((), ()))


def iota(shape, dim):
    return lax.broadcasted_iota(I32, shape, dim)


def split(x):
    high = x.astype(BF16)
    return high, (x - high.astype(F32)).astype(BF16)


def dot(a, b):
    return jnp.dot(a, b, preferred_element_type=F32)


def dot_nt(a, b):
    return lax.dot_general(a, b, NTD, preferred_element_type=F32)


def route_kernel(
    count_ref, owners_ref, cells_ref, prof_ref,
    rows_ref, meta_ref, lanes_ref,
    pos_s, m0_s, m1_s, m2_s, m3_s, m4_s, sorted_a, sorted_b, bucket, tab_v, tab_s, sem,
):
    count = count_ref[0]
    slot = iota((NBLK, BLK), 0) * BLK + iota((NBLK, BLK), 1)
    owners = owners_ref[...]
    dest = jnp.floor((owners.astype(F32) + 0.5) * (1.0 / OWN)).astype(I32)
    within = owners - dest * OWN
    live = slot < count
    dest = jnp.where(live, dest, NT)
    cells = cells_ref[...]
    m0_s[...] = (cells & 127).astype(F32)
    m1_s[...] = ((cells >> 7) & 3).astype(F32)
    m2_s[...] = (cells >> 9).astype(F32)
    m3_s[...] = (within & 255).astype(F32)
    m4_s[...] = (within >> 8).astype(F32)

    sub, lane = iota((BLK, BLK), 0), iota((BLK, BLK), 1)
    one, nil = jnp.ones((), F32), jnp.zeros((), F32)
    before = jnp.where(sub < lane, one, nil).astype(BF16)
    same_block = (sub >> 5) == (lane >> 5)
    same_dest = (sub & 31) == (lane & 31)
    seg_left = jnp.where(same_block & (lane < sub), one, nil).astype(BF16)
    seg_right = jnp.where(same_block & (sub < lane), one, nil).astype(BF16)
    base_right = jnp.where(same_dest & ((sub >> 5) < (lane >> 5)), one, nil).astype(BF16)
    all_right = jnp.where(same_dest, one, nil).astype(BF16)
    ones_a = jnp.ones((8, BLK), BF16)
    ones_b = jnp.ones((BLK, 128), BF16)
    run = jnp.zeros((8, BLK), F32)
    for c in range(8):
        part = dest[8 * c : 8 * c + 8]
        hot = jnp.where(part[:, None, :] == iota((8, NT, BLK), 1), one, nil).reshape(BLK, BLK)
        hot_b = hot.astype(BF16)
        prefix = dot(hot_b, before)
        amount = dot(hot_b, ones_b)
        seg = dot(seg_left, amount.astype(BF16))
        seg2 = jnp.concatenate([seg, seg], axis=1)
        pos = jnp.sum((hot * (prefix + seg2)).reshape(8, NT, BLK), axis=1)
        pos_s[8 * c : 8 * c + 8] = jnp.where(live[8 * c : 8 * c + 8], pos, 511.0)
        amount_l = dot_nt(ones_a, hot_b)
        amount_lb = amount_l.astype(BF16)
        src = dot(amount_lb, seg_right)
        base = dot(amount_lb, base_right) + run
        run = run + dot(amount_lb, all_right)
        most = amount_l
        for shift in (1, 2, 4, 8, 16):
            most = jnp.maximum(most, pltpu.roll(most, BLK - shift, 1))
        first = iota((8, BLK), 1) & 31
        row8 = iota((8, BLK), 0)
        packed = jnp.where(row8 == 0, src, nil)
        packed = jnp.where(row8 == 1, base + (first * STRIDE).astype(F32), packed)
        packed = jnp.where(row8 == 2, amount_l, packed)
        packed = jnp.where(row8 == 3, most, packed)
        packed = packed.astype(I32)
        tab_v[16 * c : 16 * c + 8] = packed[:, :128]
        tab_v[16 * c + 8 : 16 * c + 16] = packed[:, 128:]
    copy = pltpu.make_async_copy(tab_v, tab_s, sem)
    copy.start()
    total = run

    zero8 = jnp.zeros((STRIDE, 128), F32)

    @pl.loop(0, NT)
    def _(d):
        bucket[pl.ds(pl.multiple_of(d * STRIDE, 8), STRIDE)] = zero8

    copy.wait()

    meta_rest = jnp.zeros((56, BLK), BF16)
    low_rest = jnp.zeros((64, BLK), BF16)
    row8 = iota((8, BLK), 0)

    def sort_block(j, out):
        x = prof_ref[:, pl.ds(pl.multiple_of(j * BLK, BLK), BLK)]
        high, low = split(x)
        meta = jnp.zeros((8, BLK), F32)
        for k, ref in enumerate((m0_s, m1_s, m2_s, m3_s, m4_s)):
            meta = jnp.where(row8 == k, ref[pl.ds(j, 1), :], meta)
        data = jnp.concatenate([high, meta.astype(BF16), meta_rest, low, low_rest], axis=0)
        place = pos_s[pl.ds(j, 1), :].astype(I32)
        perm = jnp.where(place == sub, one, nil).astype(BF16)
        got = dot_nt(perm, data)
        out[0:BLK] = got[:, :128] + got[:, 128:]

    def copy_block(j, inp):
        chunk = (j >> 2) * 8
        at = (j & 3) * NT
        most = tab_s[chunk + 3, at]

        @pl.when(most <= 8)
        def _():
            for d in range(NT):
                src = tab_s[chunk, at + d]
                dst = tab_s[chunk + 1, at + d]
                bucket[pl.ds(dst, 8)] = inp[pl.ds(src, 8)]

        @pl.when((most > 8) & (most <= 16))
        def _():
            for d in range(NT):
                src = tab_s[chunk, at + d]
                dst = tab_s[chunk + 1, at + d]
                bucket[pl.ds(dst, 16)] = inp[pl.ds(src, 16)]

        @pl.when(most > 16)
        def _():
            @pl.loop(0, NT)
            def _(d):
                src = tab_s[chunk, at + d]
                dst = tab_s[chunk + 1, at + d]

                @pl.loop(0, (tab_s[chunk + 2, at + d] + 7) >> 3)
                def _(k):
                    bucket[pl.ds(dst + 8 * k, 8)] = inp[pl.ds(src + 8 * k, 8)]

    sorted_a[BLK:] = jnp.zeros((16, 128), F32)
    sorted_b[BLK:] = jnp.zeros((16, 128), F32)
    pairs = (count + 2 * BLK - 1) // (2 * BLK)
    sort_block(0, sorted_a)

    @pl.loop(0, pairs)
    def _(p):
        sort_block(2 * p + 1, sorted_b)
        copy_block(2 * p, sorted_a)
        sort_block(jnp.minimum(2 * p + 2, NBLK - 1), sorted_a)
        copy_block(2 * p + 1, sorted_b)

    low_lanes = iota((HALF, 128), 1) < 64
    r8, l8 = iota((8, 128), 0), iota((8, 128), 1)
    pick = jnp.where((r8 == 0) & (l8 == 64), one, nil)
    pick = jnp.where((r8 == 1) & (l8 == 65), one, pick)
    pick = jnp.where((r8 == 1) & (l8 == 66), 4.0 * one, pick)
    pick = jnp.where((r8 == 2) & (l8 == 67), one, pick)
    pick = jnp.where((r8 == 2) & (l8 == 68), 256.0 * one, pick)
    pick = pick.astype(BF16)
    rank = iota((8, MSG), 1)
    rank_row = iota((8, MSG), 0)
    lane_dest = iota((8, BLK), 1)

    @pl.loop(0, NT, unroll=4)
    def _(d):
        at = pl.multiple_of(d * STRIDE, 8)
        lo = bucket[pl.ds(at, HALF)]
        hi = bucket[pl.ds(pl.multiple_of(at + HALF, 8), HALF)]
        rows_ref[d, 0:HALF] = jnp.where(low_lanes, lo, pltpu.roll(hi, 64, 1))
        meta_ref[d] = jnp.where(low_lanes, pltpu.roll(lo, 64, 1), hi).astype(BF16)
        both = jnp.concatenate([lo, hi], axis=0).astype(BF16)
        nums = dot_nt(pick, both)
        mine = jnp.max(jnp.where(lane_dest == d, total, nil), axis=1, keepdims=True)
        valid = rank.astype(F32) < mine
        nums = jnp.where((rank_row == 2) & ~valid, float(OWN), nums)
        nums = jnp.where(rank_row == 3, jnp.where(valid, one, nil), nums)
        lanes_ref[d] = nums
        rows_ref[d, HALF : HALF + 8] = jnp.concatenate(
            [nums[2:3, 128 * q : 128 * q + 128] for q in range(4)] + [jnp.zeros((4, 128), F32)], axis=0
        )


def route(counts, owners, cells, profiles):
    vmem = pl.BlockSpec(memory_space=pltpu.VMEM)
    return pl.pallas_call(
        route_kernel,
        out_shape=(
            jax.ShapeDtypeStruct((NT, LOAD, 128), F32),
            jax.ShapeDtypeStruct((NT, HALF, 128), BF16),
            jax.ShapeDtypeStruct((NT, 8, MSG), F32),
        ),
        in_specs=[pl.BlockSpec(memory_space=pltpu.SMEM), vmem, vmem, vmem],
        out_specs=(vmem, vmem, vmem),
        scratch_shapes=[pltpu.VMEM((NBLK, BLK), F32)] * 6
        + [pltpu.VMEM((BLK + 16, 128), F32)] * 2
        + [
            pltpu.VMEM((NT * STRIDE, 128), F32),
            pltpu.VMEM((128, 128), I32),
            pltpu.SMEM((128, 128), I32),
            pltpu.SemaphoreType.DMA,
        ],
        compiler_params=pltpu.CompilerParams(vmem_limit_bytes=40 * 2**20),
        name="route",
    )(counts, owners.reshape(NBLK, BLK), cells.reshape(NBLK, BLK), profiles)


FAR_N = 4


def far_kernel(side_ref, meta_ref, cells_ref, fw_ref, out_ref, add_ref, table):
    one, nil = jnp.ones((), F32), jnp.zeros((), F32)
    m_rows = FAR_N * HALF

    @pl.when(pl.program_id(0) == 0)
    def _():
        cells = cells_ref[...].reshape(ROWS // 4, 4, 128)
        parts = [split(cells[:, q]) for q in range(4)]
        table[...] = jnp.concatenate([p[0] for p in parts] + [p[1] for p in parts], axis=1)

    fw0, fw1 = split(fw_ref[...])
    sub, lane = iota((128, 128), 0), iota((128, 128), 1)
    ones8 = jnp.ones((8, 256), BF16)
    place = iota((m_rows, 128), 1).astype(F32)
    meta = meta_ref[...].reshape(m_rows, 128)
    for i in range(FAR_N):
        out_ref[i, 0:4] = side_ref[i, 0:4]
    vals, picks = [], []
    for h in range(2):
        first = 0 if h == 0 else 64
        col = jnp.where(sub == first, one, nil) + jnp.where(sub == first + 1, 128.0 * one, nil)
        row = jnp.where(sub == first + 2, one, nil)
        got = dot(meta, jnp.concatenate([col, row], axis=1).astype(BF16))
        col, row = got[:, :128], got[:, 128:]
        hot = jnp.concatenate(
            [jnp.where(row == place + 128.0 * q, one, nil).astype(BF16) for q in range(2)], axis=1
        )
        val = dot(hot, table[...])
        got = jnp.zeros((m_rows, 128), F32)
        for q in range(4):
            both = val[:, 128 * q : 128 * q + 128] + val[:, 512 + 128 * q : 640 + 128 * q]
            got = jnp.where(col == place + 128.0 * q, both, got)
        v0, v1 = split(got)
        v = jnp.concatenate([v0, v1], axis=1)
        far = dot_nt(ones8, v)
        for i in range(FAR_N):
            for q in range(2):
                at = 256 * i + 128 * q
                out_ref[i, 4 + 2 * h + q : 5 + 2 * h + q] = far[0:1, at : at + 128]
        mask = (lane >= 64) if h else (lane < 64)
        w0 = jnp.where(mask, fw0.astype(F32), nil).astype(BF16)
        w1 = jnp.where(mask, fw1.astype(F32), nil).astype(BF16)
        vals.append(v)
        picks.append(jnp.concatenate([jnp.concatenate([w0, w1], axis=1)] * 2, axis=0))
    got = dot(vals[0], picks[0]) + dot(vals[1], picks[1])
    add_ref[...] = (got[:, :128] + got[:, 128:]).reshape(FAR_N, HALF, 128)


def far_gather(rows, meta, table, fw):
    side = pl.BlockSpec((FAR_N, 8, 128), lambda d: (d, HALF // 8, 0))
    return pl.pallas_call(
        far_kernel,
        grid=(NT // FAR_N,),
        out_shape=(
            jax.ShapeDtypeStruct((NT, LOAD, 128), F32),
            jax.ShapeDtypeStruct((NT, HALF, 128), F32),
        ),
        in_specs=[
            side,
            pl.BlockSpec((FAR_N, HALF, 128), lambda d: (d, 0, 0)),
            pl.BlockSpec((ROWS, 128), lambda d: (0, 0)),
            pl.BlockSpec((1, 128), lambda d: (0, 0)),
        ],
        out_specs=(side, pl.BlockSpec((FAR_N, HALF, 128), lambda d: (d, 0, 0))),
        scratch_shapes=[pltpu.VMEM((256, 1024), BF16)],
        input_output_aliases={0: 0},
        compiler_params=pltpu.CompilerParams(vmem_limit_bytes=32 * 2**20),
        cost_estimate=pl.CostEstimate(flops=10**10, bytes_accessed=8 << 20, transcendentals=0),
        name="far_gather",
    )(rows, meta, table, fw)


def step_weights(radial_step):
    zero = jnp.zeros((PTS, PTS), F32)
    w = jnp.concatenate(
        [
            jnp.concatenate([radial_step.T, zero], axis=1),
            jnp.concatenate([zero, radial_step.T], axis=1),
        ],
        axis=0,
    )
    high = lax.reduce_precision(w, 8, 7)
    w0, w1 = high.astype(BF16), (w - high).astype(BF16)
    row = jnp.concatenate([w0, w1], axis=1)
    return jnp.concatenate([row, row], axis=0)


def flux_rows(flux_weights):
    zero = jnp.zeros((PTS,), F32)
    f = jnp.stack(
        [jnp.concatenate([flux_weights, zero]), jnp.concatenate([zero, flux_weights])]
        + [jnp.zeros((128,), F32)] * 6
    )
    return f / SUB


def substep(state, add, weights):
    s0, s1 = split(state)
    got = dot(jnp.concatenate([s0, s1], axis=1), weights)
    return (got[:, :128] + got[:, 128:]) + (add + 0.25 * jnp.tanh(state))


HEAT_N = 4


def heat_kernel(rows_ref, add_ref, weights_ref, flux_ref, heat_ref):
    weights = weights_ref[...]
    state = rows_ref[...].reshape(HEAT_N * HALF, 128)
    add = add_ref[...].reshape(HEAT_N * HALF, 128)
    total = jnp.zeros_like(state)
    for _ in range(SUB):
        state = substep(state, add, weights)
        total = total + state
    t0, t1 = split(total)
    f0, f1 = split(flux_ref[...])
    heat = dot_nt(f0, t0) + dot_nt(f0, t1) + dot_nt(f1, t0)
    for i in range(HEAT_N):
        heat_ref[i] = heat[:, HALF * i : HALF * i + HALF]


def home_heat(rows, add, weights, flux):
    block = pl.BlockSpec((HEAT_N, HALF, 128), lambda d: (d, 0, 0))
    return pl.pallas_call(
        heat_kernel,
        grid=(NT // HEAT_N,),
        out_shape=jax.ShapeDtypeStruct((NT, 8, HALF), F32),
        in_specs=[
            block,
            block,
            pl.BlockSpec((256, 256), lambda d: (0, 0)),
            pl.BlockSpec((8, 128), lambda d: (0, 0)),
        ],
        out_specs=pl.BlockSpec((HEAT_N, 8, HALF), lambda d: (d, 0, 0)),
        compiler_params=pltpu.CompilerParams(vmem_limit_bytes=32 * 2**20),
        cost_estimate=pl.CostEstimate(flops=2 * 10**10, bytes_accessed=8 << 20, transcendentals=SUB << 20),
        name="home_heat",
    )(rows, add, weights, flux)


def deposit_kernel(lanes_ref, heat_ref, stepped_ref, out_ref, acc):
    d = pl.program_id(0)

    @pl.when(d == 0)
    def _():
        acc[...] = jnp.zeros_like(acc)

    one, nil = jnp.ones((), F32), jnp.zeros((), F32)
    nums = lanes_ref[0]
    s, r, valid = nums[0:1].astype(I32), nums[1:2].astype(I32), nums[3:4]
    heat = jnp.concatenate([heat_ref[0, 0:1], heat_ref[0, 1:2]], axis=1)
    heat = jnp.where(valid > 0.5, 0.5 * heat, nil)
    spread = jnp.where(s == iota((128, MSG), 0), heat, nil)
    h0, h1 = split(spread)
    hot = jnp.where(r == iota((ROWS, MSG), 0), one, nil).astype(BF16)
    acc[...] += dot_nt(hot, jnp.concatenate([h0, h1], axis=0))

    @pl.when(d == NT - 1)
    def _():
        out_ref[...] = stepped_ref[...] + acc[:, :128] + acc[:, 128:]


def deposit(lanes, heat, stepped):
    return pl.pallas_call(
        deposit_kernel,
        grid=(NT,),
        out_shape=jax.ShapeDtypeStruct((ROWS, 128), F32),
        in_specs=[
            pl.BlockSpec((1, 8, MSG), lambda d: (d, 0, 0)),
            pl.BlockSpec((1, 8, HALF), lambda d: (d, 0, 0)),
            pl.BlockSpec((ROWS, 128), lambda d: (0, 0)),
        ],
        out_specs=pl.BlockSpec((ROWS, 128), lambda d: (0, 0)),
        scratch_shapes=[pltpu.VMEM((ROWS, 256), F32)],
        compiler_params=pltpu.CompilerParams(vmem_limit_bytes=24 * 2**20),
        cost_estimate=pl.CostEstimate(flops=16384 * 1024 * 512, bytes_accessed=2 << 20, transcendentals=0),
        name="deposit",
    )(lanes, heat, stepped)


SETTLE = 1024


def settle_kernel(amount_ref, slot_ref, rows_ref, fw_ref, weights_ref, out_ref, stage, comb):
    low_lanes = iota((HALF, 128), 1) < 64
    row8 = iota((8, MSG), 0)
    pick = jnp.where(iota((8, 128), 0) < 2, 1.0, 0.0).astype(BF16)
    tn = (((0,), (0,)), ((), ()))

    @pl.loop(0, NT, unroll=4)
    def _(t):
        rows = rows_ref[t, 0:HALF]
        side = rows_ref[t, HALF : HALF + 8]
        far = jnp.concatenate([side[4 + q : 5 + q] for q in range(4)], axis=1)
        rest = far - far.astype(BF16).astype(F32)
        terms = jnp.where(row8 == 0, far, jnp.where(row8 == 1, rest, 0.0)).astype(BF16)
        col = lax.dot_general(terms, pick, tn, preferred_element_type=F32)
        at = pl.multiple_of(t * MSG, MSG)
        comb[pl.ds(at, HALF)] = jnp.where(low_lanes, rows, col[:HALF])
        comb[pl.ds(pl.multiple_of(at + HALF, HALF), HALF)] = jnp.where(
            low_lanes, pltpu.roll(rows, 64, 1), col[HALF:]
        )

    @pl.loop(0, NT)
    def _(t):
        @pl.loop(0, (amount_ref[t] + 31) >> 5)
        def _(k):
            at = pl.multiple_of(t * MSG + 32 * k, 32)
            for i in range(32):
                stage[pl.ds(slot_ref[at + i], 1)] = comb[pl.ds(at + i, 1)]

    weights = weights_ref[...]
    fw = fw_ref[...]
    low_lanes = iota((SETTLE, 128), 1) < 64
    for c in range(OWN2 // SETTLE):
        at = c * SETTLE
        a = stage[at : at + SETTLE]
        b = stage[at + OWN2 : at + OWN2 + SETTLE]
        state = jnp.where(low_lanes, a, pltpu.roll(b, 64, 1))
        add = fw * jnp.where(low_lanes, pltpu.roll(a, 64, 1), b)
        for _ in range(SUB):
            state = substep(state, add, weights)
        for k in range(SETTLE // 128):
            turned = state[128 * k : 128 * k + 128].T
            out_ref[:, at + 128 * k : at + 128 * k + 128] = turned[:64]
            out_ref[:, at + OWN2 + 128 * k : at + OWN2 + 128 * k + 128] = turned[64:]


def settle(amount, slots, rows, fw, weights):
    vmem, smem = pl.BlockSpec(memory_space=pltpu.VMEM), pl.BlockSpec(memory_space=pltpu.SMEM)
    return pl.pallas_call(
        settle_kernel,
        out_shape=jax.ShapeDtypeStruct((PTS, OWN), F32),
        in_specs=[smem, smem, vmem, vmem, vmem],
        out_specs=vmem,
        scratch_shapes=[pltpu.VMEM((OWN + 8, 128), F32), pltpu.VMEM((NT * MSG, 128), F32)],
        compiler_params=pltpu.CompilerParams(vmem_limit_bytes=40 * 2**20),
        name="settle",
    )(amount, slots, rows, fw, weights)


def halo(cells):
    n_x, n_s = lax.axis_size("stream"), lax.axis_size("tile")
    up_x = [(i, i + 1) for i in range(n_x - 1)]
    down_x = [(i + 1, i) for i in range(n_x - 1)]
    up_s = [(i, (i + 1) % n_s) for i in range(n_s)]
    down_s = [((i + 1) % n_s, i) for i in range(n_s)]
    before_x = lax.ppermute(cells[-1:], "stream", up_x)
    after_x = lax.ppermute(cells[:1], "stream", down_x)
    before_s = lax.ppermute(cells[:, :, -1], "tile", up_s)[:, :, None]
    after_s = lax.ppermute(cells[:, :, 0], "tile", down_s)[:, :, None]
    return (
        jnp.concatenate([before_x, cells[:-1]], axis=0),
        jnp.concatenate([cells[1:], after_x], axis=0),
        jnp.concatenate([before_s, cells[..., :-1]], axis=2),
        jnp.concatenate([cells[..., 1:], after_s], axis=2),
    )


def stencil(enthalpy, x_lower, x_upper, s_lower, s_upper, velocity, diffusivity, wall_flux):
    wall_low = jnp.concatenate([enthalpy[:, :1], enthalpy[:, :-1]], axis=1)
    wall_high = jnp.concatenate([enthalpy[:, 1:], enthalpy[:, -1:]], axis=1)
    laplace = x_lower + x_upper + (wall_low + wall_high) + (s_lower + s_upper) - 6.0 * enthalpy
    stepped = enthalpy + diffusivity * laplace - velocity * (enthalpy - x_lower)
    at_wall = lax.broadcasted_iota(I32, stepped.shape, 1) == 0
    return stepped + jnp.where(at_wall, wall_flux[:, None, :], 0.0)


def on_device(
    enthalpy, velocity, diffusivity, wall_flux, profiles, counts, owners, cells,
    radial_step, far_weights, flux_weights,
):
    weights = step_weights(radial_step)
    fw = jnp.concatenate([far_weights, far_weights])[None, :]
    flux = flux_rows(flux_weights)
    rows, meta, lanes = route(counts, owners, cells, profiles)
    rows, add = far_gather(rows, meta, enthalpy.reshape(ROWS, 128), fw)
    got = lax.all_to_all(rows, "tile", split_axis=0, concat_axis=0, tiled=True)
    heat = home_heat(rows, add, weights, flux)
    edges, heat = lax.optimization_barrier((enthalpy, heat))
    stepped = stencil(enthalpy, *halo(edges), velocity, diffusivity, wall_flux)
    new_enthalpy = deposit(lanes, heat, stepped.reshape(ROWS, 128)).reshape(enthalpy.shape)
    slots = got[:, HALF : HALF + 4].reshape(NT, MSG).astype(I32)
    amount = jnp.sum((slots < OWN).astype(I32), axis=1)
    new_profiles = settle(amount, slots.reshape(-1), got, fw, weights)
    return new_enthalpy, new_profiles


def solution(mesh):
    return jax.shard_map(
        on_device,
        mesh=mesh,
        in_specs=(
            P("stream", None, "tile"),
            P("stream", None, "tile"),
            P("stream", None, "tile"),
            P("stream", "tile"),
            P(None, ("stream", "tile")),
            P(("stream", "tile")),
            P(("stream", "tile")),
            P(("stream", "tile")),
            P(),
            P(),
            P(),
        ),
        out_specs=(P("stream", None, "tile"), P(None, ("stream", "tile"))),
        check_vma=False,
    )
```

```python
import jax
import jax.numpy as jnp
from jax import lax
from jax.experimental import pallas as pl
from jax.experimental.pallas import tpu as pltpu
from jax.sharding import PartitionSpec as P

SUB = 16
PTS = 64
NT = 32
CAP = 16384
OWN = 6144
MSG = 512
HALF = MSG // 2
LOAD = HALF + 8
BLK = 256
NBLK = CAP // BLK
STRIDE = MSG + 16
ROWS = 1024
OWN2 = OWN // 2

ROOM = 60 * 2**20

F32, BF16, I32 = jnp.float32, jnp.bfloat16, jnp.int32
NTD = (((1,), (1,)), ((), ()))


def iota(shape, dim):
    return lax.broadcasted_iota(I32, shape, dim)


def split(x):
    high = x.astype(BF16)
    return high, (x - high.astype(F32)).astype(BF16)


def dot(a, b):
    return jnp.dot(a, b, preferred_element_type=F32)


def dot_nt(a, b):
    return lax.dot_general(a, b, NTD, preferred_element_type=F32)


def route_kernel(
    count_ref, owners_ref, cells_ref, prof_ref,
    rows_ref, meta_ref, lanes_ref,
    pos_s, m0_s, m1_s, m2_s, m3_s, m4_s, sorted_a, sorted_b, sorted_c, sorted_d,
    bucket, tab_v, tab_s, sem, prof_v, prof_sem, pack_v, pack_sem,
):
    count = count_ref[0]
    fetch = pltpu.make_async_copy(prof_ref, prof_v, prof_sem)
    fetch.start()

    def blocks(ref):
        x = ref[...].reshape(NBLK, 2, 128)
        return jnp.concatenate([x[:, 0], x[:, 1]], axis=1)

    slot = iota((NBLK, BLK), 0) * BLK + iota((NBLK, BLK), 1)
    owners = blocks(owners_ref)
    dest = jnp.floor((owners.astype(F32) + 0.5) * (1.0 / OWN)).astype(I32)
    within = owners - dest * OWN
    live = slot < count
    dest = jnp.where(live, dest, NT)
    cells = blocks(cells_ref)
    m0_s[...] = (cells & 127).astype(F32)
    m1_s[...] = ((cells >> 7) & 3).astype(F32)
    m2_s[...] = (cells >> 9).astype(F32)
    m3_s[...] = (within & 255).astype(F32)
    m4_s[...] = (within >> 8).astype(F32)

    sub, lane = iota((BLK, BLK), 0), iota((BLK, BLK), 1)
    one, nil = jnp.ones((), F32), jnp.zeros((), F32)
    before = jnp.where(sub < lane, one, nil).astype(BF16)
    same_block = (sub >> 5) == (lane >> 5)
    same_dest = (sub & 31) == (lane & 31)
    seg_left = jnp.where(same_block & (lane < sub), one, nil).astype(BF16)
    seg_right = jnp.where(same_block & (sub < lane), one, nil).astype(BF16)
    base_right = jnp.where(same_dest & ((sub >> 5) < (lane >> 5)), one, nil).astype(BF16)
    all_right = jnp.where(same_dest, one, nil).astype(BF16)
    ones_a = jnp.ones((8, BLK), BF16)
    ones_b = jnp.ones((BLK, 128), BF16)
    run = jnp.zeros((8, BLK), F32)
    longest = jnp.zeros((8, BLK), F32)
    for c in range(8):
        part = dest[8 * c : 8 * c + 8]
        hot = jnp.where(part[:, None, :] == iota((8, NT, BLK), 1), one, nil).reshape(BLK, BLK)
        hot_b = hot.astype(BF16)
        prefix = dot(hot_b, before)
        amount = dot(hot_b, ones_b)
        seg = dot(seg_left, amount.astype(BF16))
        seg2 = jnp.concatenate([seg, seg], axis=1)
        pos = jnp.sum((hot * (prefix + seg2)).reshape(8, NT, BLK), axis=1)
        pos_s[8 * c : 8 * c + 8] = jnp.where(live[8 * c : 8 * c + 8], pos, 511.0)
        amount_l = dot_nt(ones_a, hot_b)
        amount_lb = amount_l.astype(BF16)
        src = dot(amount_lb, seg_right)
        base = dot(amount_lb, base_right) + run
        run = run + dot(amount_lb, all_right)
        longest = jnp.maximum(longest, amount_l)
        most = amount_l
        for shift in (1, 2, 4, 8, 16):
            most = jnp.maximum(most, pltpu.roll(most, BLK - shift, 1))
        first = iota((8, BLK), 1) & 31
        row8 = iota((8, BLK), 0)
        packed = jnp.where(row8 == 0, src, nil)
        packed = jnp.where(row8 == 1, base + (first * STRIDE).astype(F32), packed)
        packed = jnp.where(row8 == 2, amount_l, packed)
        packed = jnp.where(row8 == 3, most, packed)
        packed = packed.astype(I32)
        tab_v[16 * c : 16 * c + 8] = packed[:, :128]
        tab_v[16 * c + 8 : 16 * c + 16] = packed[:, 128:]
    copy = pltpu.make_async_copy(tab_v, tab_s, sem)
    copy.start()
    short = jnp.max(longest) <= 8.0
    total = run

    zero8 = jnp.zeros((STRIDE, 128), F32)

    @pl.loop(0, NT)
    def _(d):
        bucket[pl.ds(pl.multiple_of(d * STRIDE, 8), STRIDE)] = zero8

    copy.wait()
    fetch.wait()

    meta_rest = jnp.zeros((56, BLK), BF16)
    low_rest = jnp.zeros((64, BLK), BF16)
    row8 = iota((8, BLK), 0)

    def sort_block(j, out):
        x = prof_v[:, pl.ds(pl.multiple_of(j * BLK, BLK), BLK)]
        high, low = split(x)
        meta = jnp.zeros((8, BLK), F32)
        for k, ref in enumerate((m0_s, m1_s, m2_s, m3_s, m4_s)):
            meta = jnp.where(row8 == k, ref[pl.ds(j, 1), :], meta)
        data = jnp.concatenate([high, meta.astype(BF16), meta_rest, low, low_rest], axis=0)
        place = pos_s[pl.ds(j, 1), :].astype(I32)
        perm = jnp.where(place == sub, one, nil).astype(BF16)
        got = dot_nt(perm, data)
        out[0:BLK] = got[:, :128] + got[:, 128:]

    def copy_block(j, inp):
        chunk = (j >> 2) * 8
        at = (j & 3) * NT
        most = tab_s[chunk + 3, at]

        @pl.when(most <= 8)
        def _():
            for d in range(NT):
                src = tab_s[chunk, at + d]
                dst = tab_s[chunk + 1, at + d]
                bucket[pl.ds(dst, 8)] = inp[pl.ds(src, 8)]

        @pl.when((most > 8) & (most <= 16))
        def _():
            for d in range(NT):
                src = tab_s[chunk, at + d]
                dst = tab_s[chunk + 1, at + d]
                bucket[pl.ds(dst, 16)] = inp[pl.ds(src, 16)]

        @pl.when(most > 16)
        def _():
            @pl.loop(0, NT)
            def _(d):
                src = tab_s[chunk, at + d]
                dst = tab_s[chunk + 1, at + d]

                @pl.loop(0, (tab_s[chunk + 2, at + d] + 7) >> 3)
                def _(k):
                    bucket[pl.ds(dst + 8 * k, 8)] = inp[pl.ds(src + 8 * k, 8)]

    def copy_short(j, inp):
        chunk = (j >> 2) * 8
        at = (j & 3) * NT
        for d in range(NT):
            src = tab_s[chunk, at + d]
            dst = tab_s[chunk + 1, at + d]
            bucket[pl.ds(dst, 8)] = inp[pl.ds(src, 8)]

    for ref in (sorted_a, sorted_b, sorted_c, sorted_d):
        ref[BLK:] = jnp.zeros((16, 128), F32)
    quads = (count + 4 * BLK - 1) // (4 * BLK)
    sort_block(0, sorted_a)
    sort_block(1, sorted_b)

    def quad(copy_any):
        @pl.loop(0, quads)
        def _(p):
            sort_block(4 * p + 2, sorted_c)
            copy_any(4 * p, sorted_a)
            sort_block(4 * p + 3, sorted_d)
            copy_any(4 * p + 1, sorted_b)
            sort_block(jnp.minimum(4 * p + 4, NBLK - 1), sorted_a)
            copy_any(4 * p + 2, sorted_c)
            sort_block(jnp.minimum(4 * p + 5, NBLK - 1), sorted_b)
            copy_any(4 * p + 3, sorted_d)

    pl.when(short)(lambda: quad(copy_short))
    pl.when(jnp.logical_not(short))(lambda: quad(copy_block))

    low_lanes = iota((HALF, 128), 1) < 64
    r8, l8 = iota((8, 128), 0), iota((8, 128), 1)
    pick = jnp.where((r8 == 0) & (l8 == 64), one, nil)
    pick = jnp.where((r8 == 1) & (l8 == 65), one, pick)
    pick = jnp.where((r8 == 1) & (l8 == 66), 4.0 * one, pick)
    pick = jnp.where((r8 == 2) & (l8 == 67), one, pick)
    pick = jnp.where((r8 == 2) & (l8 == 68), 256.0 * one, pick)
    pick = pick.astype(BF16)
    rank = iota((8, MSG), 1)
    rank_row = iota((8, MSG), 0)
    lane_dest = iota((8, BLK), 1)

    def send(g):
        part = pl.ds(g * 4, 4)
        return pltpu.make_async_copy(pack_v.at[part], rows_ref.at[part], pack_sem.at[g])

    @pl.loop(0, NT // 4)
    def _(g):
        for k in range(4):
            d = 4 * g + k
            at = pl.multiple_of(d * STRIDE, 8)
            lo = bucket[pl.ds(at, HALF)]
            hi = bucket[pl.ds(pl.multiple_of(at + HALF, 8), HALF)]
            pack_v[d, 0:HALF] = jnp.where(low_lanes, lo, pltpu.roll(hi, 64, 1))
            meta_ref[d] = jnp.where(low_lanes, pltpu.roll(lo, 64, 1), hi).astype(BF16)
            both = jnp.concatenate([lo, hi], axis=0).astype(BF16)
            nums = dot_nt(pick, both)
            mine = jnp.max(jnp.where(lane_dest == d, total, nil), axis=1, keepdims=True)
            valid = rank.astype(F32) < mine
            nums = jnp.where((rank_row == 2) & ~valid, float(OWN), nums)
            nums = jnp.where(rank_row == 3, jnp.where(valid, one, nil), nums)
            lanes_ref[d] = nums
            pack_v[d, HALF:LOAD] = jnp.concatenate(
                [nums[2:3, 128 * q : 128 * q + 128] for q in range(4)] + [jnp.zeros((4, 128), F32)],
                axis=0,
            )
        send(g).start()

    for g in range(NT // 4):
        send(g).wait()


def route(counts, owners, cells, profiles):
    vmem = pl.BlockSpec(memory_space=pltpu.VMEM)
    return pl.pallas_call(
        route_kernel,
        out_shape=(
            jax.ShapeDtypeStruct((NT, LOAD, 128), F32),
            jax.ShapeDtypeStruct((NT, HALF, 128), BF16),
            jax.ShapeDtypeStruct((NT, 8, MSG), F32),
        ),
        in_specs=[pl.BlockSpec(memory_space=pltpu.SMEM), vmem, vmem, pl.BlockSpec(memory_space=pl.ANY)],
        out_specs=(pl.BlockSpec(memory_space=pl.ANY), vmem, vmem),
        scratch_shapes=[pltpu.VMEM((NBLK, BLK), F32)] * 6
        + [pltpu.VMEM((BLK + 16, 128), F32)] * 4
        + [
            pltpu.VMEM((NT * STRIDE, 128), F32),
            pltpu.VMEM((128, 128), I32),
            pltpu.SMEM((128, 128), I32),
            pltpu.SemaphoreType.DMA,
            pltpu.VMEM((PTS, CAP), F32),
            pltpu.SemaphoreType.DMA,
            pltpu.VMEM((NT, LOAD, 128), F32),
            pltpu.SemaphoreType.DMA((NT // 4,)),
        ],
        compiler_params=pltpu.CompilerParams(vmem_limit_bytes=ROOM),
        name="route",
    )(counts, owners.reshape(128, 128), cells.reshape(128, 128), profiles)


FAR_N = 4


def far_kernel(side_ref, meta_ref, cells_ref, out_ref, table):
    one, nil = jnp.ones((), F32), jnp.zeros((), F32)
    m_rows = FAR_N * HALF

    @pl.when(pl.program_id(0) == 0)
    def _():
        cells = cells_ref[...].reshape(ROWS // 4, 4, 128)
        parts = [split(cells[:, q]) for q in range(4)]
        table[...] = jnp.concatenate([p[0] for p in parts] + [p[1] for p in parts], axis=1)

    sub = iota((128, 128), 0)
    ones8 = jnp.ones((8, 256), BF16)
    place = iota((m_rows, 128), 1).astype(F32)
    meta = meta_ref[...].reshape(m_rows, 128)
    for i in range(FAR_N):
        out_ref[i, 0:4] = side_ref[i, 0:4]
    for h in range(2):
        first = 0 if h == 0 else 64
        col = jnp.where(sub == first, one, nil) + jnp.where(sub == first + 1, 128.0 * one, nil)
        row = jnp.where(sub == first + 2, one, nil)
        got = dot(meta, jnp.concatenate([col, row], axis=1).astype(BF16))
        col, row = got[:, :128], got[:, 128:]
        hot = jnp.concatenate(
            [jnp.where(row == place + 128.0 * q, one, nil).astype(BF16) for q in range(2)], axis=1
        )
        val = dot(hot, table[...])
        got = jnp.zeros((m_rows, 128), F32)
        for q in range(4):
            both = val[:, 128 * q : 128 * q + 128] + val[:, 512 + 128 * q : 640 + 128 * q]
            got = jnp.where(col == place + 128.0 * q, both, got)
        v0, v1 = split(got)
        v = jnp.concatenate([v0, v1], axis=1)
        far = dot_nt(ones8, v)
        for i in range(FAR_N):
            for q in range(2):
                at = 256 * i + 128 * q
                out_ref[i, 4 + 2 * h + q : 5 + 2 * h + q] = far[0:1, at : at + 128]


def far_gather(rows, meta, table):
    side = pl.BlockSpec((FAR_N, 8, 128), lambda d: (d, HALF // 8, 0))
    return pl.pallas_call(
        far_kernel,
        grid=(NT // FAR_N,),
        out_shape=jax.ShapeDtypeStruct((NT, LOAD, 128), F32),
        in_specs=[
            side,
            pl.BlockSpec((FAR_N, HALF, 128), lambda d: (d, 0, 0)),
            pl.BlockSpec((ROWS, 128), lambda d: (0, 0)),
        ],
        out_specs=side,
        scratch_shapes=[pltpu.VMEM((256, 1024), BF16)],
        input_output_aliases={0: 0},
        compiler_params=pltpu.CompilerParams(vmem_limit_bytes=ROOM),
        cost_estimate=pl.CostEstimate(flops=10**10, bytes_accessed=8 << 20, transcendentals=0),
        name="far_gather",
    )(rows, meta, table)


def step_weights(radial_step):
    zero = jnp.zeros((PTS, PTS), F32)
    w = jnp.concatenate(
        [
            jnp.concatenate([radial_step.T, zero], axis=1),
            jnp.concatenate([zero, radial_step.T], axis=1),
        ],
        axis=0,
    )
    high = lax.reduce_precision(w, 8, 7)
    w0, w1 = high.astype(BF16), (w - high).astype(BF16)
    row = jnp.concatenate([w0, w1], axis=1)
    return jnp.concatenate([row, row], axis=0)


def flux_rows(flux_weights):
    zero = jnp.zeros((PTS,), F32)
    f = jnp.stack(
        [jnp.concatenate([flux_weights, zero]), jnp.concatenate([zero, flux_weights])]
        + [jnp.zeros((128,), F32)] * 6
    )
    return f / SUB


def substep(state, add, weights):
    s0, s1 = split(state)
    got = dot(jnp.concatenate([s0, s1], axis=1), weights)
    return (got[:, :128] + got[:, 128:]) + (add + 0.25 * jnp.tanh(state))


HEAT_N = 4


def far_columns(side):
    far = jnp.concatenate([side[4 + q : 5 + q] for q in range(4)], axis=1)
    rest = far - far.astype(BF16).astype(F32)
    row8 = iota((8, MSG), 0)
    terms = jnp.where(row8 == 0, far, jnp.where(row8 == 1, rest, 0.0)).astype(BF16)
    pick = jnp.where(iota((8, 128), 0) < 2, 1.0, 0.0).astype(BF16)
    return lax.dot_general(terms, pick, (((0,), (0,)), ((), ())), preferred_element_type=F32)


def heat_kernel(rows_ref, side_ref, fw_ref, weights_ref, flux_ref, heat_ref):
    weights = weights_ref[...]
    state = rows_ref[...].reshape(HEAT_N * HALF, 128)
    low_lanes = iota((HALF, 128), 1) < 64
    adds = []
    for i in range(HEAT_N):
        far = far_columns(side_ref[i])
        adds.append(fw_ref[...] * jnp.where(low_lanes, far[:HALF], far[HALF:]))
    add = jnp.concatenate(adds, axis=0)
    total = jnp.zeros_like(state)
    for _ in range(SUB):
        state = substep(state, add, weights)
        total = total + state
    t0, t1 = split(total)
    f0, f1 = split(flux_ref[...])
    heat = dot_nt(f0, t0) + dot_nt(f0, t1) + dot_nt(f1, t0)
    for i in range(HEAT_N):
        heat_ref[i] = heat[:, HALF * i : HALF * i + HALF]


def home_heat(rows, fw, weights, flux):
    block = pl.BlockSpec((HEAT_N, HALF, 128), lambda d: (d, 0, 0))
    return pl.pallas_call(
        heat_kernel,
        grid=(NT // HEAT_N,),
        out_shape=jax.ShapeDtypeStruct((NT, 8, HALF), F32),
        in_specs=[
            block,
            pl.BlockSpec((HEAT_N, 8, 128), lambda d: (d, HALF // 8, 0)),
            pl.BlockSpec((1, 128), lambda d: (0, 0)),
            pl.BlockSpec((256, 256), lambda d: (0, 0)),
            pl.BlockSpec((8, 128), lambda d: (0, 0)),
        ],
        out_specs=pl.BlockSpec((HEAT_N, 8, HALF), lambda d: (d, 0, 0)),
        compiler_params=pltpu.CompilerParams(vmem_limit_bytes=ROOM),
        cost_estimate=pl.CostEstimate(flops=2 * 10**10, bytes_accessed=8 << 20, transcendentals=SUB << 20),
        name="home_heat",
    )(rows, rows, fw, weights, flux)


DEP_N = 4


def deposit_kernel(
    lanes_ref, heat_ref, cells_ref, vel_ref, dif_ref, flux_ref, below_ref, above_ref, left_ref, right_ref,
    out_ref, acc,
):
    d = pl.program_id(0)

    @pl.when(d == 0)
    def _():
        acc[...] = jnp.zeros_like(acc)

    one, nil = jnp.ones((), F32), jnp.zeros((), F32)
    width = DEP_N * MSG
    cols, rows, heats = [], [], []
    for i in range(DEP_N):
        nums = lanes_ref[i]
        heat = jnp.concatenate([heat_ref[i, 0:1], heat_ref[i, 1:2]], axis=1)
        cols.append(nums[0:1])
        rows.append(nums[1:2])
        heats.append(jnp.where(nums[3:4] > 0.5, 0.5 * heat, nil))
    col = jnp.concatenate(cols, axis=1).astype(I32)
    row = jnp.concatenate(rows, axis=1).astype(I32)
    heat = jnp.concatenate(heats, axis=1)
    high = heat.astype(BF16).astype(F32)
    here = col == iota((128, width), 0)
    spread = jnp.concatenate(
        [jnp.where(here, high, nil).astype(BF16), jnp.where(here, heat - high, nil).astype(BF16)], axis=0
    )
    hot = jnp.where(row == iota((ROWS, width), 0), one, nil).astype(BF16)
    acc[...] += dot_nt(hot, spread)

    @pl.when(d == NT // DEP_N - 1)
    def _():
        layers = ROWS // 64
        wall, lane = iota((64, 128), 0), iota((64, 128), 1)
        left, right = left_ref[...], right_ref[...]
        for x in range(layers):
            at = 64 * x
            h = cells_ref[at : at + 64]
            x_lower = cells_ref[at - 64 : at] if x else below_ref[...]
            x_upper = cells_ref[at + 64 : at + 128] if x < layers - 1 else above_ref[...]
            w_lower = jnp.where(wall == 0, h, pltpu.roll(h, 1, 0))
            w_upper = jnp.where(wall == 63, h, pltpu.roll(h, 63, 0))
            s_lower = jnp.where(lane == 0, left[:, x : x + 1], pltpu.roll(h, 1, 1))
            s_upper = jnp.where(lane == 127, right[:, x : x + 1], pltpu.roll(h, 127, 1))
            laplace = (x_lower + x_upper) + (w_lower + w_upper) + (s_lower + s_upper) - 6.0 * h
            new = h + dif_ref[at : at + 64] * laplace - vel_ref[at : at + 64] * (h - x_lower)
            new = new + jnp.where(wall == 0, flux_ref[x : x + 1], nil)
            out_ref[at : at + 64] = new + (acc[at : at + 64, :128] + acc[at : at + 64, 128:])


def deposit(lanes, heat, cells, velocity, diffusivity, wall_flux, edges):
    def whole(shape):
        return pl.BlockSpec(shape, lambda d: (0, 0))

    field = whole((ROWS, 128))
    return pl.pallas_call(
        deposit_kernel,
        grid=(NT // DEP_N,),
        out_shape=jax.ShapeDtypeStruct((ROWS, 128), F32),
        in_specs=[
            pl.BlockSpec((DEP_N, 8, MSG), lambda d: (d, 0, 0)),
            pl.BlockSpec((DEP_N, 8, HALF), lambda d: (d, 0, 0)),
            field,
            field,
            field,
            whole((ROWS // 64, 128)),
            whole((64, 128)),
            whole((64, 128)),
            whole((64, ROWS // 64)),
            whole((64, ROWS // 64)),
        ],
        out_specs=field,
        scratch_shapes=[pltpu.VMEM((ROWS, 256), F32)],
        compiler_params=pltpu.CompilerParams(vmem_limit_bytes=40 * 2**20),
        cost_estimate=pl.CostEstimate(flops=10**10, bytes_accessed=4 << 20, transcendentals=0),
        name="deposit",
    )(lanes, heat, cells, velocity, diffusivity, wall_flux, *edges)


SETTLE = 1024


def settle_kernel(amount_ref, slot_ref, rows_ref, fw_ref, weights_ref, out_ref, stage, comb):
    low_lanes = iota((HALF, 128), 1) < 64

    @pl.loop(0, NT, unroll=4)
    def _(t):
        rows = rows_ref[t, 0:HALF]
        col = far_columns(rows_ref[t, HALF:LOAD])
        at = pl.multiple_of(t * MSG, MSG)
        comb[pl.ds(at, HALF)] = jnp.where(low_lanes, rows, col[:HALF])
        comb[pl.ds(pl.multiple_of(at + HALF, HALF), HALF)] = jnp.where(
            low_lanes, pltpu.roll(rows, 64, 1), col[HALF:]
        )

    @pl.loop(0, NT)
    def _(t):
        @pl.loop(0, (amount_ref[t] + 31) >> 5)
        def _(k):
            at = pl.multiple_of(t * MSG + 32 * k, 32)
            for i in range(32):
                stage[pl.ds(slot_ref[at + i], 1)] = comb[pl.ds(at + i, 1)]

    weights = weights_ref[...]
    fw = fw_ref[...]
    low_lanes = iota((SETTLE, 128), 1) < 64
    for c in range(OWN2 // SETTLE):
        at = c * SETTLE
        a = stage[at : at + SETTLE]
        b = stage[at + OWN2 : at + OWN2 + SETTLE]
        state = jnp.where(low_lanes, a, pltpu.roll(b, 64, 1))
        add = fw * jnp.where(low_lanes, pltpu.roll(a, 64, 1), b)
        for _ in range(SUB):
            state = substep(state, add, weights)
        for k in range(SETTLE // 128):
            turned = state[128 * k : 128 * k + 128].T
            out_ref[:, at + 128 * k : at + 128 * k + 128] = turned[:64]
            out_ref[:, at + OWN2 + 128 * k : at + OWN2 + 128 * k + 128] = turned[64:]


def settle(amount, slots, rows, fw, weights):
    vmem, smem = pl.BlockSpec(memory_space=pltpu.VMEM), pl.BlockSpec(memory_space=pltpu.SMEM)
    return pl.pallas_call(
        settle_kernel,
        out_shape=jax.ShapeDtypeStruct((PTS, OWN), F32),
        in_specs=[smem, smem, vmem, vmem, vmem],
        out_specs=vmem,
        scratch_shapes=[pltpu.VMEM((OWN + 8, 128), F32), pltpu.VMEM((NT * MSG, 128), F32)],
        compiler_params=pltpu.CompilerParams(vmem_limit_bytes=40 * 2**20),
        name="settle",
    )(amount, slots, rows, fw, weights)


def edges_of(cells):
    n_x, n_s = lax.axis_size("stream"), lax.axis_size("tile")
    x, s = lax.axis_index("stream"), lax.axis_index("tile")
    ends_x = jnp.stack([cells[0], cells[-1]])
    ends_s = jnp.stack([cells[:, :, 0].T, cells[:, :, -1].T])
    all_x = lax.all_gather(ends_x, "stream")
    all_s = lax.all_gather(ends_s.reshape(2, -1, 128), "tile")

    def of(arrays, i, end):
        return lax.dynamic_index_in_dim(arrays[:, end], i, 0, keepdims=False)

    below = jnp.where(x > 0, of(all_x, lax.rem(x + n_x - 1, n_x), 1), 0.0)
    above = jnp.where(x < n_x - 1, of(all_x, lax.rem(x + 1, n_x), 0), 0.0)
    left = of(all_s, lax.rem(s + n_s - 1, n_s), 1).reshape(ends_s.shape[1:])
    right = of(all_s, lax.rem(s + 1, n_s), 0).reshape(ends_s.shape[1:])
    return below, above, left, right


def on_device(
    enthalpy, velocity, diffusivity, wall_flux, profiles, counts, owners, cells,
    radial_step, far_weights, flux_weights,
):
    table = enthalpy.reshape(ROWS, 128)
    rows, meta, lanes = route(counts, owners, cells, profiles)
    rows = far_gather(rows, meta, table)
    rows, radial_step, far_weights, flux_weights = lax.optimization_barrier(
        (rows, radial_step, far_weights, flux_weights)
    )
    weights = step_weights(radial_step)
    fw = jnp.concatenate([far_weights, far_weights])[None, :]
    flux = flux_rows(flux_weights)
    got = lax.all_to_all(rows, "tile", split_axis=0, concat_axis=0, tiled=True)
    heat = home_heat(rows, fw, weights, flux)
    new_enthalpy = deposit(
        lanes, heat, table, velocity.reshape(ROWS, 128), diffusivity.reshape(ROWS, 128), wall_flux,
        edges_of(enthalpy),
    ).reshape(enthalpy.shape)
    slots = got[:, HALF : HALF + 4].reshape(NT, MSG).astype(I32)
    amount = jnp.sum((slots < OWN).astype(I32), axis=1)
    new_profiles = settle(amount, slots.reshape(-1), got, fw, weights)
    return new_enthalpy, new_profiles


def solution(mesh):
    return jax.shard_map(
        on_device,
        mesh=mesh,
        in_specs=(
            P("stream", None, "tile"),
            P("stream", None, "tile"),
            P("stream", None, "tile"),
            P("stream", "tile"),
            P(None, ("stream", "tile")),
            P(("stream", "tile")),
            P(("stream", "tile")),
            P(("stream", "tile")),
            P(),
            P(),
            P(),
        ),
        out_specs=(P("stream", None, "tile"), P(None, ("stream", "tile"))),
        check_vma=False,
    )
```

```python
import jax
import jax.numpy as jnp
from jax import lax
from jax.experimental import pallas as pl
from jax.experimental.pallas import tpu as pltpu
from jax.sharding import PartitionSpec as P

SUB = 16
PTS = 64
NT = 32
CAP = 16384
OWN = 6144
MSG = 512
HALF = MSG // 2
LOAD = HALF + 8
BLK = 256
NBLK = CAP // BLK
STRIDE = MSG + 16
ROWS = 1024
OWN2 = OWN // 2

ROOM = 60 * 2**20

F32, BF16, I32 = jnp.float32, jnp.bfloat16, jnp.int32
NTD = (((1,), (1,)), ((), ()))


def iota(shape, dim):
    return lax.broadcasted_iota(I32, shape, dim)


def split(x):
    high = x.astype(BF16)
    return high, (x - high.astype(F32)).astype(BF16)


def dot(a, b):
    return jnp.dot(a, b, preferred_element_type=F32)


def dot_nt(a, b):
    return lax.dot_general(a, b, NTD, preferred_element_type=F32)


def route_kernel(
    count_ref, owners_ref, cells_ref, prof_ref,
    rows_ref, meta_ref, lanes_ref,
    pos_s, m0_s, m1_s, m2_s, m3_s, m4_s, sorted_a, sorted_b, sorted_c, sorted_d,
    bucket, tab_v, tab_s, sem, prof_v, prof_sem, pack_v, pack_sem,
):
    count = count_ref[0]
    fetch = pltpu.make_async_copy(prof_ref, prof_v, prof_sem)
    fetch.start()

    def blocks(ref):
        x = ref[...].reshape(NBLK, 2, 128)
        return jnp.concatenate([x[:, 0], x[:, 1]], axis=1)

    slot = iota((NBLK, BLK), 0) * BLK + iota((NBLK, BLK), 1)
    owners = blocks(owners_ref)
    dest = jnp.floor((owners.astype(F32) + 0.5) * (1.0 / OWN)).astype(I32)
    within = owners - dest * OWN
    live = slot < count
    dest = jnp.where(live, dest, NT)
    cells = blocks(cells_ref)
    m0_s[...] = (cells & 127).astype(F32)
    m1_s[...] = ((cells >> 7) & 3).astype(F32)
    m2_s[...] = (cells >> 9).astype(F32)
    m3_s[...] = (within & 255).astype(F32)
    m4_s[...] = (within >> 8).astype(F32)

    sub, lane = iota((BLK, BLK), 0), iota((BLK, BLK), 1)
    one, nil = jnp.ones((), F32), jnp.zeros((), F32)
    before = jnp.where(sub < lane, one, nil).astype(BF16)
    same_block = (sub >> 5) == (lane >> 5)
    same_dest = (sub & 31) == (lane & 31)
    seg_left = jnp.where(same_block & (lane < sub), one, nil).astype(BF16)
    seg_right = jnp.where(same_block & (sub < lane), one, nil).astype(BF16)
    base_right = jnp.where(same_dest & ((sub >> 5) < (lane >> 5)), one, nil).astype(BF16)
    all_right = jnp.where(same_dest, one, nil).astype(BF16)
    ones_a = jnp.ones((8, BLK), BF16)
    ones_b = jnp.ones((BLK, 128), BF16)
    run = jnp.zeros((8, BLK), F32)
    longest = jnp.zeros((8, BLK), F32)
    for c in range(8):
        part = dest[8 * c : 8 * c + 8]
        hot = jnp.where(part[:, None, :] == iota((8, NT, BLK), 1), one, nil).reshape(BLK, BLK)
        hot_b = hot.astype(BF16)
        prefix = dot(hot_b, before)
        amount = dot(hot_b, ones_b)
        seg = dot(seg_left, amount.astype(BF16))
        seg2 = jnp.concatenate([seg, seg], axis=1)
        pos = jnp.sum((hot * (prefix + seg2)).reshape(8, NT, BLK), axis=1)
        pos_s[8 * c : 8 * c + 8] = jnp.where(live[8 * c : 8 * c + 8], pos, 511.0)
        amount_l = dot_nt(ones_a, hot_b)
        amount_lb = amount_l.astype(BF16)
        src = dot(amount_lb, seg_right)
        base = dot(amount_lb, base_right) + run
        run = run + dot(amount_lb, all_right)
        longest = jnp.maximum(longest, amount_l)
        most = amount_l
        for shift in (1, 2, 4, 8, 16):
            most = jnp.maximum(most, pltpu.roll(most, BLK - shift, 1))
        first = iota((8, BLK), 1) & 31
        row8 = iota((8, BLK), 0)
        packed = jnp.where(row8 == 0, src, nil)
        packed = jnp.where(row8 == 1, base + (first * STRIDE).astype(F32), packed)
        packed = jnp.where(row8 == 2, amount_l, packed)
        packed = jnp.where(row8 == 3, most, packed)
        packed = packed.astype(I32)
        tab_v[16 * c : 16 * c + 8] = packed[:, :128]
        tab_v[16 * c + 8 : 16 * c + 16] = packed[:, 128:]
    copy = pltpu.make_async_copy(tab_v, tab_s, sem)
    copy.start()
    short = jnp.max(longest) <= 8.0
    total = run

    zero8 = jnp.zeros((STRIDE, 128), F32)

    @pl.loop(0, NT)
    def _(d):
        bucket[pl.ds(pl.multiple_of(d * STRIDE, 8), STRIDE)] = zero8

    copy.wait()
    fetch.wait()

    meta_rest = jnp.zeros((56, BLK), BF16)
    low_rest = jnp.zeros((64, BLK), BF16)
    row8 = iota((8, BLK), 0)

    def sort_block(j, out):
        x = prof_v[:, pl.ds(pl.multiple_of(j * BLK, BLK), BLK)]
        high, low = split(x)
        meta = jnp.zeros((8, BLK), F32)
        for k, ref in enumerate((m0_s, m1_s, m2_s, m3_s, m4_s)):
            meta = jnp.where(row8 == k, ref[pl.ds(j, 1), :], meta)
        data = jnp.concatenate([high, meta.astype(BF16), meta_rest, low, low_rest], axis=0)
        place = pos_s[pl.ds(j, 1), :].astype(I32)
        perm = jnp.where(place == sub, one, nil).astype(BF16)
        got = dot_nt(perm, data)
        out[0:BLK] = got[:, :128] + got[:, 128:]

    def copy_block(j, inp):
        chunk = (j >> 2) * 8
        at = (j & 3) * NT
        most = tab_s[chunk + 3, at]

        @pl.when(most <= 8)
        def _():
            for d in range(NT):
                src = tab_s[chunk, at + d]
                dst = tab_s[chunk + 1, at + d]
                bucket[pl.ds(dst, 8)] = inp[pl.ds(src, 8)]

        @pl.when((most > 8) & (most <= 16))
        def _():
            for d in range(NT):
                src = tab_s[chunk, at + d]
                dst = tab_s[chunk + 1, at + d]
                bucket[pl.ds(dst, 16)] = inp[pl.ds(src, 16)]

        @pl.when(most > 16)
        def _():
            @pl.loop(0, NT)
            def _(d):
                src = tab_s[chunk, at + d]
                dst = tab_s[chunk + 1, at + d]

                @pl.loop(0, (tab_s[chunk + 2, at + d] + 7) >> 3)
                def _(k):
                    bucket[pl.ds(dst + 8 * k, 8)] = inp[pl.ds(src + 8 * k, 8)]

    def copy_short(j, inp):
        chunk = (j >> 2) * 8
        at = (j & 3) * NT
        for d in range(NT):
            src = tab_s[chunk, at + d]
            dst = tab_s[chunk + 1, at + d]
            bucket[pl.ds(dst, 8)] = inp[pl.ds(src, 8)]

    for ref in (sorted_a, sorted_b, sorted_c, sorted_d):
        ref[BLK:] = jnp.zeros((16, 128), F32)
    quads = (count + 4 * BLK - 1) // (4 * BLK)
    sort_block(0, sorted_a)
    sort_block(1, sorted_b)

    def quad(copy_any):
        @pl.loop(0, quads)
        def _(p):
            sort_block(4 * p + 2, sorted_c)
            copy_any(4 * p, sorted_a)
            sort_block(4 * p + 3, sorted_d)
            copy_any(4 * p + 1, sorted_b)
            sort_block(jnp.minimum(4 * p + 4, NBLK - 1), sorted_a)
            copy_any(4 * p + 2, sorted_c)
            sort_block(jnp.minimum(4 * p + 5, NBLK - 1), sorted_b)
            copy_any(4 * p + 3, sorted_d)

    pl.when(short)(lambda: quad(copy_short))
    pl.when(jnp.logical_not(short))(lambda: quad(copy_block))

    low_lanes = iota((HALF, 128), 1) < 64
    r8, l8 = iota((8, 128), 0), iota((8, 128), 1)
    pick = jnp.where((r8 == 0) & (l8 == 64), one, nil)
    pick = jnp.where((r8 == 1) & (l8 == 65), one, pick)
    pick = jnp.where((r8 == 1) & (l8 == 66), 4.0 * one, pick)
    pick = jnp.where((r8 == 2) & (l8 == 67), one, pick)
    pick = jnp.where((r8 == 2) & (l8 == 68), 256.0 * one, pick)
    pick = pick.astype(BF16)
    rank = iota((8, MSG), 1)
    rank_row = iota((8, MSG), 0)
    lane_dest = iota((8, BLK), 1)

    def send(g):
        part = pl.ds(g * 4, 4)
        return pltpu.make_async_copy(pack_v.at[part], rows_ref.at[part], pack_sem.at[g])

    @pl.loop(0, NT // 4)
    def _(g):
        for k in range(4):
            d = 4 * g + k
            at = pl.multiple_of(d * STRIDE, 8)
            lo = bucket[pl.ds(at, HALF)]
            hi = bucket[pl.ds(pl.multiple_of(at + HALF, 8), HALF)]
            pack_v[d, 0:HALF] = jnp.where(low_lanes, lo, pltpu.roll(hi, 64, 1))
            meta_ref[d] = jnp.where(low_lanes, pltpu.roll(lo, 64, 1), hi).astype(BF16)
            both = jnp.concatenate([lo, hi], axis=0).astype(BF16)
            nums = dot_nt(pick, both)
            mine = jnp.max(jnp.where(lane_dest == d, total, nil), axis=1, keepdims=True)
            valid = rank.astype(F32) < mine
            nums = jnp.where((rank_row == 2) & ~valid, float(OWN), nums)
            nums = jnp.where(rank_row == 3, jnp.where(valid, one, nil), nums)
            lanes_ref[d] = nums
            pack_v[d, HALF:LOAD] = jnp.concatenate(
                [nums[2:3, 128 * q : 128 * q + 128] for q in range(4)] + [jnp.zeros((4, 128), F32)],
                axis=0,
            )
        send(g).start()

    for g in range(NT // 4):
        send(g).wait()


def route(counts, owners, cells, profiles):
    vmem = pl.BlockSpec(memory_space=pltpu.VMEM)
    return pl.pallas_call(
        route_kernel,
        out_shape=(
            jax.ShapeDtypeStruct((NT, LOAD, 128), F32),
            jax.ShapeDtypeStruct((NT, HALF, 128), BF16),
            jax.ShapeDtypeStruct((NT, 8, MSG), F32),
        ),
        in_specs=[pl.BlockSpec(memory_space=pltpu.SMEM), vmem, vmem, pl.BlockSpec(memory_space=pl.ANY)],
        out_specs=(pl.BlockSpec(memory_space=pl.ANY), vmem, vmem),
        scratch_shapes=[pltpu.VMEM((NBLK, BLK), F32)] * 6
        + [pltpu.VMEM((BLK + 16, 128), F32)] * 4
        + [
            pltpu.VMEM((NT * STRIDE, 128), F32),
            pltpu.VMEM((128, 128), I32),
            pltpu.SMEM((128, 128), I32),
            pltpu.SemaphoreType.DMA,
            pltpu.VMEM((PTS, CAP), F32),
            pltpu.SemaphoreType.DMA,
            pltpu.VMEM((NT, LOAD, 128), F32),
            pltpu.SemaphoreType.DMA((NT // 4,)),
        ],
        compiler_params=pltpu.CompilerParams(vmem_limit_bytes=ROOM),
        name="route",
    )(counts, owners.reshape(128, 128), cells.reshape(128, 128), profiles)


FAR_N = 4


def far_kernel(side_ref, meta_ref, cells_ref, out_ref, table):
    one, nil = jnp.ones((), F32), jnp.zeros((), F32)
    m_rows = FAR_N * HALF

    @pl.when(pl.program_id(0) == 0)
    def _():
        cells = cells_ref[...].reshape(ROWS // 4, 4, 128)
        parts = [split(cells[:, q]) for q in range(4)]
        table[...] = jnp.concatenate([p[0] for p in parts] + [p[1] for p in parts], axis=1)

    sub = iota((128, 128), 0)
    ones8 = jnp.ones((8, 256), BF16)
    place = iota((m_rows, 128), 1).astype(F32)
    meta = meta_ref[...].reshape(m_rows, 128)
    for i in range(FAR_N):
        out_ref[i, 0:4] = side_ref[i, 0:4]
    for h in range(2):
        first = 0 if h == 0 else 64
        col = jnp.where(sub == first, one, nil) + jnp.where(sub == first + 1, 128.0 * one, nil)
        row = jnp.where(sub == first + 2, one, nil)
        got = dot(meta, jnp.concatenate([col, row], axis=1).astype(BF16))
        col, row = got[:, :128], got[:, 128:]
        hot = jnp.concatenate(
            [jnp.where(row == place + 128.0 * q, one, nil).astype(BF16) for q in range(2)], axis=1
        )
        val = dot(hot, table[...])
        got = jnp.zeros((m_rows, 128), F32)
        for q in range(4):
            both = val[:, 128 * q : 128 * q + 128] + val[:, 512 + 128 * q : 640 + 128 * q]
            got = jnp.where(col == place + 128.0 * q, both, got)
        v0, v1 = split(got)
        v = jnp.concatenate([v0, v1], axis=1)
        far = dot_nt(ones8, v)
        for i in range(FAR_N):
            for q in range(2):
                at = 256 * i + 128 * q
                out_ref[i, 4 + 2 * h + q : 5 + 2 * h + q] = far[0:1, at : at + 128]


def far_gather(rows, meta, table):
    side = pl.BlockSpec((FAR_N, 8, 128), lambda d: (d, HALF // 8, 0))
    return pl.pallas_call(
        far_kernel,
        grid=(NT // FAR_N,),
        out_shape=jax.ShapeDtypeStruct((NT, LOAD, 128), F32),
        in_specs=[
            side,
            pl.BlockSpec((FAR_N, HALF, 128), lambda d: (d, 0, 0)),
            pl.BlockSpec((ROWS, 128), lambda d: (0, 0)),
        ],
        out_specs=side,
        scratch_shapes=[pltpu.VMEM((256, 1024), BF16)],
        input_output_aliases={0: 0},
        compiler_params=pltpu.CompilerParams(vmem_limit_bytes=ROOM),
        cost_estimate=pl.CostEstimate(flops=10**10, bytes_accessed=8 << 20, transcendentals=0),
        name="far_gather",
    )(rows, meta, table)


def step_weights(radial_step):
    zero = jnp.zeros((PTS, PTS), F32)
    w = jnp.concatenate(
        [
            jnp.concatenate([radial_step.T, zero], axis=1),
            jnp.concatenate([zero, radial_step.T], axis=1),
        ],
        axis=0,
    )
    high = lax.reduce_precision(w, 8, 7)
    w0, w1 = high.astype(BF16), (w - high).astype(BF16)
    row = jnp.concatenate([w0, w1], axis=1)
    return jnp.concatenate([row, row], axis=0)


def flux_rows(flux_weights):
    zero = jnp.zeros((PTS,), F32)
    f = jnp.stack(
        [jnp.concatenate([flux_weights, zero]), jnp.concatenate([zero, flux_weights])]
        + [jnp.zeros((128,), F32)] * 6
    )
    return f / SUB


def substep(state, add, weights):
    s0, s1 = split(state)
    got = dot(jnp.concatenate([s0, s1], axis=1), weights)
    return (got[:, :128] + got[:, 128:]) + (add + 0.25 * jnp.tanh(state))


HEAT_N = 4


def far_columns(side):
    far = jnp.concatenate([side[4 + q : 5 + q] for q in range(4)], axis=1)
    rest = far - far.astype(BF16).astype(F32)
    row8 = iota((8, MSG), 0)
    terms = jnp.where(row8 == 0, far, jnp.where(row8 == 1, rest, 0.0)).astype(BF16)
    pick = jnp.where(iota((8, 128), 0) < 2, 1.0, 0.0).astype(BF16)
    return lax.dot_general(terms, pick, (((0,), (0,)), ((), ())), preferred_element_type=F32)


def heat_kernel(rows_ref, side_ref, fw_ref, weights_ref, flux_ref, heat_ref):
    weights = weights_ref[...]
    state = rows_ref[...].reshape(HEAT_N * HALF, 128)
    low_lanes = iota((HALF, 128), 1) < 64
    adds = []
    for i in range(HEAT_N):
        far = far_columns(side_ref[i])
        adds.append(fw_ref[...] * jnp.where(low_lanes, far[:HALF], far[HALF:]))
    add = jnp.concatenate(adds, axis=0)
    total = jnp.zeros_like(state)
    for _ in range(SUB):
        state = substep(state, add, weights)
        total = total + state
    t0, t1 = split(total)
    f0, f1 = split(flux_ref[...])
    heat = dot_nt(f0, t0) + dot_nt(f0, t1) + dot_nt(f1, t0)
    for i in range(HEAT_N):
        heat_ref[i] = heat[:, HALF * i : HALF * i + HALF]


def home_heat(rows, fw, weights, flux):
    block = pl.BlockSpec((HEAT_N, HALF, 128), lambda d: (d, 0, 0))
    return pl.pallas_call(
        heat_kernel,
        grid=(NT // HEAT_N,),
        out_shape=jax.ShapeDtypeStruct((NT, 8, HALF), F32),
        in_specs=[
            block,
            pl.BlockSpec((HEAT_N, 8, 128), lambda d: (d, HALF // 8, 0)),
            pl.BlockSpec((1, 128), lambda d: (0, 0)),
            pl.BlockSpec((256, 256), lambda d: (0, 0)),
            pl.BlockSpec((8, 128), lambda d: (0, 0)),
        ],
        out_specs=pl.BlockSpec((HEAT_N, 8, HALF), lambda d: (d, 0, 0)),
        compiler_params=pltpu.CompilerParams(vmem_limit_bytes=ROOM),
        cost_estimate=pl.CostEstimate(flops=2 * 10**10, bytes_accessed=8 << 20, transcendentals=SUB << 20),
        name="home_heat",
    )(rows, rows, fw, weights, flux)


DEP_N = 4


def deposit_kernel(
    lanes_ref, heat_ref, cells_ref, vel_ref, dif_ref, flux_ref, below_ref, above_ref, left_ref, right_ref,
    out_ref, acc,
):
    d = pl.program_id(0)

    @pl.when(d == 0)
    def _():
        acc[...] = jnp.zeros_like(acc)

    one, nil = jnp.ones((), F32), jnp.zeros((), F32)
    width = DEP_N * MSG
    cols, rows, heats = [], [], []
    for i in range(DEP_N):
        nums = lanes_ref[i]
        heat = jnp.concatenate([heat_ref[i, 0:1], heat_ref[i, 1:2]], axis=1)
        cols.append(nums[0:1])
        rows.append(nums[1:2])
        heats.append(jnp.where(nums[3:4] > 0.5, 0.5 * heat, nil))
    col = jnp.concatenate(cols, axis=1).astype(I32)
    row = jnp.concatenate(rows, axis=1).astype(I32)
    heat = jnp.concatenate(heats, axis=1)
    high = heat.astype(BF16).astype(F32)
    here = col == iota((128, width), 0)
    spread = jnp.concatenate(
        [jnp.where(here, high, nil).astype(BF16), jnp.where(here, heat - high, nil).astype(BF16)], axis=0
    )
    hot = jnp.where(row == iota((ROWS, width), 0), one, nil).astype(BF16)
    acc[...] += dot_nt(hot, spread)

    @pl.when(d == NT // DEP_N - 1)
    def _():
        layers = ROWS // 64
        wall, lane = iota((64, 128), 0), iota((64, 128), 1)
        left, right = left_ref[...], right_ref[...]
        for x in range(layers):
            at = 64 * x
            h = cells_ref[at : at + 64]
            x_lower = cells_ref[at - 64 : at] if x else below_ref[...]
            x_upper = cells_ref[at + 64 : at + 128] if x < layers - 1 else above_ref[...]
            w_lower = jnp.where(wall == 0, h, pltpu.roll(h, 1, 0))
            w_upper = jnp.where(wall == 63, h, pltpu.roll(h, 63, 0))
            s_lower = jnp.where(lane == 0, left[:, x : x + 1], pltpu.roll(h, 1, 1))
            s_upper = jnp.where(lane == 127, right[:, x : x + 1], pltpu.roll(h, 127, 1))
            laplace = (x_lower + x_upper) + (w_lower + w_upper) + (s_lower + s_upper) - 6.0 * h
            new = h + dif_ref[at : at + 64] * laplace - vel_ref[at : at + 64] * (h - x_lower)
            new = new + jnp.where(wall == 0, flux_ref[x : x + 1], nil)
            out_ref[at : at + 64] = new + (acc[at : at + 64, :128] + acc[at : at + 64, 128:])


def deposit(lanes, heat, cells, velocity, diffusivity, wall_flux, edges):
    def whole(shape):
        return pl.BlockSpec(shape, lambda d: (0, 0))

    field = whole((ROWS, 128))
    return pl.pallas_call(
        deposit_kernel,
        grid=(NT // DEP_N,),
        out_shape=jax.ShapeDtypeStruct((ROWS, 128), F32),
        in_specs=[
            pl.BlockSpec((DEP_N, 8, MSG), lambda d: (d, 0, 0)),
            pl.BlockSpec((DEP_N, 8, HALF), lambda d: (d, 0, 0)),
            field,
            field,
            field,
            whole((ROWS // 64, 128)),
            whole((64, 128)),
            whole((64, 128)),
            whole((64, ROWS // 64)),
            whole((64, ROWS // 64)),
        ],
        out_specs=field,
        scratch_shapes=[pltpu.VMEM((ROWS, 256), F32)],
        compiler_params=pltpu.CompilerParams(vmem_limit_bytes=40 * 2**20),
        cost_estimate=pl.CostEstimate(flops=10**10, bytes_accessed=4 << 20, transcendentals=0),
        name="deposit",
    )(lanes, heat, cells, velocity, diffusivity, wall_flux, *edges)


SETTLE = 1024


def settle_kernel(amount_ref, slot_ref, rows_ref, fw_ref, weights_ref, out_ref, stage, comb):
    low_lanes = iota((HALF, 128), 1) < 64

    @pl.loop(0, NT, unroll=4)
    def _(t):
        rows = rows_ref[t, 0:HALF]
        col = far_columns(rows_ref[t, HALF:LOAD])
        at = pl.multiple_of(t * MSG, MSG)
        comb[pl.ds(at, HALF)] = jnp.where(low_lanes, rows, col[:HALF])
        comb[pl.ds(pl.multiple_of(at + HALF, HALF), HALF)] = jnp.where(
            low_lanes, pltpu.roll(rows, 64, 1), col[HALF:]
        )

    @pl.loop(0, NT)
    def _(t):
        @pl.loop(0, (amount_ref[t] + 31) >> 5)
        def _(k):
            at = pl.multiple_of(t * MSG + 32 * k, 32)
            for i in range(32):
                stage[pl.ds(slot_ref[at + i], 1)] = comb[pl.ds(at + i, 1)]

    weights = weights_ref[...]
    fw = fw_ref[...]
    low_lanes = iota((SETTLE, 128), 1) < 64
    for c in range(OWN2 // SETTLE):
        at = c * SETTLE
        a = stage[at : at + SETTLE]
        b = stage[at + OWN2 : at + OWN2 + SETTLE]
        state = jnp.where(low_lanes, a, pltpu.roll(b, 64, 1))
        add = fw * jnp.where(low_lanes, pltpu.roll(a, 64, 1), b)
        for _ in range(SUB):
            state = substep(state, add, weights)
        for k in range(SETTLE // 128):
            turned = state[128 * k : 128 * k + 128].T
            out_ref[:, at + 128 * k : at + 128 * k + 128] = turned[:64]
            out_ref[:, at + OWN2 + 128 * k : at + OWN2 + 128 * k + 128] = turned[64:]


def settle(amount, slots, rows, fw, weights):
    vmem, smem = pl.BlockSpec(memory_space=pltpu.VMEM), pl.BlockSpec(memory_space=pltpu.SMEM)
    return pl.pallas_call(
        settle_kernel,
        out_shape=jax.ShapeDtypeStruct((PTS, OWN), F32),
        in_specs=[smem, smem, vmem, vmem, vmem],
        out_specs=vmem,
        scratch_shapes=[pltpu.VMEM((OWN + 8, 128), F32), pltpu.VMEM((NT * MSG, 128), F32)],
        compiler_params=pltpu.CompilerParams(vmem_limit_bytes=40 * 2**20),
        name="settle",
    )(amount, slots, rows, fw, weights)


def edges_of(cells):
    n_x, n_s = lax.axis_size("stream"), lax.axis_size("tile")
    up_x = [(i, i + 1) for i in range(n_x - 1)]
    down_x = [(i + 1, i) for i in range(n_x - 1)]
    up_s = [(i, (i + 1) % n_s) for i in range(n_s)]
    down_s = [((i + 1) % n_s, i) for i in range(n_s)]
    below = lax.ppermute(cells[-1], "stream", up_x)
    above = lax.ppermute(cells[0], "stream", down_x)
    left = lax.ppermute(cells[:, :, -1], "tile", up_s)
    right = lax.ppermute(cells[:, :, 0], "tile", down_s)
    return below, above, left.T, right.T


def on_device(
    enthalpy, velocity, diffusivity, wall_flux, profiles, counts, owners, cells,
    radial_step, far_weights, flux_weights,
):
    table = enthalpy.reshape(ROWS, 128)
    rows, meta, lanes = route(counts, owners, cells, profiles)
    rows = far_gather(rows, meta, table)
    rows, radial_step, far_weights, flux_weights = lax.optimization_barrier(
        (rows, radial_step, far_weights, flux_weights)
    )
    weights = step_weights(radial_step)
    fw = jnp.concatenate([far_weights, far_weights])[None, :]
    flux = flux_rows(flux_weights)
    got = lax.all_to_all(rows, "tile", split_axis=0, concat_axis=0, tiled=True)
    heat = home_heat(rows, fw, weights, flux)
    ends, heat = lax.optimization_barrier((enthalpy, heat))
    new_enthalpy = deposit(
        lanes, heat, table, velocity.reshape(ROWS, 128), diffusivity.reshape(ROWS, 128), wall_flux,
        edges_of(ends),
    ).reshape(enthalpy.shape)
    slots = got[:, HALF : HALF + 4].reshape(NT, MSG).astype(I32)
    amount = jnp.sum((slots < OWN).astype(I32), axis=1)
    new_profiles = settle(amount, slots.reshape(-1), got, fw, weights)
    return new_enthalpy, new_profiles


def solution(mesh):
    return jax.shard_map(
        on_device,
        mesh=mesh,
        in_specs=(
            P("stream", None, "tile"),
            P("stream", None, "tile"),
            P("stream", None, "tile"),
            P("stream", "tile"),
            P(None, ("stream", "tile")),
            P(("stream", "tile")),
            P(("stream", "tile")),
            P(("stream", "tile")),
            P(),
            P(),
            P(),
        ),
        out_specs=(P("stream", None, "tile"), P(None, ("stream", "tile"))),
        check_vma=False,
    )
```

```python
import jax
import jax.numpy as jnp
from jax import lax
from jax.experimental import pallas as pl
from jax.experimental.pallas import tpu as pltpu
from jax.sharding import PartitionSpec as P

SUB = 16
PTS = 64
NT = 32
CAP = 16384
OWN = 6144
MSG = 512
HALF = MSG // 2
LOAD = HALF + 8
BLK = 256
NBLK = CAP // BLK
STRIDE = MSG + 16
ROWS = 1024
OWN2 = OWN // 2

GROUP = 4
ROOM = 60 * 2**20

F32, BF16, I32 = jnp.float32, jnp.bfloat16, jnp.int32
NTD = (((1,), (1,)), ((), ()))


def iota(shape, dim):
    return lax.broadcasted_iota(I32, shape, dim)


def split(x):
    high = x.astype(BF16)
    return high, (x - high.astype(F32)).astype(BF16)


def dot(a, b):
    return jnp.dot(a, b, preferred_element_type=F32)


def dot_nt(a, b):
    return lax.dot_general(a, b, NTD, preferred_element_type=F32)


def route_kernel(
    count_ref, owners_ref, cells_ref, field_ref, prof_ref,
    rows_ref, lanes_ref, ends_ref,
    pos_s, m0_s, m1_s, m2_s, m3_s, m4_s, sorted_a, sorted_b, sorted_c, sorted_d,
    bucket, tab_v, tab_s, sem, prof_v, prof_sem, pack_v, pack_sem, meta_v, table,
):
    count = count_ref[0]
    fetch = pltpu.make_async_copy(prof_ref, prof_v, prof_sem)
    fetch.start()

    def blocks(ref):
        x = ref[...].reshape(NBLK, 2, 128)
        return jnp.concatenate([x[:, 0], x[:, 1]], axis=1)

    slot = iota((NBLK, BLK), 0) * BLK + iota((NBLK, BLK), 1)
    owners = blocks(owners_ref)
    dest = jnp.floor((owners.astype(F32) + 0.5) * (1.0 / OWN)).astype(I32)
    within = owners - dest * OWN
    live = slot < count
    dest = jnp.where(live, dest, NT)
    cells = blocks(cells_ref)
    m0_s[...] = (cells & 127).astype(F32)
    m1_s[...] = ((cells >> 7) & 3).astype(F32)
    m2_s[...] = (cells >> 9).astype(F32)
    m3_s[...] = (within & 255).astype(F32)
    m4_s[...] = (within >> 8).astype(F32)

    sub, lane = iota((BLK, BLK), 0), iota((BLK, BLK), 1)
    one, nil = jnp.ones((), F32), jnp.zeros((), F32)
    before = jnp.where(sub < lane, one, nil).astype(BF16)
    same_block = (sub >> 5) == (lane >> 5)
    same_dest = (sub & 31) == (lane & 31)
    seg_left = jnp.where(same_block & (lane < sub), one, nil).astype(BF16)
    seg_right = jnp.where(same_block & (sub < lane), one, nil).astype(BF16)
    base_right = jnp.where(same_dest & ((sub >> 5) < (lane >> 5)), one, nil).astype(BF16)
    all_right = jnp.where(same_dest, one, nil).astype(BF16)
    ones_a = jnp.ones((8, BLK), BF16)
    ones_b = jnp.ones((BLK, 128), BF16)
    run = jnp.zeros((8, BLK), F32)
    longest = jnp.zeros((8, BLK), F32)
    for c in range(8):
        part = dest[8 * c : 8 * c + 8]
        hot = jnp.where(part[:, None, :] == iota((8, NT, BLK), 1), one, nil).reshape(BLK, BLK)
        hot_b = hot.astype(BF16)
        prefix = dot(hot_b, before)
        amount = dot(hot_b, ones_b)
        seg = dot(seg_left, amount.astype(BF16))
        seg2 = jnp.concatenate([seg, seg], axis=1)
        pos = jnp.sum((hot * (prefix + seg2)).reshape(8, NT, BLK), axis=1)
        pos_s[8 * c : 8 * c + 8] = jnp.where(live[8 * c : 8 * c + 8], pos, 511.0)
        amount_l = dot_nt(ones_a, hot_b)
        amount_lb = amount_l.astype(BF16)
        src = dot(amount_lb, seg_right)
        base = dot(amount_lb, base_right) + run
        run = run + dot(amount_lb, all_right)
        longest = jnp.maximum(longest, amount_l)
        most = amount_l
        for shift in (1, 2, 4, 8, 16):
            most = jnp.maximum(most, pltpu.roll(most, BLK - shift, 1))
        first = iota((8, BLK), 1) & 31
        row8 = iota((8, BLK), 0)
        packed = jnp.where(row8 == 0, src, nil)
        packed = jnp.where(row8 == 1, base + (first * STRIDE).astype(F32), packed)
        packed = jnp.where(row8 == 2, amount_l, packed)
        packed = jnp.where(row8 == 3, most, packed)
        packed = packed.astype(I32)
        tab_v[16 * c : 16 * c + 8] = packed[:, :128]
        tab_v[16 * c + 8 : 16 * c + 16] = packed[:, 128:]
    copy = pltpu.make_async_copy(tab_v, tab_s, sem)
    copy.start()
    short = jnp.max(longest) <= 8.0
    total = run

    zero8 = jnp.zeros((STRIDE, 128), F32)

    @pl.loop(0, NT)
    def _(d):
        bucket[pl.ds(pl.multiple_of(d * STRIDE, 8), STRIDE)] = zero8

    copy.wait()
    fetch.wait()

    meta_rest = jnp.zeros((56, BLK), BF16)
    low_rest = jnp.zeros((64, BLK), BF16)
    row8 = iota((8, BLK), 0)

    def sort_block(j, out):
        x = prof_v[:, pl.ds(pl.multiple_of(j * BLK, BLK), BLK)]
        high, low = split(x)
        meta = jnp.zeros((8, BLK), F32)
        for k, ref in enumerate((m0_s, m1_s, m2_s, m3_s, m4_s)):
            meta = jnp.where(row8 == k, ref[pl.ds(j, 1), :], meta)
        data = jnp.concatenate([high, meta.astype(BF16), meta_rest, low, low_rest], axis=0)
        place = pos_s[pl.ds(j, 1), :].astype(I32)
        perm = jnp.where(place == sub, one, nil).astype(BF16)
        got = dot_nt(perm, data)
        out[0:BLK] = got[:, :128] + got[:, 128:]

    def copy_block(j, inp):
        chunk = (j >> 2) * 8
        at = (j & 3) * NT
        most = tab_s[chunk + 3, at]

        @pl.when(most <= 8)
        def _():
            for d in range(NT):
                src = tab_s[chunk, at + d]
                dst = tab_s[chunk + 1, at + d]
                bucket[pl.ds(dst, 8)] = inp[pl.ds(src, 8)]

        @pl.when((most > 8) & (most <= 16))
        def _():
            for d in range(NT):
                src = tab_s[chunk, at + d]
                dst = tab_s[chunk + 1, at + d]
                bucket[pl.ds(dst, 16)] = inp[pl.ds(src, 16)]

        @pl.when(most > 16)
        def _():
            @pl.loop(0, NT)
            def _(d):
                src = tab_s[chunk, at + d]
                dst = tab_s[chunk + 1, at + d]

                @pl.loop(0, (tab_s[chunk + 2, at + d] + 7) >> 3)
                def _(k):
                    bucket[pl.ds(dst + 8 * k, 8)] = inp[pl.ds(src + 8 * k, 8)]

    def copy_short(j, inp):
        chunk = (j >> 2) * 8
        at = (j & 3) * NT
        for d in range(NT):
            src = tab_s[chunk, at + d]
            dst = tab_s[chunk + 1, at + d]
            bucket[pl.ds(dst, 8)] = inp[pl.ds(src, 8)]

    for ref in (sorted_a, sorted_b, sorted_c, sorted_d):
        ref[BLK:] = jnp.zeros((16, 128), F32)
    quads = (count + 4 * BLK - 1) // (4 * BLK)
    sort_block(0, sorted_a)
    sort_block(1, sorted_b)

    def quad(copy_any):
        @pl.loop(0, quads)
        def _(p):
            sort_block(4 * p + 2, sorted_c)
            copy_any(4 * p, sorted_a)
            sort_block(4 * p + 3, sorted_d)
            copy_any(4 * p + 1, sorted_b)
            sort_block(jnp.minimum(4 * p + 4, NBLK - 1), sorted_a)
            copy_any(4 * p + 2, sorted_c)
            sort_block(jnp.minimum(4 * p + 5, NBLK - 1), sorted_b)
            copy_any(4 * p + 3, sorted_d)

    pl.when(short)(lambda: quad(copy_short))
    pl.when(jnp.logical_not(short))(lambda: quad(copy_block))

    low_lanes = iota((HALF, 128), 1) < 64
    r8, l8 = iota((8, 128), 0), iota((8, 128), 1)
    pick = jnp.where((r8 == 0) & (l8 == 64), one, nil)
    pick = jnp.where((r8 == 1) & (l8 == 65), one, pick)
    pick = jnp.where((r8 == 1) & (l8 == 66), 4.0 * one, pick)
    pick = jnp.where((r8 == 2) & (l8 == 67), one, pick)
    pick = jnp.where((r8 == 2) & (l8 == 68), 256.0 * one, pick)
    pick = pick.astype(BF16)
    rank = iota((8, MSG), 1)
    rank_row = iota((8, MSG), 0)
    lane_dest = iota((8, BLK), 1)

    def send(g):
        part = pl.ds(g * GROUP, GROUP)
        return pltpu.make_async_copy(pack_v.at[part], rows_ref.at[part], pack_sem.at[g])

    def pack(g):
        for k in range(GROUP):
            d = GROUP * g + k
            at = pl.multiple_of(d * STRIDE, 8)
            lo = bucket[pl.ds(at, HALF)]
            hi = bucket[pl.ds(pl.multiple_of(at + HALF, 8), HALF)]
            pack_v[d, 0:HALF] = jnp.where(low_lanes, lo, pltpu.roll(hi, 64, 1))
            meta_v[d] = jnp.where(low_lanes, pltpu.roll(lo, 64, 1), hi).astype(BF16)
            both = jnp.concatenate([lo, hi], axis=0).astype(BF16)
            nums = dot_nt(pick, both)
            mine = jnp.max(jnp.where(lane_dest == d, total, nil), axis=1, keepdims=True)
            valid = rank.astype(F32) < mine
            nums = jnp.where((rank_row == 2) & ~valid, float(OWN), nums)
            nums = jnp.where(rank_row == 3, jnp.where(valid, one, nil), nums)
            lanes_ref[d] = nums
            pack_v[d, HALF : HALF + 4] = jnp.concatenate(
                [nums[2:3, 128 * q : 128 * q + 128] for q in range(4)], axis=0
            )

    cells = field_ref[...].reshape(ROWS // 4, 4, 128)
    parts = [split(cells[:, q]) for q in range(4)]
    table[...] = jnp.concatenate([p[0] for p in parts] + [p[1] for p in parts], axis=1)
    m_rows = GROUP * HALF
    ones8 = jnp.ones((8, 256), BF16)
    sub128 = iota((128, 128), 0)
    place = iota((m_rows, 128), 1).astype(F32)

    def far(g):
        meta = meta_v[pl.ds(g * GROUP, GROUP)].reshape(m_rows, 128)
        for h in range(2):
            first = 0 if h == 0 else 64
            col = jnp.where(sub128 == first, one, nil) + jnp.where(sub128 == first + 1, 128.0 * one, nil)
            row = jnp.where(sub128 == first + 2, one, nil)
            got = dot(meta, jnp.concatenate([col, row], axis=1).astype(BF16))
            col, row = got[:, :128], got[:, 128:]
            hot = jnp.concatenate(
                [jnp.where(row == place + 128.0 * q, one, nil).astype(BF16) for q in range(2)], axis=1
            )
            val = dot(hot, table[...])
            got = jnp.zeros((m_rows, 128), F32)
            for q in range(4):
                both = val[:, 128 * q : 128 * q + 128] + val[:, 512 + 128 * q : 640 + 128 * q]
                got = jnp.where(col == place + 128.0 * q, both, got)
            v0, v1 = split(got)
            far_l = dot_nt(ones8, jnp.concatenate([v0, v1], axis=1))
            for i in range(GROUP):
                for q in range(2):
                    at = HALF * i + 128 * q
                    row_at = HALF + 4 + 2 * h + q
                    pack_v[GROUP * g + i, row_at : row_at + 1] = far_l[0:1, at : at + 128]

    pack(0)

    @pl.loop(0, NT // GROUP - 1)
    def _(g):
        far(g)
        pack(g + 1)
        send(g).start()

    far(NT // GROUP - 1)
    send(NT // GROUP - 1).start()
    pick = jnp.where((r8 == 0) & (l8 == 0), one, nil) + jnp.where((r8 == 1) & (l8 == 127), one, nil)
    pick = pick.astype(BF16)
    f0, f1 = split(field_ref[...])
    f2 = (field_ref[...] - f0.astype(F32) - f1.astype(F32)).astype(BF16)
    ends_ref[...] = dot_nt(pick, f0) + dot_nt(pick, f1) + dot_nt(pick, f2)
    for g in range(NT // GROUP):
        send(g).wait()


def route(counts, owners, cells, field, profiles):
    vmem = pl.BlockSpec(memory_space=pltpu.VMEM)
    anywhere = pl.BlockSpec(memory_space=pl.ANY)
    return pl.pallas_call(
        route_kernel,
        out_shape=(
            jax.ShapeDtypeStruct((NT, LOAD, 128), F32),
            jax.ShapeDtypeStruct((NT, 8, MSG), F32),
            jax.ShapeDtypeStruct((8, ROWS), F32),
        ),
        in_specs=[pl.BlockSpec(memory_space=pltpu.SMEM), vmem, vmem, vmem, anywhere],
        out_specs=(anywhere, vmem, vmem),
        scratch_shapes=[pltpu.VMEM((NBLK, BLK), F32)] * 6
        + [pltpu.VMEM((BLK + 16, 128), F32)] * 4
        + [
            pltpu.VMEM((NT * STRIDE, 128), F32),
            pltpu.VMEM((128, 128), I32),
            pltpu.SMEM((128, 128), I32),
            pltpu.SemaphoreType.DMA,
            pltpu.VMEM((PTS, CAP), F32),
            pltpu.SemaphoreType.DMA,
            pltpu.VMEM((NT, LOAD, 128), F32),
            pltpu.SemaphoreType.DMA((NT // GROUP,)),
            pltpu.VMEM((NT, HALF, 128), BF16),
            pltpu.VMEM((ROWS // 4, 1024), BF16),
        ],
        compiler_params=pltpu.CompilerParams(vmem_limit_bytes=ROOM),
        name="route",
    )(counts, owners.reshape(128, 128), cells.reshape(128, 128), field, profiles)


def step_weights(radial_step):
    zero = jnp.zeros((PTS, PTS), F32)
    w = jnp.concatenate(
        [
            jnp.concatenate([radial_step.T, zero], axis=1),
            jnp.concatenate([zero, radial_step.T], axis=1),
        ],
        axis=0,
    )
    high = lax.reduce_precision(w, 8, 7)
    w0, w1 = high.astype(BF16), (w - high).astype(BF16)
    row = jnp.concatenate([w0, w1], axis=1)
    return jnp.concatenate([row, row], axis=0)


def flux_rows(flux_weights):
    zero = jnp.zeros((PTS,), F32)
    f = jnp.stack(
        [jnp.concatenate([flux_weights, zero]), jnp.concatenate([zero, flux_weights])]
        + [jnp.zeros((128,), F32)] * 6
    )
    return f / SUB


def substep(state, add, weights):
    s0, s1 = split(state)
    got = dot(jnp.concatenate([s0, s1], axis=1), weights)
    return (got[:, :128] + got[:, 128:]) + (add + 0.25 * jnp.tanh(state))


HEAT_N = GROUP


def far_columns(side):
    far = jnp.concatenate([side[4 + q : 5 + q] for q in range(4)], axis=1)
    rest = far - far.astype(BF16).astype(F32)
    row8 = iota((8, MSG), 0)
    terms = jnp.where(row8 == 0, far, jnp.where(row8 == 1, rest, 0.0)).astype(BF16)
    pick = jnp.where(iota((8, 128), 0) < 2, 1.0, 0.0).astype(BF16)
    return lax.dot_general(terms, pick, (((0,), (0,)), ((), ())), preferred_element_type=F32)


def heat_kernel(rows_ref, side_ref, fw_ref, weights_ref, flux_ref, heat_ref):
    weights = weights_ref[...]
    state = rows_ref[...].reshape(HEAT_N * HALF, 128)
    low_lanes = iota((HALF, 128), 1) < 64
    adds = []
    for i in range(HEAT_N):
        far = far_columns(side_ref[i])
        adds.append(fw_ref[...] * jnp.where(low_lanes, far[:HALF], far[HALF:]))
    add = jnp.concatenate(adds, axis=0)
    total = jnp.zeros_like(state)
    for _ in range(SUB):
        state = substep(state, add, weights)
        total = total + state
    t0, t1 = split(total)
    f0, f1 = split(flux_ref[...])
    heat = dot_nt(f0, t0) + dot_nt(f0, t1) + dot_nt(f1, t0)
    for i in range(HEAT_N):
        heat_ref[i] = heat[:, HALF * i : HALF * i + HALF]


def home_heat(rows, fw, weights, flux, first, steps):
    return pl.pallas_call(
        heat_kernel,
        grid=(steps,),
        out_shape=jax.ShapeDtypeStruct((steps * HEAT_N, 8, HALF), F32),
        in_specs=[
            pl.BlockSpec((HEAT_N, HALF, 128), lambda d: (d + first, 0, 0)),
            pl.BlockSpec((HEAT_N, 8, 128), lambda d: (d + first, HALF // 8, 0)),
            pl.BlockSpec((1, 128), lambda d: (0, 0)),
            pl.BlockSpec((256, 256), lambda d: (0, 0)),
            pl.BlockSpec((8, 128), lambda d: (0, 0)),
        ],
        out_specs=pl.BlockSpec((HEAT_N, 8, HALF), lambda d: (d, 0, 0)),
        compiler_params=pltpu.CompilerParams(vmem_limit_bytes=ROOM),
        cost_estimate=pl.CostEstimate(
            flops=25 * 10**8 * steps, bytes_accessed=steps << 20, transcendentals=steps << 21
        ),
        name="home_heat",
    )(rows, rows, fw, weights, flux)


DEP_N = GROUP
HEAT_A = 2


def columns(values):
    v0 = values.astype(BF16).astype(F32)
    v1 = (values - v0).astype(BF16).astype(F32)
    row8 = iota((8, values.shape[1]), 0)
    terms = jnp.where(row8 == 0, v0, jnp.where(row8 == 1, v1, jnp.where(row8 == 2, values - v0 - v1, 0.0)))
    pick = jnp.where(iota((8, 128), 0) < 3, 1.0, 0.0).astype(BF16)
    return lax.dot_general(
        terms.astype(BF16), pick, (((0,), (0,)), ((), ())), preferred_element_type=F32
    )


def deposit_kernel(
    lanes_ref, heat_a_ref, heat_b_ref, cells_ref, vel_ref, dif_ref, flux_ref, below_ref, above_ref, left_ref, right_ref,
    out_ref, acc,
):
    d = pl.program_id(0)

    @pl.when(d == 0)
    def _():
        acc[...] = jnp.zeros_like(acc)

    one, nil = jnp.ones((), F32), jnp.zeros((), F32)
    width = DEP_N * MSG
    cols, rows, heats = [], [], []
    for i in range(DEP_N):
        nums = lanes_ref[i]
        both = jnp.where(d < HEAT_A, heat_a_ref[i], heat_b_ref[i])
        heat = jnp.concatenate([both[0:1], both[1:2]], axis=1)
        cols.append(nums[0:1])
        rows.append(nums[1:2])
        heats.append(jnp.where(nums[3:4] > 0.5, 0.5 * heat, nil))
    col = jnp.concatenate(cols, axis=1).astype(I32)
    row = jnp.concatenate(rows, axis=1).astype(I32)
    heat = jnp.concatenate(heats, axis=1)
    high = heat.astype(BF16).astype(F32)
    here = col == iota((128, width), 0)
    spread = jnp.concatenate(
        [jnp.where(here, high, nil).astype(BF16), jnp.where(here, heat - high, nil).astype(BF16)], axis=0
    )
    hot = jnp.where(row == iota((ROWS, width), 0), one, nil).astype(BF16)
    acc[...] += dot_nt(hot, spread)

    @pl.when(d == NT // DEP_N - 1)
    def _():
        layers = ROWS // 64
        wall, lane = iota((64, 128), 0), iota((64, 128), 1)
        left, right = columns(left_ref[...]), columns(right_ref[...])
        for x in range(layers):
            at = 64 * x
            h = cells_ref[at : at + 64]
            x_lower = cells_ref[at - 64 : at] if x else below_ref[...]
            x_upper = cells_ref[at + 64 : at + 128] if x < layers - 1 else above_ref[...]
            w_lower = jnp.where(wall == 0, h, pltpu.roll(h, 1, 0))
            w_upper = jnp.where(wall == 63, h, pltpu.roll(h, 63, 0))
            s_lower = jnp.where(lane == 0, left[at : at + 64], pltpu.roll(h, 1, 1))
            s_upper = jnp.where(lane == 127, right[at : at + 64], pltpu.roll(h, 127, 1))
            laplace = (x_lower + x_upper) + (w_lower + w_upper) + (s_lower + s_upper) - 6.0 * h
            new = h + dif_ref[at : at + 64] * laplace - vel_ref[at : at + 64] * (h - x_lower)
            new = new + jnp.where(wall == 0, flux_ref[x : x + 1], nil)
            out_ref[at : at + 64] = new + (acc[at : at + 64, :128] + acc[at : at + 64, 128:])


def deposit(lanes, heat_a, heat_b, cells, velocity, diffusivity, wall_flux, edges):
    def whole(shape):
        return pl.BlockSpec(shape, lambda d: (0, 0))

    field = whole((ROWS, 128))
    return pl.pallas_call(
        deposit_kernel,
        grid=(NT // DEP_N,),
        out_shape=jax.ShapeDtypeStruct((ROWS, 128), F32),
        in_specs=[
            pl.BlockSpec((DEP_N, 8, MSG), lambda d: (d, 0, 0)),
            pl.BlockSpec((DEP_N, 8, HALF), lambda d: (jnp.minimum(d, HEAT_A - 1), 0, 0)),
            pl.BlockSpec((DEP_N, 8, HALF), lambda d: (jnp.maximum(d - HEAT_A, 0), 0, 0)),
            field,
            field,
            field,
            whole((ROWS // 64, 128)),
            whole((64, 128)),
            whole((64, 128)),
            whole((1, ROWS)),
            whole((1, ROWS)),
        ],
        out_specs=field,
        scratch_shapes=[pltpu.VMEM((ROWS, 256), F32)],
        compiler_params=pltpu.CompilerParams(vmem_limit_bytes=40 * 2**20),
        cost_estimate=pl.CostEstimate(flops=10**10, bytes_accessed=4 << 20, transcendentals=0),
        name="deposit",
    )(lanes, heat_a, heat_b, cells, velocity, diffusivity, wall_flux, *edges)


SETTLE = 1024


def settle_kernel(
    rows_ref, fw_ref, weights_ref, out_ref,
    stage, comb, got, got_sem, side, side_sem, slot_v, slot_s, slot_sem, amount_v, amount_s, amount_sem,
):
    fetch_side = pltpu.make_async_copy(rows_ref.at[:, pl.ds(HALF, 8)], side, side_sem)
    fetch_side.start()

    def fetch(g):
        part = pl.ds(g * GROUP, GROUP)
        return pltpu.make_async_copy(rows_ref.at[part, pl.ds(0, HALF)], got.at[part], got_sem.at[g])

    for g in range(NT // GROUP):
        fetch(g).start()
    fetch_side.wait()
    for t in range(NT):
        slot_v[4 * t : 4 * t + 4] = side[t, 0:4].astype(I32)
    valid = jnp.where(slot_v[...] < OWN, 1.0, 0.0).astype(BF16)
    by_row = dot(valid, jnp.ones((128, 128), BF16)).astype(BF16)
    of_sender = jnp.where(iota((NT, 128), 1) >> 2 == iota((NT, 128), 0), 1.0, 0.0).astype(BF16)
    amount_v[...] = dot(of_sender, by_row).astype(I32)
    copies = (
        pltpu.make_async_copy(slot_v, slot_s, slot_sem),
        pltpu.make_async_copy(amount_v, amount_s, amount_sem),
    )
    for copy in copies:
        copy.start()

    low_lanes = iota((HALF, 128), 1) < 64

    @pl.loop(0, NT // GROUP)
    def _(g):
        fetch(g).wait()
        for k in range(GROUP):
            t = GROUP * g + k
            rows = got[t]
            col = far_columns(side[t])
            at = pl.multiple_of(t * MSG, MSG)
            comb[pl.ds(at, HALF)] = jnp.where(low_lanes, rows, col[:HALF])
            comb[pl.ds(pl.multiple_of(at + HALF, HALF), HALF)] = jnp.where(
                low_lanes, pltpu.roll(rows, 64, 1), col[HALF:]
            )

    for copy in copies:
        copy.wait()

    @pl.loop(0, NT)
    def _(t):
        @pl.loop(0, (amount_s[t, 0] + 31) >> 5)
        def _(k):
            at = pl.multiple_of(t * MSG + 32 * k, 32)
            row, lane = t * 4 + (k >> 2), (k & 3) * 32
            for i in range(32):
                stage[pl.ds(slot_s[row, lane + i], 1)] = comb[pl.ds(at + i, 1)]

    weights = weights_ref[...]
    fw = fw_ref[...]
    low_lanes = iota((SETTLE, 128), 1) < 64
    for c in range(OWN2 // SETTLE):
        at = c * SETTLE
        a = stage[at : at + SETTLE]
        b = stage[at + OWN2 : at + OWN2 + SETTLE]
        state = jnp.where(low_lanes, a, pltpu.roll(b, 64, 1))
        add = fw * jnp.where(low_lanes, pltpu.roll(a, 64, 1), b)
        for _ in range(SUB):
            state = substep(state, add, weights)
        for k in range(SETTLE // 128):
            turned = state[128 * k : 128 * k + 128].T
            out_ref[:, at + 128 * k : at + 128 * k + 128] = turned[:64]
            out_ref[:, at + OWN2 + 128 * k : at + OWN2 + 128 * k + 128] = turned[64:]


def settle(rows, fw, weights):
    vmem = pl.BlockSpec(memory_space=pltpu.VMEM)
    return pl.pallas_call(
        settle_kernel,
        out_shape=jax.ShapeDtypeStruct((PTS, OWN), F32),
        in_specs=[pl.BlockSpec(memory_space=pl.ANY), vmem, vmem],
        out_specs=vmem,
        scratch_shapes=[
            pltpu.VMEM((OWN + 8, 128), F32),
            pltpu.VMEM((NT * MSG, 128), F32),
            pltpu.VMEM((NT, HALF, 128), F32),
            pltpu.SemaphoreType.DMA((NT // GROUP,)),
            pltpu.VMEM((NT, 8, 128), F32),
            pltpu.SemaphoreType.DMA,
            pltpu.VMEM((128, 128), I32),
            pltpu.SMEM((128, 128), I32),
            pltpu.SemaphoreType.DMA,
            pltpu.VMEM((NT, 128), I32),
            pltpu.SMEM((NT, 128), I32),
            pltpu.SemaphoreType.DMA,
        ],
        compiler_params=pltpu.CompilerParams(vmem_limit_bytes=ROOM),
        name="settle",
    )(rows, fw, weights)


def edges_of(cells, ends):
    n_x, n_s = lax.axis_size("stream"), lax.axis_size("tile")
    up_x = [(i, i + 1) for i in range(n_x - 1)]
    down_x = [(i + 1, i) for i in range(n_x - 1)]
    up_s = [(i, (i + 1) % n_s) for i in range(n_s)]
    down_s = [((i + 1) % n_s, i) for i in range(n_s)]
    below = lax.ppermute(cells[-1], "stream", up_x)
    above = lax.ppermute(cells[0], "stream", down_x)
    left = lax.ppermute(ends[1:2], "tile", up_s)
    right = lax.ppermute(ends[0:1], "tile", down_s)
    return below, above, left, right


def on_device(
    enthalpy, velocity, diffusivity, wall_flux, profiles, counts, owners, cells,
    radial_step, far_weights, flux_weights,
):
    table = enthalpy.reshape(ROWS, 128)
    rows, lanes, ends = route(counts, owners, cells, table, profiles)
    rows, radial_step, far_weights, flux_weights = lax.optimization_barrier(
        (rows, radial_step, far_weights, flux_weights)
    )
    weights = step_weights(radial_step)
    fw = jnp.concatenate([far_weights, far_weights])[None, :]
    flux = flux_rows(flux_weights)
    got = lax.all_to_all(rows, "tile", split_axis=0, concat_axis=0, tiled=True)
    heat_a = home_heat(rows, fw, weights, flux, 0, HEAT_A)
    layers, ends, heat_a = lax.optimization_barrier((enthalpy, ends, heat_a))
    heat_b = home_heat(rows, fw, weights, flux, HEAT_A, NT // HEAT_N - HEAT_A)
    new_enthalpy = deposit(
        lanes, heat_a, heat_b, table, velocity.reshape(ROWS, 128), diffusivity.reshape(ROWS, 128),
        wall_flux, edges_of(layers, ends),
    ).reshape(enthalpy.shape)
    new_profiles = settle(got, fw, weights)
    return new_enthalpy, new_profiles


def solution(mesh):
    return jax.shard_map(
        on_device,
        mesh=mesh,
        in_specs=(
            P("stream", None, "tile"),
            P("stream", None, "tile"),
            P("stream", None, "tile"),
            P("stream", "tile"),
            P(None, ("stream", "tile")),
            P(("stream", "tile")),
            P(("stream", "tile")),
            P(("stream", "tile")),
            P(),
            P(),
            P(),
        ),
        out_specs=(P("stream", None, "tile"), P(None, ("stream", "tile"))),
        check_vma=False,
    )
```

```python
import jax
import jax.numpy as jnp
from jax import lax
from jax.experimental import pallas as pl
from jax.experimental.pallas import tpu as pltpu
from jax.sharding import PartitionSpec as P

SUB = 16
PTS = 64
NT = 32
CAP = 16384
OWN = 6144
MSG = 512
HALF = MSG // 2
LOAD = HALF + 8
BLK = 256
NBLK = CAP // BLK
STRIDE = MSG + 16
ROWS = 1024
OWN2 = OWN // 2

GROUP = 4
ROOM = 60 * 2**20

F32, BF16, I32 = jnp.float32, jnp.bfloat16, jnp.int32
NTD = (((1,), (1,)), ((), ()))


def iota(shape, dim):
    return lax.broadcasted_iota(I32, shape, dim)


def split(x):
    high = x.astype(BF16)
    return high, (x - high.astype(F32)).astype(BF16)


def dot(a, b):
    return jnp.dot(a, b, preferred_element_type=F32)


def dot_nt(a, b):
    return lax.dot_general(a, b, NTD, preferred_element_type=F32)


def route_kernel(
    count_ref, owners_ref, cells_ref, field_ref, prof_ref,
    rows_ref, lanes_ref, ends_ref,
    pos_s, m0_s, m1_s, m2_s, m3_s, m4_s, sorted_a, sorted_b, sorted_c, sorted_d,
    bucket, tab_v, tab_s, sem, prof_v, prof_sem, pack_v, pack_sem, meta_v, table,
):
    count = count_ref[0]
    fetch = pltpu.make_async_copy(prof_ref, prof_v, prof_sem)
    fetch.start()

    def blocks(ref):
        x = ref[...].reshape(NBLK, 2, 128)
        return jnp.concatenate([x[:, 0], x[:, 1]], axis=1)

    slot = iota((NBLK, BLK), 0) * BLK + iota((NBLK, BLK), 1)
    owners = blocks(owners_ref)
    dest = jnp.floor((owners.astype(F32) + 0.5) * (1.0 / OWN)).astype(I32)
    within = owners - dest * OWN
    live = slot < count
    dest = jnp.where(live, dest, NT)
    cells = blocks(cells_ref)
    m0_s[...] = (cells & 127).astype(F32)
    m1_s[...] = ((cells >> 7) & 3).astype(F32)
    m2_s[...] = (cells >> 9).astype(F32)
    m3_s[...] = (within & 255).astype(F32)
    m4_s[...] = (within >> 8).astype(F32)

    sub, lane = iota((BLK, BLK), 0), iota((BLK, BLK), 1)
    one, nil = jnp.ones((), F32), jnp.zeros((), F32)
    before = jnp.where(sub < lane, one, nil).astype(BF16)
    same_block = (sub >> 5) == (lane >> 5)
    same_dest = (sub & 31) == (lane & 31)
    seg_left = jnp.where(same_block & (lane < sub), one, nil).astype(BF16)
    seg_right = jnp.where(same_block & (sub < lane), one, nil).astype(BF16)
    base_right = jnp.where(same_dest & ((sub >> 5) < (lane >> 5)), one, nil).astype(BF16)
    all_right = jnp.where(same_dest, one, nil).astype(BF16)
    ones_a = jnp.ones((8, BLK), BF16)
    ones_b = jnp.ones((BLK, 128), BF16)
    run = jnp.zeros((8, BLK), F32)
    longest = jnp.zeros((8, BLK), F32)
    for c in range(8):
        part = dest[8 * c : 8 * c + 8]
        hot = jnp.where(part[:, None, :] == iota((8, NT, BLK), 1), one, nil).reshape(BLK, BLK)
        hot_b = hot.astype(BF16)
        prefix = dot(hot_b, before)
        amount = dot(hot_b, ones_b)
        seg = dot(seg_left, amount.astype(BF16))
        seg2 = jnp.concatenate([seg, seg], axis=1)
        pos = jnp.sum((hot * (prefix + seg2)).reshape(8, NT, BLK), axis=1)
        pos_s[8 * c : 8 * c + 8] = jnp.where(live[8 * c : 8 * c + 8], pos, 511.0)
        amount_l = dot_nt(ones_a, hot_b)
        amount_lb = amount_l.astype(BF16)
        src = dot(amount_lb, seg_right)
        base = dot(amount_lb, base_right) + run
        run = run + dot(amount_lb, all_right)
        longest = jnp.maximum(longest, amount_l)
        most = amount_l
        for shift in (1, 2, 4, 8, 16):
            most = jnp.maximum(most, pltpu.roll(most, BLK - shift, 1))
        first = iota((8, BLK), 1) & 31
        row8 = iota((8, BLK), 0)
        packed = jnp.where(row8 == 0, src, nil)
        packed = jnp.where(row8 == 1, base + (first * STRIDE).astype(F32), packed)
        packed = jnp.where(row8 == 2, amount_l, packed)
        packed = jnp.where(row8 == 3, most, packed)
        packed = packed.astype(I32)
        tab_v[16 * c : 16 * c + 8] = packed[:, :128]
        tab_v[16 * c + 8 : 16 * c + 16] = packed[:, 128:]
    copy = pltpu.make_async_copy(tab_v, tab_s, sem)
    copy.start()
    short = jnp.max(longest) <= 8.0
    total = run

    zero8 = jnp.zeros((STRIDE, 128), F32)

    @pl.loop(0, NT)
    def _(d):
        bucket[pl.ds(pl.multiple_of(d * STRIDE, 8), STRIDE)] = zero8

    copy.wait()
    fetch.wait()

    meta_rest = jnp.zeros((56, BLK), BF16)
    low_rest = jnp.zeros((64, BLK), BF16)
    row8 = iota((8, BLK), 0)

    def sort_block(j, out):
        x = prof_v[:, pl.ds(pl.multiple_of(j * BLK, BLK), BLK)]
        high, low = split(x)
        meta = jnp.zeros((8, BLK), F32)
        for k, ref in enumerate((m0_s, m1_s, m2_s, m3_s, m4_s)):
            meta = jnp.where(row8 == k, ref[pl.ds(j, 1), :], meta)
        data = jnp.concatenate([high, meta.astype(BF16), meta_rest, low, low_rest], axis=0)
        place = pos_s[pl.ds(j, 1), :].astype(I32)
        perm = jnp.where(place == sub, one, nil).astype(BF16)
        got = dot_nt(perm, data)
        out[0:BLK] = got[:, :128] + got[:, 128:]

    def copy_block(p, c, inp):
        chunk, at = p * 8, c * NT
        most = tab_s[chunk + 3, at]

        @pl.when(most <= 8)
        def _():
            for d in range(NT):
                src = tab_s[chunk, at + d]
                dst = tab_s[chunk + 1, at + d]
                bucket[pl.ds(dst, 8)] = inp[pl.ds(src, 8)]

        @pl.when((most > 8) & (most <= 16))
        def _():
            for d in range(NT):
                src = tab_s[chunk, at + d]
                dst = tab_s[chunk + 1, at + d]
                bucket[pl.ds(dst, 16)] = inp[pl.ds(src, 16)]

        @pl.when(most > 16)
        def _():
            @pl.loop(0, NT)
            def _(d):
                src = tab_s[chunk, at + d]
                dst = tab_s[chunk + 1, at + d]

                @pl.loop(0, (tab_s[chunk + 2, at + d] + 7) >> 3)
                def _(k):
                    bucket[pl.ds(dst + 8 * k, 8)] = inp[pl.ds(src + 8 * k, 8)]

    def copy_short(p, c, inp):
        chunk, at = p * 8, c * NT
        for d in range(NT):
            src = tab_s[chunk, at + d]
            dst = tab_s[chunk + 1, at + d]
            bucket[pl.ds(dst, 8)] = inp[pl.ds(src, 8)]

    for ref in (sorted_a, sorted_b, sorted_c, sorted_d):
        ref[BLK:] = jnp.zeros((16, 128), F32)
    quads = (count + 4 * BLK - 1) // (4 * BLK)
    sort_block(0, sorted_a)
    sort_block(1, sorted_b)

    def quad(copy_any):
        @pl.loop(0, quads)
        def _(p):
            sort_block(4 * p + 2, sorted_c)
            copy_any(p, 0, sorted_a)
            sort_block(4 * p + 3, sorted_d)
            copy_any(p, 1, sorted_b)
            sort_block(jnp.minimum(4 * p + 4, NBLK - 1), sorted_a)
            copy_any(p, 2, sorted_c)
            sort_block(jnp.minimum(4 * p + 5, NBLK - 1), sorted_b)
            copy_any(p, 3, sorted_d)

    pl.when(short)(lambda: quad(copy_short))
    pl.when(jnp.logical_not(short))(lambda: quad(copy_block))

    low_lanes = iota((HALF, 128), 1) < 64
    r8, l8 = iota((8, 128), 0), iota((8, 128), 1)
    pick = jnp.where((r8 == 0) & (l8 == 64), one, nil)
    pick = jnp.where((r8 == 1) & (l8 == 65), one, pick)
    pick = jnp.where((r8 == 1) & (l8 == 66), 4.0 * one, pick)
    pick = jnp.where((r8 == 2) & (l8 == 67), one, pick)
    pick = jnp.where((r8 == 2) & (l8 == 68), 256.0 * one, pick)
    pick = pick.astype(BF16)
    rank = iota((8, MSG), 1)
    rank_row = iota((8, MSG), 0)
    lane_dest = iota((8, BLK), 1)

    def send(g):
        part = pl.ds(g * GROUP, GROUP)
        return pltpu.make_async_copy(pack_v.at[part], rows_ref.at[part], pack_sem.at[g])

    def pack(g):
        for k in range(GROUP):
            d = GROUP * g + k
            at = pl.multiple_of(d * STRIDE, 8)
            lo = bucket[pl.ds(at, HALF)]
            hi = bucket[pl.ds(pl.multiple_of(at + HALF, 8), HALF)]
            pack_v[d, 0:HALF] = jnp.where(low_lanes, lo, pltpu.roll(hi, 64, 1))
            meta_v[d] = jnp.where(low_lanes, pltpu.roll(lo, 64, 1), hi).astype(BF16)
            both = jnp.concatenate([lo, hi], axis=0).astype(BF16)
            nums = dot_nt(pick, both)
            mine = jnp.max(jnp.where(lane_dest == d, total, nil), axis=1, keepdims=True)
            valid = rank.astype(F32) < mine
            nums = jnp.where((rank_row == 2) & ~valid, float(OWN), nums)
            nums = jnp.where(rank_row == 3, jnp.where(valid, one, nil), nums)
            lanes_ref[d] = nums
            pack_v[d, HALF : HALF + 4] = jnp.concatenate(
                [nums[2:3, 128 * q : 128 * q + 128] for q in range(4)], axis=0
            )

    cells = field_ref[...].reshape(ROWS // 4, 4, 128)
    parts = [split(cells[:, q]) for q in range(4)]
    table[...] = jnp.concatenate([p[0] for p in parts] + [p[1] for p in parts], axis=1)
    m_rows = GROUP * HALF
    ones8 = jnp.ones((8, 256), BF16)
    sub128 = iota((128, 128), 0)
    place = iota((m_rows, 128), 1).astype(F32)

    def far(g):
        meta = meta_v[pl.ds(g * GROUP, GROUP)].reshape(m_rows, 128)
        for h in range(2):
            first = 0 if h == 0 else 64
            col = jnp.where(sub128 == first, one, nil) + jnp.where(sub128 == first + 1, 128.0 * one, nil)
            row = jnp.where(sub128 == first + 2, one, nil)
            got = dot(meta, jnp.concatenate([col, row], axis=1).astype(BF16))
            col, row = got[:, :128], got[:, 128:]
            hot = jnp.concatenate(
                [jnp.where(row == place + 128.0 * q, one, nil).astype(BF16) for q in range(2)], axis=1
            )
            val = dot(hot, table[...])
            got = jnp.zeros((m_rows, 128), F32)
            for q in range(4):
                both = val[:, 128 * q : 128 * q + 128] + val[:, 512 + 128 * q : 640 + 128 * q]
                got = jnp.where(col == place + 128.0 * q, both, got)
            v0, v1 = split(got)
            far_l = dot_nt(ones8, jnp.concatenate([v0, v1], axis=1))
            for i in range(GROUP):
                for q in range(2):
                    at = HALF * i + 128 * q
                    row_at = HALF + 4 + 2 * h + q
                    pack_v[GROUP * g + i, row_at : row_at + 1] = far_l[0:1, at : at + 128]

    pack(0)

    @pl.loop(0, NT // GROUP - 1)
    def _(g):
        far(g)
        pack(g + 1)
        send(g).start()

    far(NT // GROUP - 1)
    send(NT // GROUP - 1).start()
    pick = jnp.where((r8 == 0) & (l8 == 0), one, nil) + jnp.where((r8 == 1) & (l8 == 127), one, nil)
    pick = pick.astype(BF16)
    f0, f1 = split(field_ref[...])
    f2 = (field_ref[...] - f0.astype(F32) - f1.astype(F32)).astype(BF16)
    ends_ref[...] = dot_nt(pick, f0) + dot_nt(pick, f1) + dot_nt(pick, f2)
    for g in range(NT // GROUP):
        send(g).wait()


def route(counts, owners, cells, field, profiles):
    vmem = pl.BlockSpec(memory_space=pltpu.VMEM)
    anywhere = pl.BlockSpec(memory_space=pl.ANY)
    return pl.pallas_call(
        route_kernel,
        out_shape=(
            jax.ShapeDtypeStruct((NT, LOAD, 128), F32),
            jax.ShapeDtypeStruct((NT, 8, MSG), F32),
            jax.ShapeDtypeStruct((8, ROWS), F32),
        ),
        in_specs=[pl.BlockSpec(memory_space=pltpu.SMEM), vmem, vmem, vmem, anywhere],
        out_specs=(anywhere, vmem, vmem),
        scratch_shapes=[pltpu.VMEM((NBLK, BLK), F32)] * 6
        + [pltpu.VMEM((BLK + 16, 128), F32)] * 4
        + [
            pltpu.VMEM((NT * STRIDE, 128), F32),
            pltpu.VMEM((128, 128), I32),
            pltpu.SMEM((128, 128), I32),
            pltpu.SemaphoreType.DMA,
            pltpu.VMEM((PTS, CAP), F32),
            pltpu.SemaphoreType.DMA,
            pltpu.VMEM((NT, LOAD, 128), F32),
            pltpu.SemaphoreType.DMA((NT // GROUP,)),
            pltpu.VMEM((NT, HALF, 128), BF16),
            pltpu.VMEM((ROWS // 4, 1024), BF16),
        ],
        compiler_params=pltpu.CompilerParams(vmem_limit_bytes=ROOM),
        name="route",
    )(counts, owners.reshape(128, 128), cells.reshape(128, 128), field, profiles)


def step_weights(radial_step):
    zero = jnp.zeros((PTS, PTS), F32)
    w = jnp.concatenate(
        [
            jnp.concatenate([radial_step.T, zero], axis=1),
            jnp.concatenate([zero, radial_step.T], axis=1),
        ],
        axis=0,
    )
    high = lax.reduce_precision(w, 8, 7)
    w0, w1 = high.astype(BF16), (w - high).astype(BF16)
    row = jnp.concatenate([w0, w1], axis=1)
    return jnp.concatenate([row, row], axis=0)


def flux_rows(flux_weights):
    zero = jnp.zeros((PTS,), F32)
    f = jnp.stack(
        [jnp.concatenate([flux_weights, zero]), jnp.concatenate([zero, flux_weights])]
        + [jnp.zeros((128,), F32)] * 6
    )
    return f / SUB


def substep(state, add, weights):
    s0, s1 = split(state)
    got = dot(jnp.concatenate([s0, s1], axis=1), weights)
    return (got[:, :128] + got[:, 128:]) + (add + 0.25 * jnp.tanh(state))


HEAT_N = GROUP


def far_columns(side):
    far = jnp.concatenate([side[4 + q : 5 + q] for q in range(4)], axis=1)
    rest = far - far.astype(BF16).astype(F32)
    row8 = iota((8, MSG), 0)
    terms = jnp.where(row8 == 0, far, jnp.where(row8 == 1, rest, 0.0)).astype(BF16)
    pick = jnp.where(iota((8, 128), 0) < 2, 1.0, 0.0).astype(BF16)
    return lax.dot_general(terms, pick, (((0,), (0,)), ((), ())), preferred_element_type=F32)


def heat_kernel(rows_ref, side_ref, fw_ref, weights_ref, flux_ref, heat_ref):
    weights = weights_ref[...]
    state = rows_ref[...].reshape(HEAT_N * HALF, 128)
    low_lanes = iota((HALF, 128), 1) < 64
    adds = []
    for i in range(HEAT_N):
        far = far_columns(side_ref[i])
        adds.append(fw_ref[...] * jnp.where(low_lanes, far[:HALF], far[HALF:]))
    add = jnp.concatenate(adds, axis=0)
    total = jnp.zeros_like(state)
    for _ in range(SUB):
        state = substep(state, add, weights)
        total = total + state
    t0, t1 = split(total)
    f0, f1 = split(flux_ref[...])
    heat = dot_nt(f0, t0) + dot_nt(f0, t1) + dot_nt(f1, t0)
    for i in range(HEAT_N):
        heat_ref[i] = heat[:, HALF * i : HALF * i + HALF]


def home_heat(rows, fw, weights, flux):
    steps = NT // HEAT_N
    return pl.pallas_call(
        heat_kernel,
        grid=(steps,),
        out_shape=jax.ShapeDtypeStruct((steps * HEAT_N, 8, HALF), F32),
        in_specs=[
            pl.BlockSpec((HEAT_N, HALF, 128), lambda d: (d, 0, 0)),
            pl.BlockSpec((HEAT_N, 8, 128), lambda d: (d, HALF // 8, 0)),
            pl.BlockSpec((1, 128), lambda d: (0, 0)),
            pl.BlockSpec((256, 256), lambda d: (0, 0)),
            pl.BlockSpec((8, 128), lambda d: (0, 0)),
        ],
        out_specs=pl.BlockSpec((HEAT_N, 8, HALF), lambda d: (d, 0, 0)),
        compiler_params=pltpu.CompilerParams(vmem_limit_bytes=ROOM),
        cost_estimate=pl.CostEstimate(
            flops=25 * 10**8 * steps, bytes_accessed=steps << 20, transcendentals=steps << 21
        ),
        name="home_heat",
    )(rows, rows, fw, weights, flux)


DEP_N = GROUP


def columns(values):
    v0 = values.astype(BF16).astype(F32)
    v1 = (values - v0).astype(BF16).astype(F32)
    row8 = iota((8, values.shape[1]), 0)
    terms = jnp.where(row8 == 0, v0, jnp.where(row8 == 1, v1, jnp.where(row8 == 2, values - v0 - v1, 0.0)))
    pick = jnp.where(iota((8, 128), 0) < 3, 1.0, 0.0).astype(BF16)
    return lax.dot_general(
        terms.astype(BF16), pick, (((0,), (0,)), ((), ())), preferred_element_type=F32
    )


def deposit_kernel(
    lanes_ref, heat_ref, cells_ref, vel_ref, dif_ref, flux_ref, below_ref, above_ref, left_ref, right_ref,
    out_ref, acc,
):
    d = pl.program_id(0)

    @pl.when(d == 0)
    def _():
        acc[...] = jnp.zeros_like(acc)

    one, nil = jnp.ones((), F32), jnp.zeros((), F32)
    width = DEP_N * MSG
    cols, rows, heats = [], [], []
    for i in range(DEP_N):
        nums = lanes_ref[i]
        heat = jnp.concatenate([heat_ref[i, 0:1], heat_ref[i, 1:2]], axis=1)
        cols.append(nums[0:1])
        rows.append(nums[1:2])
        heats.append(jnp.where(nums[3:4] > 0.5, 0.5 * heat, nil))
    col = jnp.concatenate(cols, axis=1).astype(I32)
    row = jnp.concatenate(rows, axis=1).astype(I32)
    heat = jnp.concatenate(heats, axis=1)
    high = heat.astype(BF16).astype(F32)
    here = col == iota((128, width), 0)
    spread = jnp.concatenate(
        [jnp.where(here, high, nil).astype(BF16), jnp.where(here, heat - high, nil).astype(BF16)], axis=0
    )
    hot = jnp.where(row == iota((ROWS, width), 0), one, nil).astype(BF16)
    acc[...] += dot_nt(hot, spread)

    @pl.when(d == NT // DEP_N - 1)
    def _():
        layers = ROWS // 64
        wall, lane = iota((64, 128), 0), iota((64, 128), 1)
        left, right = columns(left_ref[...]), columns(right_ref[...])
        for x in range(layers):
            at = 64 * x
            h = cells_ref[at : at + 64]
            x_lower = cells_ref[at - 64 : at] if x else below_ref[...]
            x_upper = cells_ref[at + 64 : at + 128] if x < layers - 1 else above_ref[...]
            w_lower = jnp.where(wall == 0, h, pltpu.roll(h, 1, 0))
            w_upper = jnp.where(wall == 63, h, pltpu.roll(h, 63, 0))
            s_lower = jnp.where(lane == 0, left[at : at + 64], pltpu.roll(h, 1, 1))
            s_upper = jnp.where(lane == 127, right[at : at + 64], pltpu.roll(h, 127, 1))
            laplace = (x_lower + x_upper) + (w_lower + w_upper) + (s_lower + s_upper) - 6.0 * h
            new = h + dif_ref[at : at + 64] * laplace - vel_ref[at : at + 64] * (h - x_lower)
            new = new + jnp.where(wall == 0, flux_ref[x : x + 1], nil)
            out_ref[at : at + 64] = new + (acc[at : at + 64, :128] + acc[at : at + 64, 128:])


def deposit(lanes, heat, cells, velocity, diffusivity, wall_flux, edges):
    def whole(shape):
        return pl.BlockSpec(shape, lambda d: (0, 0))

    field = whole((ROWS, 128))
    return pl.pallas_call(
        deposit_kernel,
        grid=(NT // DEP_N,),
        out_shape=jax.ShapeDtypeStruct((ROWS, 128), F32),
        in_specs=[
            pl.BlockSpec((DEP_N, 8, MSG), lambda d: (d, 0, 0)),
            pl.BlockSpec((DEP_N, 8, HALF), lambda d: (d, 0, 0)),
            field,
            field,
            field,
            whole((ROWS // 64, 128)),
            whole((64, 128)),
            whole((64, 128)),
            whole((1, ROWS)),
            whole((1, ROWS)),
        ],
        out_specs=field,
        scratch_shapes=[pltpu.VMEM((ROWS, 256), F32)],
        compiler_params=pltpu.CompilerParams(vmem_limit_bytes=40 * 2**20),
        cost_estimate=pl.CostEstimate(flops=10**10, bytes_accessed=4 << 20, transcendentals=0),
        name="deposit",
    )(lanes, heat, cells, velocity, diffusivity, wall_flux, *edges)


SETTLE = 1024


def settle_kernel(
    rows_ref, fw_ref, weights_ref, out_ref,
    stage, comb, got, got_sem, side, side_sem, slot_v, slot_s, slot_sem, amount_v, amount_s, amount_sem,
):
    fetch_side = pltpu.make_async_copy(rows_ref.at[:, pl.ds(HALF, 8)], side, side_sem)
    fetch_side.start()

    def fetch(g):
        part = pl.ds(g * GROUP, GROUP)
        return pltpu.make_async_copy(rows_ref.at[part, pl.ds(0, HALF)], got.at[part], got_sem.at[g])

    for g in range(NT // GROUP):
        fetch(g).start()
    fetch_side.wait()
    for t in range(NT):
        slot_v[4 * t : 4 * t + 4] = side[t, 0:4].astype(I32)
    valid = jnp.where(slot_v[...] < OWN, 1.0, 0.0).astype(BF16)
    by_row = dot(valid, jnp.ones((128, 128), BF16)).astype(BF16)
    of_sender = jnp.where(iota((NT, 128), 1) >> 2 == iota((NT, 128), 0), 1.0, 0.0).astype(BF16)
    amount_v[...] = dot(of_sender, by_row).astype(I32)
    copies = (
        pltpu.make_async_copy(slot_v, slot_s, slot_sem),
        pltpu.make_async_copy(amount_v, amount_s, amount_sem),
    )
    for copy in copies:
        copy.start()

    low_lanes = iota((HALF, 128), 1) < 64

    @pl.loop(0, NT // GROUP)
    def _(g):
        fetch(g).wait()
        for k in range(GROUP):
            t = GROUP * g + k
            rows = got[t]
            col = far_columns(side[t])
            at = pl.multiple_of(t * MSG, MSG)
            comb[pl.ds(at, HALF)] = jnp.where(low_lanes, rows, col[:HALF])
            comb[pl.ds(pl.multiple_of(at + HALF, HALF), HALF)] = jnp.where(
                low_lanes, pltpu.roll(rows, 64, 1), col[HALF:]
            )

    for copy in copies:
        copy.wait()

    @pl.loop(0, NT)
    def _(t):
        amount = amount_s[t, 0]
        for first in range(0, MSG, 32):
            row, lane = 4 * t + first // 128, first % 128

            @pl.when(amount > first)
            def _():
                at = pl.multiple_of(t * MSG + first, 32)
                for i in range(32):
                    stage[pl.ds(slot_s[row, lane + i], 1)] = comb[pl.ds(at + i, 1)]

    weights = weights_ref[...]
    fw = fw_ref[...]
    low_lanes = iota((SETTLE, 128), 1) < 64
    for c in range(OWN2 // SETTLE):
        at = c * SETTLE
        a = stage[at : at + SETTLE]
        b = stage[at + OWN2 : at + OWN2 + SETTLE]
        state = jnp.where(low_lanes, a, pltpu.roll(b, 64, 1))
        add = fw * jnp.where(low_lanes, pltpu.roll(a, 64, 1), b)
        for _ in range(SUB):
            state = substep(state, add, weights)
        for k in range(SETTLE // 128):
            turned = state[128 * k : 128 * k + 128].T
            out_ref[:, at + 128 * k : at + 128 * k + 128] = turned[:64]
            out_ref[:, at + OWN2 + 128 * k : at + OWN2 + 128 * k + 128] = turned[64:]


def settle(rows, fw, weights):
    vmem = pl.BlockSpec(memory_space=pltpu.VMEM)
    return pl.pallas_call(
        settle_kernel,
        out_shape=jax.ShapeDtypeStruct((PTS, OWN), F32),
        in_specs=[pl.BlockSpec(memory_space=pl.ANY), vmem, vmem],
        out_specs=vmem,
        scratch_shapes=[
            pltpu.VMEM((OWN + 8, 128), F32),
            pltpu.VMEM((NT * MSG, 128), F32),
            pltpu.VMEM((NT, HALF, 128), F32),
            pltpu.SemaphoreType.DMA((NT // GROUP,)),
            pltpu.VMEM((NT, 8, 128), F32),
            pltpu.SemaphoreType.DMA,
            pltpu.VMEM((128, 128), I32),
            pltpu.SMEM((128, 128), I32),
            pltpu.SemaphoreType.DMA,
            pltpu.VMEM((NT, 128), I32),
            pltpu.SMEM((NT, 128), I32),
            pltpu.SemaphoreType.DMA,
        ],
        compiler_params=pltpu.CompilerParams(vmem_limit_bytes=ROOM),
        name="settle",
    )(rows, fw, weights)


def edges_of(cells, ends):
    n_x, n_s = lax.axis_size("stream"), lax.axis_size("tile")
    up_x = [(i, i + 1) for i in range(n_x - 1)]
    down_x = [(i + 1, i) for i in range(n_x - 1)]
    up_s = [(i, (i + 1) % n_s) for i in range(n_s)]
    down_s = [((i + 1) % n_s, i) for i in range(n_s)]
    below = lax.ppermute(cells[-1], "stream", up_x)
    above = lax.ppermute(cells[0], "stream", down_x)
    left = lax.ppermute(ends[1:2], "tile", up_s)
    right = lax.ppermute(ends[0:1], "tile", down_s)
    return below, above, left, right


def on_device(
    enthalpy, velocity, diffusivity, wall_flux, profiles, counts, owners, cells,
    radial_step, far_weights, flux_weights,
):
    table = enthalpy.reshape(ROWS, 128)
    rows, lanes, ends = route(counts, owners, cells, table, profiles)
    rows, radial_step, far_weights, flux_weights = lax.optimization_barrier(
        (rows, radial_step, far_weights, flux_weights)
    )
    weights = step_weights(radial_step)
    fw = jnp.concatenate([far_weights, far_weights])[None, :]
    flux = flux_rows(flux_weights)
    got = lax.all_to_all(rows, "tile", split_axis=0, concat_axis=0, tiled=True)
    layers, ends = lax.optimization_barrier((enthalpy, ends))
    heat = home_heat(rows, fw, weights, flux)
    new_enthalpy = deposit(
        lanes, heat, table, velocity.reshape(ROWS, 128), diffusivity.reshape(ROWS, 128),
        wall_flux, edges_of(layers, ends),
    ).reshape(enthalpy.shape)
    new_profiles = settle(got, fw, weights)
    return new_enthalpy, new_profiles


def solution(mesh):
    return jax.shard_map(
        on_device,
        mesh=mesh,
        in_specs=(
            P("stream", None, "tile"),
            P("stream", None, "tile"),
            P("stream", None, "tile"),
            P("stream", "tile"),
            P(None, ("stream", "tile")),
            P(("stream", "tile")),
            P(("stream", "tile")),
            P(("stream", "tile")),
            P(),
            P(),
            P(),
        ),
        out_specs=(P("stream", None, "tile"), P(None, ("stream", "tile"))),
        check_vma=False,
    )
```

```python
import jax
import jax.numpy as jnp
from jax import lax
from jax.experimental import pallas as pl
from jax.experimental.pallas import tpu as pltpu
from jax.sharding import PartitionSpec as P

SUB = 16
PTS = 64
NT = 32
CAP = 16384
OWN = 6144
MSG = 512
HALF = MSG // 2
LOAD = HALF + 8
BLK = 256
NBLK = CAP // BLK
STRIDE = MSG + 16
ROWS = 1024
OWN2 = OWN // 2

GROUP = 4
ROOM = 60 * 2**20

F32, BF16, I32 = jnp.float32, jnp.bfloat16, jnp.int32
NTD = (((1,), (1,)), ((), ()))


def iota(shape, dim):
    return lax.broadcasted_iota(I32, shape, dim)


def split(x):
    high = x.astype(BF16)
    return high, (x - high.astype(F32)).astype(BF16)


def dot(a, b):
    return jnp.dot(a, b, preferred_element_type=F32)


def dot_nt(a, b):
    return lax.dot_general(a, b, NTD, preferred_element_type=F32)


def route_kernel(
    count_ref, owners_ref, cells_ref, field_ref, prof_ref,
    rows_ref, lanes_ref, ends_ref,
    pos_s, m0_s, m1_s, m2_s, m3_s, m4_s, sorted_a, sorted_b, sorted_c, sorted_d,
    bucket, tab_v, tab_s, sem, prof_v, prof_sem, pack_v, pack_sem, meta_v, table,
):
    count = count_ref[0]
    fetch = pltpu.make_async_copy(prof_ref, prof_v, prof_sem)
    fetch.start()

    def blocks(ref):
        x = ref[...].reshape(NBLK, 2, 128)
        return jnp.concatenate([x[:, 0], x[:, 1]], axis=1)

    slot = iota((NBLK, BLK), 0) * BLK + iota((NBLK, BLK), 1)
    owners = blocks(owners_ref)
    dest = jnp.floor((owners.astype(F32) + 0.5) * (1.0 / OWN)).astype(I32)
    within = owners - dest * OWN
    live = slot < count
    dest = jnp.where(live, dest, NT)
    cells = blocks(cells_ref)
    m0_s[...] = (cells & 127).astype(F32)
    m1_s[...] = ((cells >> 7) & 3).astype(F32)
    m2_s[...] = (cells >> 9).astype(F32)
    m3_s[...] = (within & 255).astype(F32)
    m4_s[...] = (within >> 8).astype(F32)

    sub, lane = iota((BLK, BLK), 0), iota((BLK, BLK), 1)
    one, nil = jnp.ones((), F32), jnp.zeros((), F32)
    before = jnp.where(sub < lane, one, nil).astype(BF16)
    same_block = (sub >> 5) == (lane >> 5)
    same_dest = (sub & 31) == (lane & 31)
    seg_left = jnp.where(same_block & (lane < sub), one, nil).astype(BF16)
    seg_right = jnp.where(same_block & (sub < lane), one, nil).astype(BF16)
    base_right = jnp.where(same_dest & ((sub >> 5) < (lane >> 5)), one, nil).astype(BF16)
    all_right = jnp.where(same_dest, one, nil).astype(BF16)
    ones_a = jnp.ones((8, BLK), BF16)
    ones_b = jnp.ones((BLK, 128), BF16)
    run = jnp.zeros((8, BLK), F32)
    longest = jnp.zeros((8, BLK), F32)
    for c in range(8):
        part = dest[8 * c : 8 * c + 8]
        hot = jnp.where(part[:, None, :] == iota((8, NT, BLK), 1), one, nil).reshape(BLK, BLK)
        hot_b = hot.astype(BF16)
        prefix = dot(hot_b, before)
        amount = dot(hot_b, ones_b)
        seg = dot(seg_left, amount.astype(BF16))
        seg2 = jnp.concatenate([seg, seg], axis=1)
        pos = jnp.sum((hot * (prefix + seg2)).reshape(8, NT, BLK), axis=1)
        pos_s[8 * c : 8 * c + 8] = jnp.where(live[8 * c : 8 * c + 8], pos, 511.0)
        amount_l = dot_nt(ones_a, hot_b)
        amount_lb = amount_l.astype(BF16)
        src = dot(amount_lb, seg_right)
        base = dot(amount_lb, base_right) + run
        run = run + dot(amount_lb, all_right)
        longest = jnp.maximum(longest, amount_l)
        most = amount_l
        for shift in (1, 2, 4, 8, 16):
            most = jnp.maximum(most, pltpu.roll(most, BLK - shift, 1))
        first = iota((8, BLK), 1) & 31
        row8 = iota((8, BLK), 0)
        packed = jnp.where(row8 == 0, src, nil)
        packed = jnp.where(row8 == 1, base + (first * STRIDE).astype(F32), packed)
        packed = jnp.where(row8 == 2, amount_l, packed)
        packed = jnp.where(row8 == 3, most, packed)
        packed = packed.astype(I32)
        tab_v[16 * c : 16 * c + 8] = packed[:, :128]
        tab_v[16 * c + 8 : 16 * c + 16] = packed[:, 128:]
    copy = pltpu.make_async_copy(tab_v, tab_s, sem)
    copy.start()
    short = jnp.max(longest) <= 8.0
    total = run

    zero8 = jnp.zeros((STRIDE, 128), F32)

    @pl.loop(0, NT)
    def _(d):
        bucket[pl.ds(pl.multiple_of(d * STRIDE, 8), STRIDE)] = zero8

    copy.wait()
    fetch.wait()

    meta_rest = jnp.zeros((56, BLK), BF16)
    low_rest = jnp.zeros((64, BLK), BF16)
    row8 = iota((8, BLK), 0)

    def sort_block(j, out):
        x = prof_v[:, pl.ds(pl.multiple_of(j * BLK, BLK), BLK)]
        high, low = split(x)
        meta = jnp.zeros((8, BLK), F32)
        for k, ref in enumerate((m0_s, m1_s, m2_s, m3_s, m4_s)):
            meta = jnp.where(row8 == k, ref[pl.ds(j, 1), :], meta)
        data = jnp.concatenate([high, meta.astype(BF16), meta_rest, low, low_rest], axis=0)
        place = pos_s[pl.ds(j, 1), :].astype(I32)
        perm = jnp.where(place == sub, one, nil).astype(BF16)
        got = dot_nt(perm, data)
        out[0:BLK] = got[:, :128] + got[:, 128:]

    def copy_block(p, c, inp):
        chunk, at = p * 8, c * NT
        most = tab_s[chunk + 3, at]

        @pl.when(most <= 8)
        def _():
            for d in range(NT):
                src = tab_s[chunk, at + d]
                dst = tab_s[chunk + 1, at + d]
                bucket[pl.ds(dst, 8)] = inp[pl.ds(src, 8)]

        @pl.when((most > 8) & (most <= 16))
        def _():
            for d in range(NT):
                src = tab_s[chunk, at + d]
                dst = tab_s[chunk + 1, at + d]
                bucket[pl.ds(dst, 16)] = inp[pl.ds(src, 16)]

        @pl.when(most > 16)
        def _():
            @pl.loop(0, NT)
            def _(d):
                src = tab_s[chunk, at + d]
                dst = tab_s[chunk + 1, at + d]

                @pl.loop(0, (tab_s[chunk + 2, at + d] + 7) >> 3)
                def _(k):
                    bucket[pl.ds(dst + 8 * k, 8)] = inp[pl.ds(src + 8 * k, 8)]

    def copy_short(p, c, inp):
        chunk, at = p * 8, c * NT
        for d in range(NT):
            src = tab_s[chunk, at + d]
            dst = tab_s[chunk + 1, at + d]
            bucket[pl.ds(dst, 8)] = inp[pl.ds(src, 8)]

    for ref in (sorted_a, sorted_b, sorted_c, sorted_d):
        ref[BLK:] = jnp.zeros((16, 128), F32)
    quads = (count + 4 * BLK - 1) // (4 * BLK)
    sort_block(0, sorted_a)
    sort_block(1, sorted_b)

    def quad(copy_any):
        @pl.loop(0, quads)
        def _(p):
            sort_block(4 * p + 2, sorted_c)
            copy_any(p, 0, sorted_a)
            sort_block(4 * p + 3, sorted_d)
            copy_any(p, 1, sorted_b)
            sort_block(jnp.minimum(4 * p + 4, NBLK - 1), sorted_a)
            copy_any(p, 2, sorted_c)
            sort_block(jnp.minimum(4 * p + 5, NBLK - 1), sorted_b)
            copy_any(p, 3, sorted_d)

    pl.when(short)(lambda: quad(copy_short))
    pl.when(jnp.logical_not(short))(lambda: quad(copy_block))

    low_lanes = iota((HALF, 128), 1) < 64
    r8, l8 = iota((8, 128), 0), iota((8, 128), 1)
    pick = jnp.where((r8 == 0) & (l8 == 64), one, nil)
    pick = jnp.where((r8 == 1) & (l8 == 65), one, pick)
    pick = jnp.where((r8 == 1) & (l8 == 66), 4.0 * one, pick)
    pick = jnp.where((r8 == 2) & (l8 == 67), one, pick)
    pick = jnp.where((r8 == 2) & (l8 == 68), 256.0 * one, pick)
    pick = pick.astype(BF16)
    rank = iota((8, MSG), 1)
    rank_row = iota((8, MSG), 0)
    lane_dest = iota((8, BLK), 1)

    def send(g):
        part = pl.ds(g * GROUP, GROUP)
        return pltpu.make_async_copy(pack_v.at[part], rows_ref.at[part], pack_sem.at[g])

    def pack(g):
        for k in range(GROUP):
            d = GROUP * g + k
            at = pl.multiple_of(d * STRIDE, 8)
            lo = bucket[pl.ds(at, HALF)]
            hi = bucket[pl.ds(pl.multiple_of(at + HALF, 8), HALF)]
            pack_v[d, 0:HALF] = jnp.where(low_lanes, lo, pltpu.roll(hi, 64, 1))
            meta_v[d] = jnp.where(low_lanes, pltpu.roll(lo, 64, 1), hi).astype(BF16)
            both = jnp.concatenate([lo, hi], axis=0).astype(BF16)
            nums = dot_nt(pick, both)
            mine = jnp.max(jnp.where(lane_dest == d, total, nil), axis=1, keepdims=True)
            valid = rank.astype(F32) < mine
            nums = jnp.where((rank_row == 2) & ~valid, float(OWN), nums)
            nums = jnp.where(rank_row == 3, jnp.where(valid, one, nil), nums)
            lanes_ref[d] = nums
            pack_v[d, HALF : HALF + 4] = jnp.concatenate(
                [nums[2:3, 128 * q : 128 * q + 128] for q in range(4)], axis=0
            )

    cells = field_ref[...].reshape(ROWS // 4, 4, 128)
    parts = [split(cells[:, q]) for q in range(4)]
    table[...] = jnp.concatenate([p[0] for p in parts] + [p[1] for p in parts], axis=1)
    m_rows = GROUP * HALF
    ones8 = jnp.ones((8, 256), BF16)
    sub128 = iota((128, 128), 0)
    place = iota((m_rows, 128), 1).astype(F32)

    def far(g):
        meta = meta_v[pl.ds(g * GROUP, GROUP)].reshape(m_rows, 128)
        for h in range(2):
            first = 0 if h == 0 else 64
            col = jnp.where(sub128 == first, one, nil) + jnp.where(sub128 == first + 1, 128.0 * one, nil)
            row = jnp.where(sub128 == first + 2, one, nil)
            got = dot(meta, jnp.concatenate([col, row], axis=1).astype(BF16))
            col, row = got[:, :128], got[:, 128:]
            hot = jnp.concatenate(
                [jnp.where(row == place + 128.0 * q, one, nil).astype(BF16) for q in range(2)], axis=1
            )
            val = dot(hot, table[...])
            got = jnp.zeros((m_rows, 128), F32)
            for q in range(4):
                both = val[:, 128 * q : 128 * q + 128] + val[:, 512 + 128 * q : 640 + 128 * q]
                got = jnp.where(col == place + 128.0 * q, both, got)
            v0, v1 = split(got)
            far_l = dot_nt(ones8, jnp.concatenate([v0, v1], axis=1))
            for i in range(GROUP):
                for q in range(2):
                    at = HALF * i + 128 * q
                    row_at = HALF + 4 + 2 * h + q
                    pack_v[GROUP * g + i, row_at : row_at + 1] = far_l[0:1, at : at + 128]

    pack(0)

    @pl.loop(0, NT // GROUP - 1)
    def _(g):
        far(g)
        pack(g + 1)
        send(g).start()

    far(NT // GROUP - 1)
    send(NT // GROUP - 1).start()
    pick = jnp.where((r8 == 0) & (l8 == 0), one, nil) + jnp.where((r8 == 1) & (l8 == 127), one, nil)
    pick = pick.astype(BF16)
    f0, f1 = split(field_ref[...])
    f2 = (field_ref[...] - f0.astype(F32) - f1.astype(F32)).astype(BF16)
    ends_ref[...] = dot_nt(pick, f0) + dot_nt(pick, f1) + dot_nt(pick, f2)
    for g in range(NT // GROUP):
        send(g).wait()


def route(counts, owners, cells, field, profiles):
    vmem = pl.BlockSpec(memory_space=pltpu.VMEM)
    anywhere = pl.BlockSpec(memory_space=pl.ANY)
    return pl.pallas_call(
        route_kernel,
        out_shape=(
            jax.ShapeDtypeStruct((NT, LOAD, 128), F32),
            jax.ShapeDtypeStruct((NT, 8, MSG), F32),
            jax.ShapeDtypeStruct((8, ROWS), F32),
        ),
        in_specs=[pl.BlockSpec(memory_space=pltpu.SMEM), vmem, vmem, vmem, anywhere],
        out_specs=(anywhere, vmem, vmem),
        scratch_shapes=[pltpu.VMEM((NBLK, BLK), F32)] * 6
        + [pltpu.VMEM((BLK + 16, 128), F32)] * 4
        + [
            pltpu.VMEM((NT * STRIDE, 128), F32),
            pltpu.VMEM((128, 128), I32),
            pltpu.SMEM((128, 128), I32),
            pltpu.SemaphoreType.DMA,
            pltpu.VMEM((PTS, CAP), F32),
            pltpu.SemaphoreType.DMA,
            pltpu.VMEM((NT, LOAD, 128), F32),
            pltpu.SemaphoreType.DMA((NT // GROUP,)),
            pltpu.VMEM((NT, HALF, 128), BF16),
            pltpu.VMEM((ROWS // 4, 1024), BF16),
        ],
        compiler_params=pltpu.CompilerParams(vmem_limit_bytes=ROOM),
        name="route",
    )(counts, owners.reshape(128, 128), cells.reshape(128, 128), field, profiles)


def step_weights(radial_step):
    zero = jnp.zeros((PTS, PTS), F32)
    w = jnp.concatenate(
        [
            jnp.concatenate([radial_step.T, zero], axis=1),
            jnp.concatenate([zero, radial_step.T], axis=1),
        ],
        axis=0,
    )
    high = lax.reduce_precision(w, 8, 7)
    w0, w1 = high.astype(BF16), (w - high).astype(BF16)
    row = jnp.concatenate([w0, w1], axis=1)
    return jnp.concatenate([row, row], axis=0)


def flux_rows(flux_weights):
    zero = jnp.zeros((PTS,), F32)
    f = jnp.stack(
        [jnp.concatenate([flux_weights, zero]), jnp.concatenate([zero, flux_weights])]
        + [jnp.zeros((128,), F32)] * 6
    )
    return f / SUB


def substep(state, add, weights):
    s0, s1 = split(state)
    got = dot(jnp.concatenate([s0, s1], axis=1), weights)
    return (got[:, :128] + got[:, 128:]) + (add + 0.25 * jnp.tanh(state))


HEAT_N = GROUP


def far_columns(side):
    far = jnp.concatenate([side[4 + q : 5 + q] for q in range(4)], axis=1)
    rest = far - far.astype(BF16).astype(F32)
    row8 = iota((8, MSG), 0)
    terms = jnp.where(row8 == 0, far, jnp.where(row8 == 1, rest, 0.0)).astype(BF16)
    pick = jnp.where(iota((8, 128), 0) < 2, 1.0, 0.0).astype(BF16)
    return lax.dot_general(terms, pick, (((0,), (0,)), ((), ())), preferred_element_type=F32)


def heat_kernel(rows_ref, side_ref, fw_ref, weights_ref, flux_ref, heat_ref):
    weights = weights_ref[...]
    state = rows_ref[...].reshape(HEAT_N * HALF, 128)
    low_lanes = iota((HALF, 128), 1) < 64
    adds = []
    for i in range(HEAT_N):
        far = far_columns(side_ref[i])
        adds.append(fw_ref[...] * jnp.where(low_lanes, far[:HALF], far[HALF:]))
    add = jnp.concatenate(adds, axis=0)
    total = jnp.zeros_like(state)
    for _ in range(SUB):
        state = substep(state, add, weights)
        total = total + state
    t0, t1 = split(total)
    f0, f1 = split(flux_ref[...])
    heat = dot_nt(f0, t0) + dot_nt(f0, t1) + dot_nt(f1, t0)
    for i in range(HEAT_N):
        heat_ref[i] = heat[:, HALF * i : HALF * i + HALF]


def home_heat(rows, fw, weights, flux):
    steps = NT // HEAT_N
    return pl.pallas_call(
        heat_kernel,
        grid=(steps,),
        out_shape=jax.ShapeDtypeStruct((steps * HEAT_N, 8, HALF), F32),
        in_specs=[
            pl.BlockSpec((HEAT_N, HALF, 128), lambda d: (d, 0, 0)),
            pl.BlockSpec((HEAT_N, 8, 128), lambda d: (d, HALF // 8, 0)),
            pl.BlockSpec((1, 128), lambda d: (0, 0)),
            pl.BlockSpec((256, 256), lambda d: (0, 0)),
            pl.BlockSpec((8, 128), lambda d: (0, 0)),
        ],
        out_specs=pl.BlockSpec((HEAT_N, 8, HALF), lambda d: (d, 0, 0)),
        compiler_params=pltpu.CompilerParams(vmem_limit_bytes=ROOM),
        cost_estimate=pl.CostEstimate(
            flops=25 * 10**8 * steps, bytes_accessed=steps << 20, transcendentals=steps << 21
        ),
        name="home_heat",
    )(rows, rows, fw, weights, flux)


DEP_N = GROUP


def deposit_kernel(
    lanes_ref, heat_ref, cells_ref, vel_ref, dif_ref, flux_ref, below_ref, above_ref,
    out_ref, acc,
):
    d = pl.program_id(0)

    @pl.when(d == 0)
    def _():
        acc[...] = jnp.zeros_like(acc)

    one, nil = jnp.ones((), F32), jnp.zeros((), F32)
    width = DEP_N * MSG
    cols, rows, heats = [], [], []
    for i in range(DEP_N):
        nums = lanes_ref[i]
        heat = jnp.concatenate([heat_ref[i, 0:1], heat_ref[i, 1:2]], axis=1)
        cols.append(nums[0:1])
        rows.append(nums[1:2])
        heats.append(jnp.where(nums[3:4] > 0.5, 0.5 * heat, nil))
    col = jnp.concatenate(cols, axis=1).astype(I32)
    row = jnp.concatenate(rows, axis=1).astype(I32)
    heat = jnp.concatenate(heats, axis=1)
    high = heat.astype(BF16).astype(F32)
    here = col == iota((128, width), 0)
    spread = jnp.concatenate(
        [jnp.where(here, high, nil).astype(BF16), jnp.where(here, heat - high, nil).astype(BF16)], axis=0
    )
    hot = jnp.where(row == iota((ROWS, width), 0), one, nil).astype(BF16)
    acc[...] += dot_nt(hot, spread)

    @pl.when(d == NT // DEP_N - 1)
    def _():
        layers = ROWS // 64
        wall, lane = iota((64, 128), 0), iota((64, 128), 1)
        for x in range(layers):
            at = 64 * x
            h = cells_ref[at : at + 64]
            x_lower = cells_ref[at - 64 : at] if x else below_ref[...]
            x_upper = cells_ref[at + 64 : at + 128] if x < layers - 1 else above_ref[...]
            w_lower = jnp.where(wall == 0, h, pltpu.roll(h, 1, 0))
            w_upper = jnp.where(wall == 63, h, pltpu.roll(h, 63, 0))
            s_lower = jnp.where(lane == 0, nil, pltpu.roll(h, 1, 1))
            s_upper = jnp.where(lane == 127, nil, pltpu.roll(h, 127, 1))
            laplace = (x_lower + x_upper) + (w_lower + w_upper) + (s_lower + s_upper) - 6.0 * h
            new = h + dif_ref[at : at + 64] * laplace - vel_ref[at : at + 64] * (h - x_lower)
            new = new + jnp.where(wall == 0, flux_ref[x : x + 1], nil)
            out_ref[at : at + 64] = new + (acc[at : at + 64, :128] + acc[at : at + 64, 128:])


def deposit(lanes, heat, cells, velocity, diffusivity, wall_flux, below, above):
    def whole(shape):
        return pl.BlockSpec(shape, lambda d: (0, 0))

    field = whole((ROWS, 128))
    return pl.pallas_call(
        deposit_kernel,
        grid=(NT // DEP_N,),
        out_shape=jax.ShapeDtypeStruct((ROWS, 128), F32),
        in_specs=[
            pl.BlockSpec((DEP_N, 8, MSG), lambda d: (d, 0, 0)),
            pl.BlockSpec((DEP_N, 8, HALF), lambda d: (d, 0, 0)),
            field,
            field,
            field,
            whole((ROWS // 64, 128)),
            whole((64, 128)),
            whole((64, 128)),
        ],
        out_specs=field,
        scratch_shapes=[pltpu.VMEM((ROWS, 256), F32)],
        compiler_params=pltpu.CompilerParams(vmem_limit_bytes=40 * 2**20),
        cost_estimate=pl.CostEstimate(flops=10**10, bytes_accessed=4 << 20, transcendentals=0),
        name="deposit",
    )(lanes, heat, cells, velocity, diffusivity, wall_flux, below, above)


def span_kernel(new_ref, dif_ref, left_ref, right_ref, out_ref):
    row8, lane = iota((8, ROWS), 0), iota((8, 128), 1)
    terms = jnp.zeros((8, ROWS), F32)
    for i, ref in enumerate((left_ref, right_ref)):
        rest = ref[...]
        for k in range(3):
            high = rest.astype(BF16).astype(F32)
            terms = jnp.where(row8 == 3 * i + k, high, terms)
            rest = rest - high
    row = iota((8, 128), 0)
    first, last = (row < 3) & (lane == 0), (row >= 3) & (row < 6) & (lane == 127)
    pick = jnp.where(first | last, 1.0, 0.0).astype(BF16)
    ends = lax.dot_general(terms.astype(BF16), pick, (((0,), (0,)), ((), ())), preferred_element_type=F32)
    out_ref[...] = new_ref[...] + dif_ref[...] * ends


def add_span(new, diffusivity, left, right):
    vmem = pl.BlockSpec(memory_space=pltpu.VMEM)
    return pl.pallas_call(
        span_kernel,
        out_shape=jax.ShapeDtypeStruct((ROWS, 128), F32),
        in_specs=[vmem] * 4,
        out_specs=vmem,
        cost_estimate=pl.CostEstimate(flops=10**7, bytes_accessed=2 << 20, transcendentals=0),
        name="span",
    )(new, diffusivity, left, right)


SETTLE = 1024


def settle_kernel(
    rows_ref, fw_ref, weights_ref, out_ref,
    stage, comb, got, got_sem, side, side_sem, slot_v, slot_s, slot_sem, amount_v, amount_s, amount_sem,
):
    fetch_side = pltpu.make_async_copy(rows_ref.at[:, pl.ds(HALF, 8)], side, side_sem)
    fetch_side.start()

    def fetch(g):
        part = pl.ds(g * GROUP, GROUP)
        return pltpu.make_async_copy(rows_ref.at[part, pl.ds(0, HALF)], got.at[part], got_sem.at[g])

    for g in range(NT // GROUP):
        fetch(g).start()
    fetch_side.wait()
    for t in range(NT):
        slot_v[4 * t : 4 * t + 4] = side[t, 0:4].astype(I32)
    valid = jnp.where(slot_v[...] < OWN, 1.0, 0.0).astype(BF16)
    by_row = dot(valid, jnp.ones((128, 128), BF16)).astype(BF16)
    of_sender = jnp.where(iota((NT, 128), 1) >> 2 == iota((NT, 128), 0), 1.0, 0.0).astype(BF16)
    amount_v[...] = dot(of_sender, by_row).astype(I32)
    copies = (
        pltpu.make_async_copy(slot_v, slot_s, slot_sem),
        pltpu.make_async_copy(amount_v, amount_s, amount_sem),
    )
    for copy in copies:
        copy.start()

    low_lanes = iota((HALF, 128), 1) < 64

    for g in range(NT // GROUP):
        fetch(g).wait()

    @pl.loop(0, NT // GROUP, unroll=2)
    def _(g):
        for k in range(GROUP):
            t = GROUP * g + k
            rows = got[t]
            col = far_columns(side[t])
            at = pl.multiple_of(t * MSG, MSG)
            comb[pl.ds(at, HALF)] = jnp.where(low_lanes, rows, col[:HALF])
            comb[pl.ds(pl.multiple_of(at + HALF, HALF), HALF)] = jnp.where(
                low_lanes, pltpu.roll(rows, 64, 1), col[HALF:]
            )

    for copy in copies:
        copy.wait()

    @pl.loop(0, NT)
    def _(t):
        amount = amount_s[t, 0]

        @pl.loop(0, (amount + 127) >> 7)
        def _(r):
            row = 4 * t + r
            for lane in range(0, 128, 32):

                @pl.when(amount > r * 128 + lane)
                def _():
                    at = pl.multiple_of(t * MSG + r * 128 + lane, 32)
                    for i in range(32):
                        stage[pl.ds(slot_s[row, lane + i], 1)] = comb[pl.ds(at + i, 1)]

    weights = weights_ref[...]
    fw = fw_ref[...]
    low_lanes = iota((SETTLE, 128), 1) < 64
    for c in range(OWN2 // SETTLE):
        at = c * SETTLE
        a = stage[at : at + SETTLE]
        b = stage[at + OWN2 : at + OWN2 + SETTLE]
        state = jnp.where(low_lanes, a, pltpu.roll(b, 64, 1))
        add = fw * jnp.where(low_lanes, pltpu.roll(a, 64, 1), b)
        for _ in range(SUB):
            state = substep(state, add, weights)
        for k in range(SETTLE // 128):
            turned = state[128 * k : 128 * k + 128].T
            out_ref[:, at + 128 * k : at + 128 * k + 128] = turned[:64]
            out_ref[:, at + OWN2 + 128 * k : at + OWN2 + 128 * k + 128] = turned[64:]


def settle(rows, fw, weights):
    vmem = pl.BlockSpec(memory_space=pltpu.VMEM)
    return pl.pallas_call(
        settle_kernel,
        out_shape=jax.ShapeDtypeStruct((PTS, OWN), F32),
        in_specs=[pl.BlockSpec(memory_space=pl.ANY), vmem, vmem],
        out_specs=vmem,
        scratch_shapes=[
            pltpu.VMEM((OWN + 8, 128), F32),
            pltpu.VMEM((NT * MSG, 128), F32),
            pltpu.VMEM((NT, HALF, 128), F32),
            pltpu.SemaphoreType.DMA((NT // GROUP,)),
            pltpu.VMEM((NT, 8, 128), F32),
            pltpu.SemaphoreType.DMA,
            pltpu.VMEM((128, 128), I32),
            pltpu.SMEM((128, 128), I32),
            pltpu.SemaphoreType.DMA,
            pltpu.VMEM((NT, 128), I32),
            pltpu.SMEM((NT, 128), I32),
            pltpu.SemaphoreType.DMA,
        ],
        compiler_params=pltpu.CompilerParams(vmem_limit_bytes=ROOM),
        name="settle",
    )(rows, fw, weights)


def edges_of(cells, ends):
    n_x, n_s = lax.axis_size("stream"), lax.axis_size("tile")
    up_x = [(i, i + 1) for i in range(n_x - 1)]
    down_x = [(i + 1, i) for i in range(n_x - 1)]
    up_s = [(i, (i + 1) % n_s) for i in range(n_s)]
    down_s = [((i + 1) % n_s, i) for i in range(n_s)]
    below = lax.ppermute(cells[-1], "stream", up_x)
    above = lax.ppermute(cells[0], "stream", down_x)
    left = lax.ppermute(ends[1:2], "tile", up_s)
    right = lax.ppermute(ends[0:1], "tile", down_s)
    return below, above, left, right


def on_device(
    enthalpy, velocity, diffusivity, wall_flux, profiles, counts, owners, cells,
    radial_step, far_weights, flux_weights,
):
    table = enthalpy.reshape(ROWS, 128)
    rows, lanes, ends = route(counts, owners, cells, table, profiles)
    rows, radial_step, far_weights, flux_weights = lax.optimization_barrier(
        (rows, radial_step, far_weights, flux_weights)
    )
    weights = step_weights(radial_step)
    fw = jnp.concatenate([far_weights, far_weights])[None, :]
    flux = flux_rows(flux_weights)
    got = lax.all_to_all(rows, "tile", split_axis=0, concat_axis=0, tiled=True)
    layers, ends = lax.optimization_barrier((enthalpy, ends))
    heat = home_heat(rows, fw, weights, flux)
    below, above, left, right = edges_of(layers, ends)
    spread = diffusivity.reshape(ROWS, 128)
    new = deposit(lanes, heat, table, velocity.reshape(ROWS, 128), spread, wall_flux, below, above)
    new_enthalpy = add_span(new, spread, left, right).reshape(enthalpy.shape)
    new_profiles = settle(got, fw, weights)
    return new_enthalpy, new_profiles


def solution(mesh):
    return jax.shard_map(
        on_device,
        mesh=mesh,
        in_specs=(
            P("stream", None, "tile"),
            P("stream", None, "tile"),
            P("stream", None, "tile"),
            P("stream", "tile"),
            P(None, ("stream", "tile")),
            P(("stream", "tile")),
            P(("stream", "tile")),
            P(("stream", "tile")),
            P(),
            P(),
            P(),
        ),
        out_specs=(P("stream", None, "tile"), P(None, ("stream", "tile"))),
        check_vma=False,
    )
```

```python
import jax
import jax.numpy as jnp
from jax import lax
from jax.experimental import pallas as pl
from jax.experimental.pallas import tpu as pltpu
from jax.sharding import PartitionSpec as P

SUB = 16
PTS = 64
NT = 32
CAP = 16384
OWN = 6144
MSG = 512
HALF = MSG // 2
LOAD = HALF + 8
BLK = 256
NBLK = CAP // BLK
STRIDE = MSG + 16
ROWS = 1024
OWN2 = OWN // 2

GROUP = 4
ROOM = 60 * 2**20

F32, BF16, I32 = jnp.float32, jnp.bfloat16, jnp.int32
NTD = (((1,), (1,)), ((), ()))


def iota(shape, dim):
    return lax.broadcasted_iota(I32, shape, dim)


def split(x):
    high = x.astype(BF16)
    return high, (x - high.astype(F32)).astype(BF16)


def dot(a, b):
    return jnp.dot(a, b, preferred_element_type=F32)


def dot_nt(a, b):
    return lax.dot_general(a, b, NTD, preferred_element_type=F32)


def route_kernel(
    count_ref, owners_ref, cells_ref, field_ref, prof_ref,
    rows_ref, lanes_ref, ends_ref,
    pos_s, m0_s, m1_s, m2_s, m3_s, m4_s, sorted_a, sorted_b, sorted_c, sorted_d,
    bucket, tab_v, tab_s, sem, prof_v, prof_sem, pack_v, pack_sem, meta_v, table,
):
    count = count_ref[0]
    fetch = pltpu.make_async_copy(prof_ref, prof_v, prof_sem)
    fetch.start()

    def blocks(ref):
        x = ref[...].reshape(NBLK, 2, 128)
        return jnp.concatenate([x[:, 0], x[:, 1]], axis=1)

    slot = iota((NBLK, BLK), 0) * BLK + iota((NBLK, BLK), 1)
    owners = blocks(owners_ref)
    dest = jnp.floor((owners.astype(F32) + 0.5) * (1.0 / OWN)).astype(I32)
    within = owners - dest * OWN
    live = slot < count
    dest = jnp.where(live, dest, NT)
    cells = blocks(cells_ref)
    m0_s[...] = (cells & 127).astype(F32)
    m1_s[...] = ((cells >> 7) & 3).astype(F32)
    m2_s[...] = (cells >> 9).astype(F32)
    m3_s[...] = (within & 255).astype(F32)
    m4_s[...] = (within >> 8).astype(F32)

    sub, lane = iota((BLK, BLK), 0), iota((BLK, BLK), 1)
    one, nil = jnp.ones((), F32), jnp.zeros((), F32)
    before = jnp.where(sub < lane, one, nil).astype(BF16)
    same_block = (sub >> 5) == (lane >> 5)
    same_dest = (sub & 31) == (lane & 31)
    seg_left = jnp.where(same_block & (lane < sub), one, nil).astype(BF16)
    seg_right = jnp.where(same_block & (sub < lane), one, nil).astype(BF16)
    base_right = jnp.where(same_dest & ((sub >> 5) < (lane >> 5)), one, nil).astype(BF16)
    all_right = jnp.where(same_dest, one, nil).astype(BF16)
    ones_a = jnp.ones((8, BLK), BF16)
    ones_b = jnp.ones((BLK, 128), BF16)
    run = jnp.zeros((8, BLK), F32)
    longest = jnp.zeros((8, BLK), F32)
    for c in range(8):
        part = dest[8 * c : 8 * c + 8]
        hot = jnp.where(part[:, None, :] == iota((8, NT, BLK), 1), one, nil).reshape(BLK, BLK)
        hot_b = hot.astype(BF16)
        prefix = dot(hot_b, before)
        amount = dot(hot_b, ones_b)
        seg = dot(seg_left, amount.astype(BF16))
        seg2 = jnp.concatenate([seg, seg], axis=1)
        pos = jnp.sum((hot * (prefix + seg2)).reshape(8, NT, BLK), axis=1)
        pos_s[8 * c : 8 * c + 8] = jnp.where(live[8 * c : 8 * c + 8], pos, 511.0)
        amount_l = dot_nt(ones_a, hot_b)
        amount_lb = amount_l.astype(BF16)
        src = dot(amount_lb, seg_right)
        base = dot(amount_lb, base_right) + run
        run = run + dot(amount_lb, all_right)
        longest = jnp.maximum(longest, amount_l)
        most = amount_l
        for shift in (1, 2, 4, 8, 16):
            most = jnp.maximum(most, pltpu.roll(most, BLK - shift, 1))
        first = iota((8, BLK), 1) & 31
        row8 = iota((8, BLK), 0)
        packed = jnp.where(row8 == 0, src, nil)
        packed = jnp.where(row8 == 1, base + (first * STRIDE).astype(F32), packed)
        packed = jnp.where(row8 == 2, amount_l, packed)
        packed = jnp.where(row8 == 3, most, packed)
        packed = packed.astype(I32)
        tab_v[16 * c : 16 * c + 8] = packed[:, :128]
        tab_v[16 * c + 8 : 16 * c + 16] = packed[:, 128:]
    copy = pltpu.make_async_copy(tab_v, tab_s, sem)
    copy.start()
    short = jnp.max(longest) <= 8.0
    total = run

    zero8 = jnp.zeros((STRIDE, 128), F32)

    @pl.loop(0, NT)
    def _(d):
        bucket[pl.ds(pl.multiple_of(d * STRIDE, 8), STRIDE)] = zero8

    copy.wait()
    fetch.wait()

    meta_rest = jnp.zeros((56, BLK), BF16)
    low_rest = jnp.zeros((64, BLK), BF16)
    row8 = iota((8, BLK), 0)

    def sort_block(j, out):
        x = prof_v[:, pl.ds(pl.multiple_of(j * BLK, BLK), BLK)]
        high, low = split(x)
        meta = jnp.zeros((8, BLK), F32)
        for k, ref in enumerate((m0_s, m1_s, m2_s, m3_s, m4_s)):
            meta = jnp.where(row8 == k, ref[pl.ds(j, 1), :], meta)
        data = jnp.concatenate([high, meta.astype(BF16), meta_rest, low, low_rest], axis=0)
        place = pos_s[pl.ds(j, 1), :].astype(I32)
        perm = jnp.where(place == sub, one, nil).astype(BF16)
        got = dot_nt(perm, data)
        out[0:BLK] = got[:, :128] + got[:, 128:]

    def copy_block(p, c, inp):
        chunk, at = p * 8, c * NT
        most = tab_s[chunk + 3, at]

        @pl.when(most <= 8)
        def _():
            for d in range(NT):
                src = tab_s[chunk, at + d]
                dst = tab_s[chunk + 1, at + d]
                bucket[pl.ds(dst, 8)] = inp[pl.ds(src, 8)]

        @pl.when((most > 8) & (most <= 16))
        def _():
            for d in range(NT):
                src = tab_s[chunk, at + d]
                dst = tab_s[chunk + 1, at + d]
                bucket[pl.ds(dst, 16)] = inp[pl.ds(src, 16)]

        @pl.when(most > 16)
        def _():
            @pl.loop(0, NT)
            def _(d):
                src = tab_s[chunk, at + d]
                dst = tab_s[chunk + 1, at + d]

                @pl.loop(0, (tab_s[chunk + 2, at + d] + 7) >> 3)
                def _(k):
                    bucket[pl.ds(dst + 8 * k, 8)] = inp[pl.ds(src + 8 * k, 8)]

    def copy_short(p, c, inp):
        chunk, at = p * 8, c * NT
        for d in range(NT):
            src = tab_s[chunk, at + d]
            dst = tab_s[chunk + 1, at + d]
            bucket[pl.ds(dst, 8)] = inp[pl.ds(src, 8)]

    for ref in (sorted_a, sorted_b, sorted_c, sorted_d):
        ref[BLK:] = jnp.zeros((16, 128), F32)
    quads = (count + 4 * BLK - 1) // (4 * BLK)
    sort_block(0, sorted_a)
    sort_block(1, sorted_b)

    def quad(copy_any):
        @pl.loop(0, quads)
        def _(p):
            sort_block(4 * p + 2, sorted_c)
            copy_any(p, 0, sorted_a)
            sort_block(4 * p + 3, sorted_d)
            copy_any(p, 1, sorted_b)
            sort_block(jnp.minimum(4 * p + 4, NBLK - 1), sorted_a)
            copy_any(p, 2, sorted_c)
            sort_block(jnp.minimum(4 * p + 5, NBLK - 1), sorted_b)
            copy_any(p, 3, sorted_d)

    pl.when(short)(lambda: quad(copy_short))
    pl.when(jnp.logical_not(short))(lambda: quad(copy_block))

    low_lanes = iota((HALF, 128), 1) < 64
    r8, l8 = iota((8, 128), 0), iota((8, 128), 1)
    pick = jnp.where((r8 == 0) & (l8 == 64), one, nil)
    pick = jnp.where((r8 == 1) & (l8 == 65), one, pick)
    pick = jnp.where((r8 == 1) & (l8 == 66), 4.0 * one, pick)
    pick = jnp.where((r8 == 2) & (l8 == 67), one, pick)
    pick = jnp.where((r8 == 2) & (l8 == 68), 256.0 * one, pick)
    pick = pick.astype(BF16)
    rank = iota((8, MSG), 1)
    rank_row = iota((8, MSG), 0)
    lane_dest = iota((8, BLK), 1)

    def send(g):
        part = pl.ds(g * GROUP, GROUP)
        return pltpu.make_async_copy(pack_v.at[part], rows_ref.at[part], pack_sem.at[g])

    def pack(g):
        for k in range(GROUP):
            d = GROUP * g + k
            at = pl.multiple_of(d * STRIDE, 8)
            lo = bucket[pl.ds(at, HALF)]
            hi = bucket[pl.ds(pl.multiple_of(at + HALF, 8), HALF)]
            pack_v[d, 0:HALF] = jnp.where(low_lanes, lo, pltpu.roll(hi, 64, 1))
            meta_v[d] = jnp.where(low_lanes, pltpu.roll(lo, 64, 1), hi).astype(BF16)
            both = jnp.concatenate([lo, hi], axis=0).astype(BF16)
            nums = dot_nt(pick, both)
            mine = jnp.max(jnp.where(lane_dest == d, total, nil), axis=1, keepdims=True)
            valid = rank.astype(F32) < mine
            nums = jnp.where((rank_row == 2) & ~valid, float(OWN), nums)
            nums = jnp.where(rank_row == 3, jnp.where(valid, one, nil), nums)
            lanes_ref[d] = nums
            pack_v[d, HALF : HALF + 4] = jnp.concatenate(
                [nums[2:3, 128 * q : 128 * q + 128] for q in range(4)], axis=0
            )

    cells = field_ref[...].reshape(ROWS // 4, 4, 128)
    parts = [split(cells[:, q]) for q in range(4)]
    table[...] = jnp.concatenate([p[0] for p in parts] + [p[1] for p in parts], axis=1)
    m_rows = GROUP * HALF
    ones8 = jnp.ones((8, 256), BF16)
    place = iota((m_rows, 128), 1).astype(F32)

    def far(g):
        meta = meta_v[pl.ds(g * GROUP, GROUP)].reshape(m_rows, 128).astype(F32)
        for h in range(2):
            first = 0 if h == 0 else 64
            col = meta[:, first : first + 1] + 128.0 * meta[:, first + 1 : first + 2]
            col = jnp.broadcast_to(col, (m_rows, 128))
            row = jnp.broadcast_to(meta[:, first + 2 : first + 3], (m_rows, 128))
            hot = jnp.concatenate(
                [jnp.where(row == place + 128.0 * q, one, nil).astype(BF16) for q in range(2)], axis=1
            )
            val = dot(hot, table[...])
            got = jnp.zeros((m_rows, 128), F32)
            for q in range(4):
                both = val[:, 128 * q : 128 * q + 128] + val[:, 512 + 128 * q : 640 + 128 * q]
                got = jnp.where(col == place + 128.0 * q, both, got)
            v0, v1 = split(got)
            far_l = dot_nt(ones8, jnp.concatenate([v0, v1], axis=1))
            for i in range(GROUP):
                for q in range(2):
                    at = HALF * i + 128 * q
                    row_at = HALF + 4 + 2 * h + q
                    pack_v[GROUP * g + i, row_at : row_at + 1] = far_l[0:1, at : at + 128]

    pack(0)

    @pl.loop(0, NT // GROUP - 1)
    def _(g):
        far(g)
        pack(g + 1)
        send(g).start()

    far(NT // GROUP - 1)
    send(NT // GROUP - 1).start()
    pick = jnp.where((r8 == 0) & (l8 == 0), one, nil) + jnp.where((r8 == 1) & (l8 == 127), one, nil)
    pick = pick.astype(BF16)
    f0, f1 = split(field_ref[...])
    f2 = (field_ref[...] - f0.astype(F32) - f1.astype(F32)).astype(BF16)
    ends_ref[...] = dot_nt(pick, f0) + dot_nt(pick, f1) + dot_nt(pick, f2)
    for g in range(NT // GROUP):
        send(g).wait()


def route(counts, owners, cells, field, profiles):
    vmem = pl.BlockSpec(memory_space=pltpu.VMEM)
    anywhere = pl.BlockSpec(memory_space=pl.ANY)
    return pl.pallas_call(
        route_kernel,
        out_shape=(
            jax.ShapeDtypeStruct((NT, LOAD, 128), F32),
            jax.ShapeDtypeStruct((NT, 8, MSG), F32),
            jax.ShapeDtypeStruct((8, ROWS), F32),
        ),
        in_specs=[pl.BlockSpec(memory_space=pltpu.SMEM), vmem, vmem, vmem, anywhere],
        out_specs=(anywhere, vmem, vmem),
        scratch_shapes=[pltpu.VMEM((NBLK, BLK), F32)] * 6
        + [pltpu.VMEM((BLK + 16, 128), F32)] * 4
        + [
            pltpu.VMEM((NT * STRIDE, 128), F32),
            pltpu.VMEM((128, 128), I32),
            pltpu.SMEM((128, 128), I32),
            pltpu.SemaphoreType.DMA,
            pltpu.VMEM((PTS, CAP), F32),
            pltpu.SemaphoreType.DMA,
            pltpu.VMEM((NT, LOAD, 128), F32),
            pltpu.SemaphoreType.DMA((NT // GROUP,)),
            pltpu.VMEM((NT, HALF, 128), BF16),
            pltpu.VMEM((ROWS // 4, 1024), BF16),
        ],
        compiler_params=pltpu.CompilerParams(vmem_limit_bytes=ROOM),
        name="route",
    )(counts, owners.reshape(128, 128), cells.reshape(128, 128), field, profiles)


def step_weights(radial_step):
    zero = jnp.zeros((PTS, PTS), F32)
    w = jnp.concatenate(
        [
            jnp.concatenate([radial_step.T, zero], axis=1),
            jnp.concatenate([zero, radial_step.T], axis=1),
        ],
        axis=0,
    )
    high = lax.reduce_precision(w, 8, 7)
    w0, w1 = high.astype(BF16), (w - high).astype(BF16)
    row = jnp.concatenate([w0, w1], axis=1)
    return jnp.concatenate([row, row], axis=0)


def flux_rows(flux_weights):
    zero = jnp.zeros((PTS,), F32)
    f = jnp.stack(
        [jnp.concatenate([flux_weights, zero]), jnp.concatenate([zero, flux_weights])]
        + [jnp.zeros((128,), F32)] * 6
    )
    return f / SUB


def substep(state, add, weights):
    s0, s1 = split(state)
    got = dot(jnp.concatenate([s0, s1], axis=1), weights)
    return (got[:, :128] + got[:, 128:]) + (add + 0.25 * jnp.tanh(state))


HEAT_N = 8


def far_columns(side):
    far = jnp.concatenate([side[4 + q : 5 + q] for q in range(4)], axis=1)
    rest = far - far.astype(BF16).astype(F32)
    row8 = iota((8, MSG), 0)
    terms = jnp.where(row8 == 0, far, jnp.where(row8 == 1, rest, 0.0)).astype(BF16)
    pick = jnp.where(iota((8, 128), 0) < 2, 1.0, 0.0).astype(BF16)
    return lax.dot_general(terms, pick, (((0,), (0,)), ((), ())), preferred_element_type=F32)


def heat_kernel(rows_ref, side_ref, fw_ref, weights_ref, flux_ref, heat_ref):
    weights = weights_ref[...]
    state = rows_ref[...].reshape(HEAT_N * HALF, 128)
    low_lanes = iota((HALF, 128), 1) < 64
    adds = []
    for i in range(HEAT_N):
        far = far_columns(side_ref[i])
        adds.append(fw_ref[...] * jnp.where(low_lanes, far[:HALF], far[HALF:]))
    add = jnp.concatenate(adds, axis=0)
    total = jnp.zeros_like(state)
    for _ in range(SUB):
        state = substep(state, add, weights)
        total = total + state
    t0, t1 = split(total)
    f0, f1 = split(flux_ref[...])
    heat = dot_nt(f0, t0) + dot_nt(f0, t1) + dot_nt(f1, t0)
    for i in range(HEAT_N):
        heat_ref[i] = heat[:, HALF * i : HALF * i + HALF]


def home_heat(rows, fw, weights, flux):
    steps = NT // HEAT_N
    return pl.pallas_call(
        heat_kernel,
        grid=(steps,),
        out_shape=jax.ShapeDtypeStruct((steps * HEAT_N, 8, HALF), F32),
        in_specs=[
            pl.BlockSpec((HEAT_N, HALF, 128), lambda d: (d, 0, 0)),
            pl.BlockSpec((HEAT_N, 8, 128), lambda d: (d, HALF // 8, 0)),
            pl.BlockSpec((1, 128), lambda d: (0, 0)),
            pl.BlockSpec((256, 256), lambda d: (0, 0)),
            pl.BlockSpec((8, 128), lambda d: (0, 0)),
        ],
        out_specs=pl.BlockSpec((HEAT_N, 8, HALF), lambda d: (d, 0, 0)),
        compiler_params=pltpu.CompilerParams(vmem_limit_bytes=ROOM),
        cost_estimate=pl.CostEstimate(
            flops=25 * 10**8 * steps, bytes_accessed=steps << 20, transcendentals=steps << 21
        ),
        name="home_heat",
    )(rows, rows, fw, weights, flux)


DEP_N = GROUP


def deposit_kernel(
    lanes_ref, heat_ref, cells_ref, vel_ref, dif_ref, flux_ref, below_ref, above_ref,
    out_ref, acc,
):
    d = pl.program_id(0)

    @pl.when(d == 0)
    def _():
        acc[...] = jnp.zeros_like(acc)

    one, nil = jnp.ones((), F32), jnp.zeros((), F32)
    width = DEP_N * MSG
    cols, rows, heats = [], [], []
    for i in range(DEP_N):
        nums = lanes_ref[i]
        heat = jnp.concatenate([heat_ref[i, 0:1], heat_ref[i, 1:2]], axis=1)
        cols.append(nums[0:1])
        rows.append(nums[1:2])
        heats.append(jnp.where(nums[3:4] > 0.5, 0.5 * heat, nil))
    col = jnp.concatenate(cols, axis=1).astype(I32)
    row = jnp.concatenate(rows, axis=1).astype(I32)
    heat = jnp.concatenate(heats, axis=1)
    high = heat.astype(BF16).astype(F32)
    here = col == iota((128, width), 0)
    spread = jnp.concatenate(
        [jnp.where(here, high, nil).astype(BF16), jnp.where(here, heat - high, nil).astype(BF16)], axis=0
    )
    hot = jnp.where(row == iota((ROWS, width), 0), one, nil).astype(BF16)
    acc[...] += dot_nt(hot, spread)

    @pl.when(d == NT // DEP_N - 1)
    def _():
        layers = ROWS // 64
        wall, lane = iota((64, 128), 0), iota((64, 128), 1)
        for x in range(layers):
            at = 64 * x
            h = cells_ref[at : at + 64]
            x_lower = cells_ref[at - 64 : at] if x else below_ref[...]
            x_upper = cells_ref[at + 64 : at + 128] if x < layers - 1 else above_ref[...]
            w_lower = jnp.where(wall == 0, h, pltpu.roll(h, 1, 0))
            w_upper = jnp.where(wall == 63, h, pltpu.roll(h, 63, 0))
            s_lower = jnp.where(lane == 0, nil, pltpu.roll(h, 1, 1))
            s_upper = jnp.where(lane == 127, nil, pltpu.roll(h, 127, 1))
            laplace = (x_lower + x_upper) + (w_lower + w_upper) + (s_lower + s_upper) - 6.0 * h
            new = h + dif_ref[at : at + 64] * laplace - vel_ref[at : at + 64] * (h - x_lower)
            new = new + jnp.where(wall == 0, flux_ref[x : x + 1], nil)
            out_ref[at : at + 64] = new + (acc[at : at + 64, :128] + acc[at : at + 64, 128:])


def deposit(lanes, heat, cells, velocity, diffusivity, wall_flux, below, above):
    def whole(shape):
        return pl.BlockSpec(shape, lambda d: (0, 0))

    field = whole((ROWS, 128))
    return pl.pallas_call(
        deposit_kernel,
        grid=(NT // DEP_N,),
        out_shape=jax.ShapeDtypeStruct((ROWS, 128), F32),
        in_specs=[
            pl.BlockSpec((DEP_N, 8, MSG), lambda d: (d, 0, 0)),
            pl.BlockSpec((DEP_N, 8, HALF), lambda d: (d, 0, 0)),
            field,
            field,
            field,
            whole((ROWS // 64, 128)),
            whole((64, 128)),
            whole((64, 128)),
        ],
        out_specs=field,
        scratch_shapes=[pltpu.VMEM((ROWS, 256), F32)],
        compiler_params=pltpu.CompilerParams(vmem_limit_bytes=40 * 2**20),
        cost_estimate=pl.CostEstimate(flops=10**10, bytes_accessed=4 << 20, transcendentals=0),
        name="deposit",
    )(lanes, heat, cells, velocity, diffusivity, wall_flux, below, above)


def span_kernel(new_ref, dif_ref, left_ref, right_ref, out_ref):
    row8, lane = iota((8, ROWS), 0), iota((8, 128), 1)
    terms = jnp.zeros((8, ROWS), F32)
    for i, ref in enumerate((left_ref, right_ref)):
        rest = ref[...]
        for k in range(3):
            high = rest.astype(BF16).astype(F32)
            terms = jnp.where(row8 == 3 * i + k, high, terms)
            rest = rest - high
    row = iota((8, 128), 0)
    first, last = (row < 3) & (lane == 0), (row >= 3) & (row < 6) & (lane == 127)
    pick = jnp.where(first | last, 1.0, 0.0).astype(BF16)
    ends = lax.dot_general(terms.astype(BF16), pick, (((0,), (0,)), ((), ())), preferred_element_type=F32)
    out_ref[...] = new_ref[...] + dif_ref[...] * ends


def add_span(new, diffusivity, left, right):
    vmem = pl.BlockSpec(memory_space=pltpu.VMEM)
    return pl.pallas_call(
        span_kernel,
        out_shape=jax.ShapeDtypeStruct((ROWS, 128), F32),
        in_specs=[vmem] * 4,
        out_specs=vmem,
        cost_estimate=pl.CostEstimate(flops=10**7, bytes_accessed=2 << 20, transcendentals=0),
        name="span",
    )(new, diffusivity, left, right)


SETTLE = 1024


def settle_kernel(
    rows_ref, fw_ref, weights_ref, out_ref,
    stage, comb, got, got_sem, side, side_sem, slot_v, slot_s, slot_sem, amount_v, amount_s, amount_sem,
    out_v, out_sem,
):
    fetch_side = pltpu.make_async_copy(rows_ref.at[:, pl.ds(HALF, 8)], side, side_sem)
    fetch_side.start()

    def fetch(g):
        part = pl.ds(g * GROUP, GROUP)
        return pltpu.make_async_copy(rows_ref.at[part, pl.ds(0, HALF)], got.at[part], got_sem.at[g])

    for g in range(NT // GROUP):
        fetch(g).start()
    fetch_side.wait()
    for t in range(NT):
        slot_v[4 * t : 4 * t + 4] = side[t, 0:4].astype(I32)
    valid = jnp.where(slot_v[...] < OWN, 1.0, 0.0).astype(BF16)
    by_row = dot(valid, jnp.ones((128, 128), BF16)).astype(BF16)
    of_sender = jnp.where(iota((NT, 128), 1) >> 2 == iota((NT, 128), 0), 1.0, 0.0).astype(BF16)
    amount_v[...] = dot(of_sender, by_row).astype(I32)
    copies = (
        pltpu.make_async_copy(slot_v, slot_s, slot_sem),
        pltpu.make_async_copy(amount_v, amount_s, amount_sem),
    )
    for copy in copies:
        copy.start()

    low_lanes = iota((HALF, 128), 1) < 64

    for g in range(NT // GROUP):
        fetch(g).wait()

    @pl.loop(0, NT // GROUP, unroll=2)
    def _(g):
        for k in range(GROUP):
            t = GROUP * g + k
            rows = got[t]
            col = far_columns(side[t])
            at = pl.multiple_of(t * MSG, MSG)
            comb[pl.ds(at, HALF)] = jnp.where(low_lanes, rows, col[:HALF])
            comb[pl.ds(pl.multiple_of(at + HALF, HALF), HALF)] = jnp.where(
                low_lanes, pltpu.roll(rows, 64, 1), col[HALF:]
            )

    for copy in copies:
        copy.wait()

    @pl.loop(0, NT)
    def _(t):
        amount = amount_s[t, 0]

        def move(r, lanes):
            row = 4 * t + r
            for lane in lanes:
                stage[pl.ds(slot_s[row, lane], 1)] = comb[pl.ds(row * 128 + lane, 1)]

        @pl.loop(0, amount >> 7)
        def _(r):
            move(r, range(128))

        last = amount >> 7
        for lane in range(0, 128, 32):

            @pl.when((amount & 127) > lane)
            def _():
                move(last, range(lane, lane + 32))

    weights = weights_ref[...]
    fw = fw_ref[...]
    low_lanes = iota((SETTLE, 128), 1) < 64

    def send(c, h):
        part = pl.ds(c * SETTLE + h * OWN2, SETTLE)
        return pltpu.make_async_copy(out_v.at[:, part], out_ref.at[:, part], out_sem.at[2 * c + h])

    for c in range(OWN2 // SETTLE):
        at = c * SETTLE
        a = stage[at : at + SETTLE]
        b = stage[at + OWN2 : at + OWN2 + SETTLE]
        state = jnp.where(low_lanes, a, pltpu.roll(b, 64, 1))
        add = fw * jnp.where(low_lanes, pltpu.roll(a, 64, 1), b)
        for _ in range(SUB):
            state = substep(state, add, weights)
        for k in range(SETTLE // 128):
            turned = state[128 * k : 128 * k + 128].T
            out_v[:, at + 128 * k : at + 128 * k + 128] = turned[:64]
            out_v[:, at + OWN2 + 128 * k : at + OWN2 + 128 * k + 128] = turned[64:]
        for h in range(2):
            send(c, h).start()
    for c in range(OWN2 // SETTLE):
        for h in range(2):
            send(c, h).wait()


def settle(rows, fw, weights):
    vmem = pl.BlockSpec(memory_space=pltpu.VMEM)
    return pl.pallas_call(
        settle_kernel,
        out_shape=jax.ShapeDtypeStruct((PTS, OWN), F32),
        in_specs=[pl.BlockSpec(memory_space=pl.ANY), vmem, vmem],
        out_specs=pl.BlockSpec(memory_space=pl.ANY),
        scratch_shapes=[
            pltpu.VMEM((OWN + 8, 128), F32),
            pltpu.VMEM((NT * MSG, 128), F32),
            pltpu.VMEM((NT, HALF, 128), F32),
            pltpu.SemaphoreType.DMA((NT // GROUP,)),
            pltpu.VMEM((NT, 8, 128), F32),
            pltpu.SemaphoreType.DMA,
            pltpu.VMEM((128, 128), I32),
            pltpu.SMEM((128, 128), I32),
            pltpu.SemaphoreType.DMA,
            pltpu.VMEM((NT, 128), I32),
            pltpu.SMEM((NT, 128), I32),
            pltpu.SemaphoreType.DMA,
            pltpu.VMEM((PTS, OWN), F32),
            pltpu.SemaphoreType.DMA((2 * OWN2 // SETTLE,)),
        ],
        compiler_params=pltpu.CompilerParams(vmem_limit_bytes=ROOM),
        name="settle",
    )(rows, fw, weights)


def edges_of(cells, ends):
    n_x, n_s = lax.axis_size("stream"), lax.axis_size("tile")
    up_x = [(i, i + 1) for i in range(n_x - 1)]
    down_x = [(i + 1, i) for i in range(n_x - 1)]
    up_s = [(i, (i + 1) % n_s) for i in range(n_s)]
    down_s = [((i + 1) % n_s, i) for i in range(n_s)]
    below = lax.ppermute(cells[-1], "stream", up_x)
    above = lax.ppermute(cells[0], "stream", down_x)
    left = lax.ppermute(ends[1:2], "tile", up_s)
    right = lax.ppermute(ends[0:1], "tile", down_s)
    return below, above, left, right


def on_device(
    enthalpy, velocity, diffusivity, wall_flux, profiles, counts, owners, cells,
    radial_step, far_weights, flux_weights,
):
    table = enthalpy.reshape(ROWS, 128)
    rows, lanes, ends = route(counts, owners, cells, table, profiles)
    rows, radial_step, far_weights, flux_weights = lax.optimization_barrier(
        (rows, radial_step, far_weights, flux_weights)
    )
    weights = step_weights(radial_step)
    fw = jnp.concatenate([far_weights, far_weights])[None, :]
    flux = flux_rows(flux_weights)
    got = lax.all_to_all(rows, "tile", split_axis=0, concat_axis=0, tiled=True)
    layers, ends = lax.optimization_barrier((enthalpy, ends))
    heat = home_heat(rows, fw, weights, flux)
    below, above, left, right = edges_of(layers, ends)
    spread = diffusivity.reshape(ROWS, 128)
    new = deposit(lanes, heat, table, velocity.reshape(ROWS, 128), spread, wall_flux, below, above)
    new_enthalpy = add_span(new, spread, left, right).reshape(enthalpy.shape)
    new_profiles = settle(got, fw, weights)
    return new_enthalpy, new_profiles


def solution(mesh):
    return jax.shard_map(
        on_device,
        mesh=mesh,
        in_specs=(
            P("stream", None, "tile"),
            P("stream", None, "tile"),
            P("stream", None, "tile"),
            P("stream", "tile"),
            P(None, ("stream", "tile")),
            P(("stream", "tile")),
            P(("stream", "tile")),
            P(("stream", "tile")),
            P(),
            P(),
            P(),
        ),
        out_specs=(P("stream", None, "tile"), P(None, ("stream", "tile"))),
        check_vma=False,
    )
```

```python
import jax
import jax.numpy as jnp
from jax import lax
from jax.experimental import pallas as pl
from jax.experimental.pallas import tpu as pltpu
from jax.sharding import PartitionSpec as P

SUB = 16
PTS = 64
NT = 32
CAP = 16384
OWN = 6144
MSG = 512
HALF = MSG // 2
LOAD = HALF + 8
BLK = 256
NBLK = CAP // BLK
STRIDE = MSG + 16
ROWS = 1024
OWN2 = OWN // 2

GROUP = 4
ROOM = 60 * 2**20

F32, BF16, I32 = jnp.float32, jnp.bfloat16, jnp.int32
NTD = (((1,), (1,)), ((), ()))


def iota(shape, dim):
    return lax.broadcasted_iota(I32, shape, dim)


def split(x):
    high = x.astype(BF16)
    return high, (x - high.astype(F32)).astype(BF16)


def dot(a, b):
    return jnp.dot(a, b, preferred_element_type=F32)


def dot_nt(a, b):
    return lax.dot_general(a, b, NTD, preferred_element_type=F32)


def route_kernel(
    count_ref, owners_ref, cells_ref, field_ref, prof_ref,
    rows_ref, lanes_ref, first_ref, last_ref,
    pos_s, m0_s, m1_s, m2_s, m3_s, m4_s, sorted_a, sorted_b, sorted_c, sorted_d,
    bucket, tab_v, tab_s, sem, prof_v, prof_sem, pack_v, pack_sem, meta_v, table,
):
    count = count_ref[0]
    fetch = pltpu.make_async_copy(prof_ref, prof_v, prof_sem)
    fetch.start()

    def blocks(ref):
        x = ref[...].reshape(NBLK, 2, 128)
        return jnp.concatenate([x[:, 0], x[:, 1]], axis=1)

    slot = iota((NBLK, BLK), 0) * BLK + iota((NBLK, BLK), 1)
    owners = blocks(owners_ref)
    dest = jnp.floor((owners.astype(F32) + 0.5) * (1.0 / OWN)).astype(I32)
    within = owners - dest * OWN
    live = slot < count
    dest = jnp.where(live, dest, NT)
    cells = blocks(cells_ref)
    m0_s[...] = (cells & 127).astype(F32)
    m1_s[...] = ((cells >> 7) & 3).astype(F32)
    m2_s[...] = (cells >> 9).astype(F32)
    m3_s[...] = (within & 255).astype(F32)
    m4_s[...] = (within >> 8).astype(F32)

    sub, lane = iota((BLK, BLK), 0), iota((BLK, BLK), 1)
    one, nil = jnp.ones((), F32), jnp.zeros((), F32)
    before = jnp.where(sub < lane, one, nil).astype(BF16)
    same_block = (sub >> 5) == (lane >> 5)
    same_dest = (sub & 31) == (lane & 31)
    seg_left = jnp.where(same_block & (lane < sub), one, nil).astype(BF16)
    seg_right = jnp.where(same_block & (sub < lane), one, nil).astype(BF16)
    base_right = jnp.where(same_dest & ((sub >> 5) < (lane >> 5)), one, nil).astype(BF16)
    all_right = jnp.where(same_dest, one, nil).astype(BF16)
    ones_a = jnp.ones((8, BLK), BF16)
    ones_b = jnp.ones((BLK, 128), BF16)
    run = jnp.zeros((8, BLK), F32)
    longest = jnp.zeros((8, BLK), F32)
    for c in range(8):
        part = dest[8 * c : 8 * c + 8]
        hot = jnp.where(part[:, None, :] == iota((8, NT, BLK), 1), one, nil).reshape(BLK, BLK)
        hot_b = hot.astype(BF16)
        prefix = dot(hot_b, before)
        amount = dot(hot_b, ones_b)
        seg = dot(seg_left, amount.astype(BF16))
        seg2 = jnp.concatenate([seg, seg], axis=1)
        pos = jnp.sum((hot * (prefix + seg2)).reshape(8, NT, BLK), axis=1)
        pos_s[8 * c : 8 * c + 8] = jnp.where(live[8 * c : 8 * c + 8], pos, 511.0)
        amount_l = dot_nt(ones_a, hot_b)
        amount_lb = amount_l.astype(BF16)
        src = dot(amount_lb, seg_right)
        base = dot(amount_lb, base_right) + run
        run = run + dot(amount_lb, all_right)
        longest = jnp.maximum(longest, amount_l)
        most = amount_l
        for shift in (1, 2, 4, 8, 16):
            most = jnp.maximum(most, pltpu.roll(most, BLK - shift, 1))
        first = iota((8, BLK), 1) & 31
        row8 = iota((8, BLK), 0)
        packed = jnp.where(row8 == 0, src, nil)
        packed = jnp.where(row8 == 1, base + (first * STRIDE).astype(F32), packed)
        packed = jnp.where(row8 == 2, amount_l, packed)
        packed = jnp.where(row8 == 3, most, packed)
        packed = packed.astype(I32)
        tab_v[16 * c : 16 * c + 8] = packed[:, :128]
        tab_v[16 * c + 8 : 16 * c + 16] = packed[:, 128:]
    copy = pltpu.make_async_copy(tab_v, tab_s, sem)
    copy.start()
    short = jnp.max(longest) <= 8.0
    total = run

    zero8 = jnp.zeros((STRIDE, 128), F32)

    @pl.loop(0, NT)
    def _(d):
        bucket[pl.ds(pl.multiple_of(d * STRIDE, 8), STRIDE)] = zero8

    copy.wait()
    fetch.wait()

    meta_rest = jnp.zeros((56, BLK), BF16)
    low_rest = jnp.zeros((64, BLK), BF16)
    row8 = iota((8, BLK), 0)

    def sort_block(j, out):
        x = prof_v[:, pl.ds(pl.multiple_of(j * BLK, BLK), BLK)]
        high, low = split(x)
        meta = jnp.zeros((8, BLK), F32)
        for k, ref in enumerate((m0_s, m1_s, m2_s, m3_s, m4_s)):
            meta = jnp.where(row8 == k, ref[pl.ds(j, 1), :], meta)
        data = jnp.concatenate([high, meta.astype(BF16), meta_rest, low, low_rest], axis=0)
        place = pos_s[pl.ds(j, 1), :].astype(I32)
        perm = jnp.where(place == sub, one, nil).astype(BF16)
        got = dot_nt(perm, data)
        out[0:BLK] = got[:, :128] + got[:, 128:]

    def copy_block(p, c, inp):
        chunk, at = p * 8, c * NT
        most = tab_s[chunk + 3, at]

        @pl.when(most <= 8)
        def _():
            for d in range(NT):
                src = tab_s[chunk, at + d]
                dst = tab_s[chunk + 1, at + d]
                bucket[pl.ds(dst, 8)] = inp[pl.ds(src, 8)]

        @pl.when((most > 8) & (most <= 16))
        def _():
            for d in range(NT):
                src = tab_s[chunk, at + d]
                dst = tab_s[chunk + 1, at + d]
                bucket[pl.ds(dst, 16)] = inp[pl.ds(src, 16)]

        @pl.when(most > 16)
        def _():
            @pl.loop(0, NT)
            def _(d):
                src = tab_s[chunk, at + d]
                dst = tab_s[chunk + 1, at + d]

                @pl.loop(0, (tab_s[chunk + 2, at + d] + 7) >> 3)
                def _(k):
                    bucket[pl.ds(dst + 8 * k, 8)] = inp[pl.ds(src + 8 * k, 8)]

    def copy_short(p, c, inp):
        chunk, at = p * 8, c * NT
        for d in range(NT):
            src = tab_s[chunk, at + d]
            dst = tab_s[chunk + 1, at + d]
            bucket[pl.ds(dst, 8)] = inp[pl.ds(src, 8)]

    for ref in (sorted_a, sorted_b, sorted_c, sorted_d):
        ref[BLK:] = jnp.zeros((16, 128), F32)
    quads = (count + 4 * BLK - 1) // (4 * BLK)
    sort_block(0, sorted_a)
    sort_block(1, sorted_b)

    def quad(copy_any):
        @pl.loop(0, quads)
        def _(p):
            sort_block(4 * p + 2, sorted_c)
            copy_any(p, 0, sorted_a)
            sort_block(4 * p + 3, sorted_d)
            copy_any(p, 1, sorted_b)
            sort_block(jnp.minimum(4 * p + 4, NBLK - 1), sorted_a)
            copy_any(p, 2, sorted_c)
            sort_block(jnp.minimum(4 * p + 5, NBLK - 1), sorted_b)
            copy_any(p, 3, sorted_d)

    pl.when(short)(lambda: quad(copy_short))
    pl.when(jnp.logical_not(short))(lambda: quad(copy_block))

    low_lanes = iota((HALF, 128), 1) < 64
    r8, l8 = iota((8, 128), 0), iota((8, 128), 1)
    pick = jnp.where((r8 == 0) & (l8 == 64), one, nil)
    pick = jnp.where((r8 == 1) & (l8 == 65), one, pick)
    pick = jnp.where((r8 == 1) & (l8 == 66), 4.0 * one, pick)
    pick = jnp.where((r8 == 2) & (l8 == 67), one, pick)
    pick = jnp.where((r8 == 2) & (l8 == 68), 256.0 * one, pick)
    pick = pick.astype(BF16)
    rank = iota((8, MSG), 1)
    rank_row = iota((8, MSG), 0)
    lane_dest = iota((8, BLK), 1)

    def send(g):
        part = pl.ds(g * GROUP, GROUP)
        return pltpu.make_async_copy(pack_v.at[part], rows_ref.at[part], pack_sem.at[g])

    def pack(g):
        for k in range(GROUP):
            d = GROUP * g + k
            at = pl.multiple_of(d * STRIDE, 8)
            lo = bucket[pl.ds(at, HALF)]
            hi = bucket[pl.ds(pl.multiple_of(at + HALF, 8), HALF)]
            pack_v[d, 0:HALF] = jnp.where(low_lanes, lo, pltpu.roll(hi, 64, 1))
            meta_v[d] = jnp.where(low_lanes, pltpu.roll(lo, 64, 1), hi).astype(BF16)
            both = jnp.concatenate([lo, hi], axis=0).astype(BF16)
            nums = dot_nt(pick, both)
            mine = jnp.max(jnp.where(lane_dest == d, total, nil), axis=1, keepdims=True)
            valid = rank.astype(F32) < mine
            nums = jnp.where((rank_row == 2) & ~valid, float(OWN), nums)
            nums = jnp.where(rank_row == 3, jnp.where(valid, one, nil), nums)
            lanes_ref[d] = nums
            pack_v[d, HALF : HALF + 4] = jnp.concatenate(
                [nums[2:3, 128 * q : 128 * q + 128] for q in range(4)], axis=0
            )

    cells = field_ref[...].reshape(ROWS // 4, 4, 128)
    parts = [split(cells[:, q]) for q in range(4)]
    table[...] = jnp.concatenate([p[0] for p in parts] + [p[1] for p in parts], axis=1)
    m_rows = GROUP * HALF
    ones8 = jnp.ones((8, 256), BF16)
    place = iota((m_rows, 128), 1).astype(F32)

    def far(g):
        meta = meta_v[pl.ds(g * GROUP, GROUP)].reshape(m_rows, 128).astype(F32)
        for h in range(2):
            first = 0 if h == 0 else 64
            col = meta[:, first : first + 1] + 128.0 * meta[:, first + 1 : first + 2]
            col = jnp.broadcast_to(col, (m_rows, 128))
            row = jnp.broadcast_to(meta[:, first + 2 : first + 3], (m_rows, 128))
            hot = jnp.concatenate(
                [jnp.where(row == place + 128.0 * q, one, nil).astype(BF16) for q in range(2)], axis=1
            )
            val = dot(hot, table[...])
            got = jnp.zeros((m_rows, 128), F32)
            for q in range(4):
                both = val[:, 128 * q : 128 * q + 128] + val[:, 512 + 128 * q : 640 + 128 * q]
                got = jnp.where(col == place + 128.0 * q, both, got)
            v0, v1 = split(got)
            far_l = dot_nt(ones8, jnp.concatenate([v0, v1], axis=1))
            for i in range(GROUP):
                for q in range(2):
                    at = HALF * i + 128 * q
                    row_at = HALF + 4 + 2 * h + q
                    pack_v[GROUP * g + i, row_at : row_at + 1] = far_l[0:1, at : at + 128]

    pack(0)

    @pl.loop(0, NT // GROUP - 1)
    def _(g):
        far(g)
        pack(g + 1)
        send(g).start()

    far(NT // GROUP - 1)
    send(NT // GROUP - 1).start()
    pick = jnp.where((r8 == 0) & (l8 == 0), one, nil) + jnp.where((r8 == 1) & (l8 == 127), one, nil)
    pick = pick.astype(BF16)
    f0, f1 = split(field_ref[...])
    f2 = (field_ref[...] - f0.astype(F32) - f1.astype(F32)).astype(BF16)
    ends = dot_nt(pick, f0) + dot_nt(pick, f1) + dot_nt(pick, f2)
    first_ref[...] = ends[0:1]
    last_ref[...] = ends[1:2]
    for g in range(NT // GROUP):
        send(g).wait()


def route(counts, owners, cells, field, profiles):
    vmem = pl.BlockSpec(memory_space=pltpu.VMEM)
    anywhere = pl.BlockSpec(memory_space=pl.ANY)
    return pl.pallas_call(
        route_kernel,
        out_shape=(
            jax.ShapeDtypeStruct((NT, LOAD, 128), F32),
            jax.ShapeDtypeStruct((NT, 8, MSG), F32),
            jax.ShapeDtypeStruct((1, ROWS), F32),
            jax.ShapeDtypeStruct((1, ROWS), F32),
        ),
        in_specs=[pl.BlockSpec(memory_space=pltpu.SMEM), vmem, vmem, vmem, anywhere],
        out_specs=(anywhere, vmem, vmem, vmem),
        scratch_shapes=[pltpu.VMEM((NBLK, BLK), F32)] * 6
        + [pltpu.VMEM((BLK + 16, 128), F32)] * 4
        + [
            pltpu.VMEM((NT * STRIDE, 128), F32),
            pltpu.VMEM((128, 128), I32),
            pltpu.SMEM((128, 128), I32),
            pltpu.SemaphoreType.DMA,
            pltpu.VMEM((PTS, CAP), F32),
            pltpu.SemaphoreType.DMA,
            pltpu.VMEM((NT, LOAD, 128), F32),
            pltpu.SemaphoreType.DMA((NT // GROUP,)),
            pltpu.VMEM((NT, HALF, 128), BF16),
            pltpu.VMEM((ROWS // 4, 1024), BF16),
        ],
        compiler_params=pltpu.CompilerParams(vmem_limit_bytes=ROOM),
        name="route",
    )(counts, owners.reshape(128, 128), cells.reshape(128, 128), field, profiles)


def twice(row):
    return jnp.concatenate([row, row], axis=1)


def step_weights(radial_step):
    w0, w1 = split(radial_step.T)
    w0, w1 = w0.astype(F32), w1.astype(F32)
    nil = jnp.zeros((PTS, PTS), F32)
    half = jnp.concatenate(
        [
            jnp.concatenate([w0, nil, w1, nil], axis=1),
            jnp.concatenate([nil, w0, nil, w1], axis=1),
        ],
        axis=0,
    ).astype(BF16)
    return jnp.concatenate([half, half], axis=0)


def flux_rows(flux_weights):
    row, low = iota((8, 128), 0), iota((8, 128), 1) < 64
    mine = ((row == 0) & low) | ((row == 1) & jnp.logical_not(low))
    return jnp.where(mine, twice(flux_weights) / SUB, 0.0)


def substep(state, add, weights):
    s0, s1 = split(state)
    got = dot(jnp.concatenate([s0, s1], axis=1), weights)
    return (got[:, :128] + got[:, 128:]) + (add + 0.25 * jnp.tanh(state))


HEAT_N = 8


def far_columns(side):
    far = jnp.concatenate([side[4 + q : 5 + q] for q in range(4)], axis=1)
    rest = far - far.astype(BF16).astype(F32)
    row8 = iota((8, MSG), 0)
    terms = jnp.where(row8 == 0, far, jnp.where(row8 == 1, rest, 0.0)).astype(BF16)
    pick = jnp.where(iota((8, 128), 0) < 2, 1.0, 0.0).astype(BF16)
    return lax.dot_general(terms, pick, (((0,), (0,)), ((), ())), preferred_element_type=F32)


def heat_kernel(rows_ref, side_ref, radial_ref, fw_ref, flux_ref, heat_ref, weights_ref):
    @pl.when(pl.program_id(0) == 0)
    def _():
        weights_ref[...] = step_weights(radial_ref[...])

    weights = weights_ref[...]
    fw = twice(fw_ref[...])
    state = rows_ref[...].reshape(HEAT_N * HALF, 128)
    low_lanes = iota((HALF, 128), 1) < 64
    adds = []
    for i in range(HEAT_N):
        far = far_columns(side_ref[i])
        adds.append(fw * jnp.where(low_lanes, far[:HALF], far[HALF:]))
    add = jnp.concatenate(adds, axis=0)
    total = jnp.zeros_like(state)
    for _ in range(SUB):
        state = substep(state, add, weights)
        total = total + state
    t0, t1 = split(total)
    f0, f1 = split(flux_rows(flux_ref[...]))
    heat = dot_nt(f0, t0) + dot_nt(f0, t1) + dot_nt(f1, t0)
    for i in range(HEAT_N):
        heat_ref[i] = heat[:, HALF * i : HALF * i + HALF]


def home_heat(rows, radial_step, far_weights, flux_weights):
    steps = NT // HEAT_N
    return pl.pallas_call(
        heat_kernel,
        grid=(steps,),
        out_shape=(
            jax.ShapeDtypeStruct((NT, 8, HALF), F32),
            jax.ShapeDtypeStruct((256, 256), BF16),
        ),
        in_specs=[
            pl.BlockSpec((HEAT_N, HALF, 128), lambda d: (d, 0, 0)),
            pl.BlockSpec((HEAT_N, 8, 128), lambda d: (d, HALF // 8, 0)),
            pl.BlockSpec((PTS, PTS), lambda d: (0, 0)),
            pl.BlockSpec((1, PTS), lambda d: (0, 0)),
            pl.BlockSpec((1, PTS), lambda d: (0, 0)),
        ],
        out_specs=(
            pl.BlockSpec((HEAT_N, 8, HALF), lambda d: (d, 0, 0)),
            pl.BlockSpec((256, 256), lambda d: (0, 0)),
        ),
        compiler_params=pltpu.CompilerParams(vmem_limit_bytes=ROOM),
        cost_estimate=pl.CostEstimate(
            flops=25 * 10**8 * steps, bytes_accessed=steps << 20, transcendentals=steps << 21
        ),
        name="home_heat",
    )(rows, rows, radial_step, far_weights[None], flux_weights[None])


DEP_N = GROUP


def deposit_kernel(
    lanes_ref, heat_ref, cells_ref, vel_ref, dif_ref, flux_ref, below_ref, above_ref,
    out_ref, acc,
):
    d = pl.program_id(0)

    @pl.when(d == 0)
    def _():
        acc[...] = jnp.zeros_like(acc)

    one, nil = jnp.ones((), F32), jnp.zeros((), F32)
    width = DEP_N * MSG
    cols, rows, heats = [], [], []
    for i in range(DEP_N):
        nums = lanes_ref[i]
        heat = jnp.concatenate([heat_ref[i, 0:1], heat_ref[i, 1:2]], axis=1)
        cols.append(nums[0:1])
        rows.append(nums[1:2])
        heats.append(jnp.where(nums[3:4] > 0.5, 0.5 * heat, nil))
    col = jnp.concatenate(cols, axis=1).astype(I32)
    row = jnp.concatenate(rows, axis=1).astype(I32)
    heat = jnp.concatenate(heats, axis=1)
    high = heat.astype(BF16).astype(F32)
    here = col == iota((128, width), 0)
    spread = jnp.concatenate(
        [jnp.where(here, high, nil).astype(BF16), jnp.where(here, heat - high, nil).astype(BF16)], axis=0
    )
    hot = jnp.where(row == iota((ROWS, width), 0), one, nil).astype(BF16)
    acc[...] += dot_nt(hot, spread)

    @pl.when(d == NT // DEP_N - 1)
    def _():
        layers = ROWS // 64
        wall, lane = iota((64, 128), 0), iota((64, 128), 1)
        for x in range(layers):
            at = 64 * x
            h = cells_ref[at : at + 64]
            x_lower = cells_ref[at - 64 : at] if x else below_ref[...]
            x_upper = cells_ref[at + 64 : at + 128] if x < layers - 1 else above_ref[...]
            w_lower = jnp.where(wall == 0, h, pltpu.roll(h, 1, 0))
            w_upper = jnp.where(wall == 63, h, pltpu.roll(h, 63, 0))
            s_lower = jnp.where(lane == 0, nil, pltpu.roll(h, 1, 1))
            s_upper = jnp.where(lane == 127, nil, pltpu.roll(h, 127, 1))
            laplace = (x_lower + x_upper) + (w_lower + w_upper) + (s_lower + s_upper) - 6.0 * h
            new = h + dif_ref[at : at + 64] * laplace - vel_ref[at : at + 64] * (h - x_lower)
            new = new + jnp.where(wall == 0, flux_ref[x : x + 1], nil)
            out_ref[at : at + 64] = new + (acc[at : at + 64, :128] + acc[at : at + 64, 128:])


def deposit(lanes, heat, cells, velocity, diffusivity, wall_flux, below, above):
    def whole(shape):
        return pl.BlockSpec(shape, lambda d: (0, 0))

    field = whole((ROWS, 128))
    return pl.pallas_call(
        deposit_kernel,
        grid=(NT // DEP_N,),
        out_shape=jax.ShapeDtypeStruct((ROWS, 128), F32),
        in_specs=[
            pl.BlockSpec((DEP_N, 8, MSG), lambda d: (d, 0, 0)),
            pl.BlockSpec((DEP_N, 8, HALF), lambda d: (d, 0, 0)),
            field,
            field,
            field,
            whole((ROWS // 64, 128)),
            whole((64, 128)),
            whole((64, 128)),
        ],
        out_specs=field,
        scratch_shapes=[pltpu.VMEM((ROWS, 256), F32)],
        compiler_params=pltpu.CompilerParams(vmem_limit_bytes=ROOM),
        cost_estimate=pl.CostEstimate(flops=10**10, bytes_accessed=4 << 20, transcendentals=0),
        name="deposit",
    )(lanes, heat, cells, velocity, diffusivity, wall_flux, below, above)


def span_term(ends):
    row8, lane = iota((8, ROWS), 0), iota((8, 128), 1)
    terms = jnp.zeros((8, ROWS), F32)
    for i, rest in enumerate(ends):
        for k in range(3):
            high = rest.astype(BF16).astype(F32)
            terms = jnp.where(row8 == 3 * i + k, high, terms)
            rest = rest - high
    row = iota((8, 128), 0)
    first, last = (row < 3) & (lane == 0), (row >= 3) & (row < 6) & (lane == 127)
    pick = jnp.where(first | last, 1.0, 0.0).astype(BF16)
    return lax.dot_general(
        terms.astype(BF16), pick, (((0,), (0,)), ((), ())), preferred_element_type=F32
    )


SETTLE = 1024


def settle_kernel(
    rows_ref, fw_ref, weights_ref, new_ref, dif_ref, left_ref, right_ref, out_ref, field_ref,
    stage, comb, got, got_sem, side, side_sem, slot_v, slot_s, slot_sem, amount_v, amount_s, amount_sem,
    out_v, out_sem,
):
    fetch_side = pltpu.make_async_copy(rows_ref.at[:, pl.ds(HALF, 8)], side, side_sem)
    fetch_side.start()

    def fetch(g):
        part = pl.ds(g * GROUP, GROUP)
        return pltpu.make_async_copy(rows_ref.at[part, pl.ds(0, HALF)], got.at[part], got_sem.at[g])

    for g in range(NT // GROUP):
        fetch(g).start()
    field_ref[...] = new_ref[...] + dif_ref[...] * span_term((left_ref[...], right_ref[...]))
    fetch_side.wait()
    for t in range(NT):
        slot_v[4 * t : 4 * t + 4] = side[t, 0:4].astype(I32)
    valid = jnp.where(slot_v[...] < OWN, 1.0, 0.0).astype(BF16)
    by_row = dot(valid, jnp.ones((128, 128), BF16)).astype(BF16)
    of_sender = jnp.where(iota((NT, 128), 1) >> 2 == iota((NT, 128), 0), 1.0, 0.0).astype(BF16)
    amount_v[...] = dot(of_sender, by_row).astype(I32)
    copies = (
        pltpu.make_async_copy(slot_v, slot_s, slot_sem),
        pltpu.make_async_copy(amount_v, amount_s, amount_sem),
    )
    for copy in copies:
        copy.start()

    low_lanes = iota((HALF, 128), 1) < 64

    for g in range(NT // GROUP):
        fetch(g).wait()

    @pl.loop(0, NT // GROUP, unroll=2)
    def _(g):
        for k in range(GROUP):
            t = GROUP * g + k
            rows = got[t]
            col = far_columns(side[t])
            at = pl.multiple_of(t * MSG, MSG)
            comb[pl.ds(at, HALF)] = jnp.where(low_lanes, rows, col[:HALF])
            comb[pl.ds(pl.multiple_of(at + HALF, HALF), HALF)] = jnp.where(
                low_lanes, pltpu.roll(rows, 64, 1), col[HALF:]
            )

    for copy in copies:
        copy.wait()

    @pl.loop(0, NT)
    def _(t):
        amount = amount_s[t, 0]

        def move(r, lanes):
            row = 4 * t + r
            for lane in lanes:
                stage[pl.ds(slot_s[row, lane], 1)] = comb[pl.ds(row * 128 + lane, 1)]

        @pl.loop(0, amount >> 7)
        def _(r):
            move(r, range(128))

        last = amount >> 7
        for lane in range(0, 128, 32):

            @pl.when((amount & 127) > lane)
            def _():
                move(last, range(lane, lane + 32))

    weights = weights_ref[...]
    fw = twice(fw_ref[...])
    low_lanes = iota((SETTLE, 128), 1) < 64

    def send(c, h):
        part = pl.ds(c * SETTLE + h * OWN2, SETTLE)
        return pltpu.make_async_copy(out_v.at[:, part], out_ref.at[:, part], out_sem.at[2 * c + h])

    for c in range(OWN2 // SETTLE):
        at = c * SETTLE
        a = stage[at : at + SETTLE]
        b = stage[at + OWN2 : at + OWN2 + SETTLE]
        state = jnp.where(low_lanes, a, pltpu.roll(b, 64, 1))
        add = fw * jnp.where(low_lanes, pltpu.roll(a, 64, 1), b)
        for _ in range(SUB):
            state = substep(state, add, weights)
        for k in range(SETTLE // 128):
            turned = state[128 * k : 128 * k + 128].T
            out_v[:, at + 128 * k : at + 128 * k + 128] = turned[:64]
            out_v[:, at + OWN2 + 128 * k : at + OWN2 + 128 * k + 128] = turned[64:]
        for h in range(2):
            send(c, h).start()
    for c in range(OWN2 // SETTLE):
        for h in range(2):
            send(c, h).wait()


def settle(rows, far_weights, weights, new, diffusivity, left, right):
    vmem = pl.BlockSpec(memory_space=pltpu.VMEM)
    return pl.pallas_call(
        settle_kernel,
        out_shape=(jax.ShapeDtypeStruct((PTS, OWN), F32), jax.ShapeDtypeStruct((ROWS, 128), F32)),
        in_specs=[pl.BlockSpec(memory_space=pl.ANY)] + [vmem] * 6,
        out_specs=(pl.BlockSpec(memory_space=pl.ANY), vmem),
        scratch_shapes=[
            pltpu.VMEM((OWN + 8, 128), F32),
            pltpu.VMEM((NT * MSG, 128), F32),
            pltpu.VMEM((NT, HALF, 128), F32),
            pltpu.SemaphoreType.DMA((NT // GROUP,)),
            pltpu.VMEM((NT, 8, 128), F32),
            pltpu.SemaphoreType.DMA,
            pltpu.VMEM((128, 128), I32),
            pltpu.SMEM((128, 128), I32),
            pltpu.SemaphoreType.DMA,
            pltpu.VMEM((NT, 128), I32),
            pltpu.SMEM((NT, 128), I32),
            pltpu.SemaphoreType.DMA,
            pltpu.VMEM((PTS, OWN), F32),
            pltpu.SemaphoreType.DMA((2 * OWN2 // SETTLE,)),
        ],
        compiler_params=pltpu.CompilerParams(vmem_limit_bytes=ROOM),
        name="settle",
    )(rows, far_weights[None], weights, new, diffusivity, left, right)


def edges_of(cells, first, last):
    n_x, n_s = lax.axis_size("stream"), lax.axis_size("tile")
    up_x = [(i, i + 1) for i in range(n_x - 1)]
    down_x = [(i + 1, i) for i in range(n_x - 1)]
    up_s = [(i, (i + 1) % n_s) for i in range(n_s)]
    down_s = [((i + 1) % n_s, i) for i in range(n_s)]
    below = lax.ppermute(cells[-1], "stream", up_x)
    above = lax.ppermute(cells[0], "stream", down_x)
    left = lax.ppermute(last, "tile", up_s)
    right = lax.ppermute(first, "tile", down_s)
    return below, above, left, right


def on_device(
    enthalpy, velocity, diffusivity, wall_flux, profiles, counts, owners, cells,
    radial_step, far_weights, flux_weights,
):
    table = enthalpy.reshape(ROWS, 128)
    rows, lanes, first, last = route(counts, owners, cells, table, profiles)
    rows, radial_step, far_weights, flux_weights = lax.optimization_barrier(
        (rows, radial_step, far_weights, flux_weights)
    )
    got = lax.all_to_all(rows, "tile", split_axis=0, concat_axis=0, tiled=True)
    layers, first, last = lax.optimization_barrier((enthalpy, first, last))
    heat, weights = home_heat(rows, radial_step, far_weights, flux_weights)
    below, above, left, right = edges_of(layers, first, last)
    spread = diffusivity.reshape(ROWS, 128)
    new = deposit(lanes, heat, table, velocity.reshape(ROWS, 128), spread, wall_flux, below, above)
    new_profiles, field = settle(got, far_weights, weights, new, spread, left, right)
    new_enthalpy = field.reshape(enthalpy.shape)
    return new_enthalpy, new_profiles


def solution(mesh):
    return jax.shard_map(
        on_device,
        mesh=mesh,
        in_specs=(
            P("stream", None, "tile"),
            P("stream", None, "tile"),
            P("stream", None, "tile"),
            P("stream", "tile"),
            P(None, ("stream", "tile")),
            P(("stream", "tile")),
            P(("stream", "tile")),
            P(("stream", "tile")),
            P(),
            P(),
            P(),
        ),
        out_specs=(P("stream", None, "tile"), P(None, ("stream", "tile"))),
        check_vma=False,
    )
```

```python
import jax
import jax.numpy as jnp
from jax import lax
from jax.experimental import pallas as pl
from jax.experimental.pallas import tpu as pltpu
from jax.sharding import PartitionSpec as P

SUB = 16
PTS = 64
NT = 32
CAP = 16384
OWN = 6144
MSG = 512
HALF = MSG // 2
LOAD = HALF + 8
BLK = 256
NBLK = CAP // BLK
STRIDE = MSG + 16
ROWS = 1024
OWN2 = OWN // 2

GROUP = 4
ROOM = 60 * 2**20

F32, BF16, I32 = jnp.float32, jnp.bfloat16, jnp.int32
NTD = (((1,), (1,)), ((), ()))


def iota(shape, dim):
    return lax.broadcasted_iota(I32, shape, dim)


def split(x):
    high = x.astype(BF16)
    return high, (x - high.astype(F32)).astype(BF16)


def dot(a, b):
    return jnp.dot(a, b, preferred_element_type=F32)


def dot_nt(a, b):
    return lax.dot_general(a, b, NTD, preferred_element_type=F32)


def route_kernel(
    count_ref, owners_ref, cells_ref, field_ref, prof_ref,
    rows_ref, lanes_ref, first_ref, last_ref,
    pos_s, m0_s, m1_s, m2_s, m3_s, m4_s, sorted_a, sorted_b, sorted_c, sorted_d,
    bucket, tab_v, tab_s, sem, prof_v, prof_sem, pack_v, pack_sem, meta_v, table,
):
    count = count_ref[0]
    fetch = pltpu.make_async_copy(prof_ref, prof_v, prof_sem)
    fetch.start()

    def blocks(ref):
        x = ref[...].reshape(NBLK, 2, 128)
        return jnp.concatenate([x[:, 0], x[:, 1]], axis=1)

    slot = iota((NBLK, BLK), 0) * BLK + iota((NBLK, BLK), 1)
    owners = blocks(owners_ref)
    dest = jnp.floor((owners.astype(F32) + 0.5) * (1.0 / OWN)).astype(I32)
    within = owners - dest * OWN
    live = slot < count
    dest = jnp.where(live, dest, NT)
    cells = blocks(cells_ref)
    m0_s[...] = (cells & 127).astype(F32)
    m1_s[...] = ((cells >> 7) & 3).astype(F32)
    m2_s[...] = (cells >> 9).astype(F32)
    m3_s[...] = (within & 255).astype(F32)
    m4_s[...] = (within >> 8).astype(F32)

    sub, lane = iota((BLK, BLK), 0), iota((BLK, BLK), 1)
    one, nil = jnp.ones((), F32), jnp.zeros((), F32)
    before = jnp.where(sub < lane, one, nil).astype(BF16)
    same_block = (sub >> 5) == (lane >> 5)
    same_dest = (sub & 31) == (lane & 31)
    seg_left = jnp.where(same_block & (lane < sub), one, nil).astype(BF16)
    seg_right = jnp.where(same_block & (sub < lane), one, nil).astype(BF16)
    base_right = jnp.where(same_dest & ((sub >> 5) < (lane >> 5)), one, nil).astype(BF16)
    all_right = jnp.where(same_dest, one, nil).astype(BF16)
    ones_a = jnp.ones((8, BLK), BF16)
    ones_b = jnp.ones((BLK, 128), BF16)
    run = jnp.zeros((8, BLK), F32)
    longest = jnp.zeros((8, BLK), F32)
    for c in range(8):
        part = dest[8 * c : 8 * c + 8]
        hot = jnp.where(part[:, None, :] == iota((8, NT, BLK), 1), one, nil).reshape(BLK, BLK)
        hot_b = hot.astype(BF16)
        prefix = dot(hot_b, before)
        amount = dot(hot_b, ones_b)
        seg = dot(seg_left, amount.astype(BF16))
        seg2 = jnp.concatenate([seg, seg], axis=1)
        pos = jnp.sum((hot * (prefix + seg2)).reshape(8, NT, BLK), axis=1)
        pos_s[8 * c : 8 * c + 8] = jnp.where(live[8 * c : 8 * c + 8], pos, 511.0)
        amount_l = dot_nt(ones_a, hot_b)
        amount_lb = amount_l.astype(BF16)
        src = dot(amount_lb, seg_right)
        base = dot(amount_lb, base_right) + run
        run = run + dot(amount_lb, all_right)
        longest = jnp.maximum(longest, amount_l)
        most = amount_l
        for shift in (1, 2, 4, 8, 16):
            most = jnp.maximum(most, pltpu.roll(most, BLK - shift, 1))
        first = iota((8, BLK), 1) & 31
        row8 = iota((8, BLK), 0)
        packed = jnp.where(row8 == 0, src, nil)
        packed = jnp.where(row8 == 1, base + (first * STRIDE).astype(F32), packed)
        packed = jnp.where(row8 == 2, amount_l, packed)
        packed = jnp.where(row8 == 3, most, packed)
        packed = packed.astype(I32)
        tab_v[16 * c : 16 * c + 8] = packed[:, :128]
        tab_v[16 * c + 8 : 16 * c + 16] = packed[:, 128:]
    copy = pltpu.make_async_copy(tab_v, tab_s, sem)
    copy.start()
    short = jnp.max(longest) <= 8.0
    total = run

    zero8 = jnp.zeros((STRIDE, 128), F32)

    @pl.loop(0, NT)
    def _(d):
        bucket[pl.ds(pl.multiple_of(d * STRIDE, 8), STRIDE)] = zero8

    copy.wait()
    fetch.wait()

    meta_rest = jnp.zeros((56, BLK), BF16)
    low_rest = jnp.zeros((64, BLK), BF16)
    row8 = iota((8, BLK), 0)

    def sort_block(j, out):
        x = prof_v[:, pl.ds(pl.multiple_of(j * BLK, BLK), BLK)]
        high, low = split(x)
        meta = jnp.zeros((8, BLK), F32)
        for k, ref in enumerate((m0_s, m1_s, m2_s, m3_s, m4_s)):
            meta = jnp.where(row8 == k, ref[pl.ds(j, 1), :], meta)
        data = jnp.concatenate([high, meta.astype(BF16), meta_rest, low, low_rest], axis=0)
        place = pos_s[pl.ds(j, 1), :].astype(I32)
        perm = jnp.where(place == sub, one, nil).astype(BF16)
        got = dot_nt(perm, data)
        out[0:BLK] = got[:, :128] + got[:, 128:]

    def copy_block(p, c, inp):
        chunk, at = p * 8, c * NT
        most = tab_s[chunk + 3, at]

        @pl.when(most <= 8)
        def _():
            for d in range(NT):
                src = tab_s[chunk, at + d]
                dst = tab_s[chunk + 1, at + d]
                bucket[pl.ds(dst, 8)] = inp[pl.ds(src, 8)]

        @pl.when((most > 8) & (most <= 16))
        def _():
            for d in range(NT):
                src = tab_s[chunk, at + d]
                dst = tab_s[chunk + 1, at + d]
                bucket[pl.ds(dst, 16)] = inp[pl.ds(src, 16)]

        @pl.when(most > 16)
        def _():
            @pl.loop(0, NT)
            def _(d):
                src = tab_s[chunk, at + d]
                dst = tab_s[chunk + 1, at + d]

                @pl.loop(0, (tab_s[chunk + 2, at + d] + 7) >> 3)
                def _(k):
                    bucket[pl.ds(dst + 8 * k, 8)] = inp[pl.ds(src + 8 * k, 8)]

    def copy_short(p, c, inp):
        chunk, at = p * 8, c * NT
        for d in range(NT):
            src = tab_s[chunk, at + d]
            dst = tab_s[chunk + 1, at + d]
            bucket[pl.ds(dst, 8)] = inp[pl.ds(src, 8)]

    for ref in (sorted_a, sorted_b, sorted_c, sorted_d):
        ref[BLK:] = jnp.zeros((16, 128), F32)
    quads = (count + 4 * BLK - 1) // (4 * BLK)
    sort_block(0, sorted_a)
    sort_block(1, sorted_b)

    def quad(copy_any):
        @pl.loop(0, quads)
        def _(p):
            sort_block(4 * p + 2, sorted_c)
            copy_any(p, 0, sorted_a)
            sort_block(4 * p + 3, sorted_d)
            copy_any(p, 1, sorted_b)
            sort_block(jnp.minimum(4 * p + 4, NBLK - 1), sorted_a)
            copy_any(p, 2, sorted_c)
            sort_block(jnp.minimum(4 * p + 5, NBLK - 1), sorted_b)
            copy_any(p, 3, sorted_d)

    pl.when(short)(lambda: quad(copy_short))
    pl.when(jnp.logical_not(short))(lambda: quad(copy_block))

    low_lanes = iota((HALF, 128), 1) < 64
    r8, l8 = iota((8, 128), 0), iota((8, 128), 1)
    pick = jnp.where((r8 == 0) & (l8 == 64), one, nil)
    pick = jnp.where((r8 == 1) & (l8 == 65), one, pick)
    pick = jnp.where((r8 == 1) & (l8 == 66), 4.0 * one, pick)
    pick = jnp.where((r8 == 2) & (l8 == 67), one, pick)
    pick = jnp.where((r8 == 2) & (l8 == 68), 256.0 * one, pick)
    pick = pick.astype(BF16)
    rank = iota((8, MSG), 1)
    rank_row = iota((8, MSG), 0)
    lane_dest = iota((8, BLK), 1)

    def send(g):
        part = pl.ds(g * GROUP, GROUP)
        return pltpu.make_async_copy(pack_v.at[part], rows_ref.at[part], pack_sem.at[g])

    def pack(g):
        for k in range(GROUP):
            d = GROUP * g + k
            at = pl.multiple_of(d * STRIDE, 8)
            lo = bucket[pl.ds(at, HALF)]
            hi = bucket[pl.ds(pl.multiple_of(at + HALF, 8), HALF)]
            pack_v[d, 0:HALF] = jnp.where(low_lanes, lo, pltpu.roll(hi, 64, 1))
            meta_v[d] = jnp.where(low_lanes, pltpu.roll(lo, 64, 1), hi).astype(BF16)
            both = jnp.concatenate([lo, hi], axis=0).astype(BF16)
            nums = dot_nt(pick, both)
            mine = jnp.max(jnp.where(lane_dest == d, total, nil), axis=1, keepdims=True)
            valid = rank.astype(F32) < mine
            nums = jnp.where((rank_row == 2) & ~valid, float(OWN), nums)
            nums = jnp.where(rank_row == 3, jnp.where(valid, one, nil), nums)
            lanes_ref[d] = nums
            pack_v[d, HALF : HALF + 4] = jnp.concatenate(
                [nums[2:3, 128 * q : 128 * q + 128] for q in range(4)], axis=0
            )

    cells = field_ref[...].reshape(ROWS // 4, 4, 128)
    parts = [split(cells[:, q]) for q in range(4)]
    table[...] = jnp.concatenate([p[0] for p in parts] + [p[1] for p in parts], axis=1)
    m_rows = GROUP * HALF
    ones8 = jnp.ones((8, 256), BF16)
    place = iota((m_rows, 128), 1).astype(F32)

    def far(g):
        meta = meta_v[pl.ds(g * GROUP, GROUP)].reshape(m_rows, 128).astype(F32)
        for h in range(2):
            first = 0 if h == 0 else 64
            col = meta[:, first : first + 1] + 128.0 * meta[:, first + 1 : first + 2]
            col = jnp.broadcast_to(col, (m_rows, 128))
            row = jnp.broadcast_to(meta[:, first + 2 : first + 3], (m_rows, 128))
            hot = jnp.concatenate(
                [jnp.where(row == place + 128.0 * q, one, nil).astype(BF16) for q in range(2)], axis=1
            )
            val = dot(hot, table[...])
            got = jnp.zeros((m_rows, 128), F32)
            for q in range(4):
                both = val[:, 128 * q : 128 * q + 128] + val[:, 512 + 128 * q : 640 + 128 * q]
                got = jnp.where(col == place + 128.0 * q, both, got)
            v0, v1 = split(got)
            far_l = dot_nt(ones8, jnp.concatenate([v0, v1], axis=1))
            for i in range(GROUP):
                for q in range(2):
                    at = HALF * i + 128 * q
                    row_at = HALF + 4 + 2 * h + q
                    pack_v[GROUP * g + i, row_at : row_at + 1] = far_l[0:1, at : at + 128]

    pack(0)

    @pl.loop(0, NT // GROUP - 1)
    def _(g):
        far(g)
        pack(g + 1)
        send(g).start()

    far(NT // GROUP - 1)
    send(NT // GROUP - 1).start()
    pick = jnp.where((r8 == 0) & (l8 == 0), one, nil) + jnp.where((r8 == 1) & (l8 == 127), one, nil)
    pick = pick.astype(BF16)
    f0, f1 = split(field_ref[...])
    f2 = (field_ref[...] - f0.astype(F32) - f1.astype(F32)).astype(BF16)
    ends = dot_nt(pick, f0) + dot_nt(pick, f1) + dot_nt(pick, f2)
    first_ref[...] = ends[0:1]
    last_ref[...] = ends[1:2]
    for g in range(NT // GROUP):
        send(g).wait()


def route(counts, owners, cells, field, profiles):
    vmem = pl.BlockSpec(memory_space=pltpu.VMEM)
    anywhere = pl.BlockSpec(memory_space=pl.ANY)
    return pl.pallas_call(
        route_kernel,
        out_shape=(
            jax.ShapeDtypeStruct((NT, LOAD, 128), F32),
            jax.ShapeDtypeStruct((NT, 8, MSG), F32),
            jax.ShapeDtypeStruct((1, ROWS), F32),
            jax.ShapeDtypeStruct((1, ROWS), F32),
        ),
        in_specs=[pl.BlockSpec(memory_space=pltpu.SMEM), vmem, vmem, vmem, anywhere],
        out_specs=(anywhere, vmem, vmem, vmem),
        scratch_shapes=[pltpu.VMEM((NBLK, BLK), F32)] * 6
        + [pltpu.VMEM((BLK + 16, 128), F32)] * 4
        + [
            pltpu.VMEM((NT * STRIDE, 128), F32),
            pltpu.VMEM((128, 128), I32),
            pltpu.SMEM((128, 128), I32),
            pltpu.SemaphoreType.DMA,
            pltpu.VMEM((PTS, CAP), F32),
            pltpu.SemaphoreType.DMA,
            pltpu.VMEM((NT, LOAD, 128), F32),
            pltpu.SemaphoreType.DMA((NT // GROUP,)),
            pltpu.VMEM((NT, HALF, 128), BF16),
            pltpu.VMEM((ROWS // 4, 1024), BF16),
        ],
        compiler_params=pltpu.CompilerParams(vmem_limit_bytes=ROOM),
        name="route",
    )(counts, owners.reshape(128, 128), cells.reshape(128, 128), field, profiles)


def twice(row):
    return jnp.concatenate([row, row], axis=1)


def step_weights(radial_step):
    w0, w1 = split(radial_step.T)
    w0, w1 = w0.astype(F32), w1.astype(F32)
    nil = jnp.zeros((PTS, PTS), F32)
    half = jnp.concatenate(
        [
            jnp.concatenate([w0, nil, w1, nil], axis=1),
            jnp.concatenate([nil, w0, nil, w1], axis=1),
        ],
        axis=0,
    ).astype(BF16)
    return jnp.concatenate([half, half], axis=0)


def flux_rows(flux_weights):
    row, low = iota((8, 128), 0), iota((8, 128), 1) < 64
    mine = ((row == 0) & low) | ((row == 1) & jnp.logical_not(low))
    return jnp.where(mine, twice(flux_weights) / SUB, 0.0)


def substep(state, add, weights):
    s0, s1 = split(state)
    got = dot(jnp.concatenate([s0, s1], axis=1), weights)
    return (got[:, :128] + got[:, 128:]) + (add + 0.25 * jnp.tanh(state))


HEAT_N = 8


def far_columns(side):
    far = jnp.concatenate([side[4 + q : 5 + q] for q in range(4)], axis=1)
    rest = far - far.astype(BF16).astype(F32)
    row8 = iota((8, MSG), 0)
    terms = jnp.where(row8 == 0, far, jnp.where(row8 == 1, rest, 0.0)).astype(BF16)
    pick = jnp.where(iota((8, 128), 0) < 2, 1.0, 0.0).astype(BF16)
    return lax.dot_general(terms, pick, (((0,), (0,)), ((), ())), preferred_element_type=F32)


def heat_kernel(rows_ref, side_ref, radial_ref, fw_ref, flux_ref, heat_ref, weights_ref):
    @pl.when(pl.program_id(0) == 0)
    def _():
        weights_ref[...] = step_weights(radial_ref[...])

    weights = weights_ref[...]
    fw = twice(fw_ref[...])
    state = rows_ref[...].reshape(HEAT_N * HALF, 128)
    low_lanes = iota((HALF, 128), 1) < 64
    adds = []
    for i in range(HEAT_N):
        far = far_columns(side_ref[i])
        adds.append(fw * jnp.where(low_lanes, far[:HALF], far[HALF:]))
    add = jnp.concatenate(adds, axis=0)
    total = jnp.zeros_like(state)
    for _ in range(SUB):
        state = substep(state, add, weights)
        total = total + state
    t0, t1 = split(total)
    f0, f1 = split(flux_rows(flux_ref[...]))
    heat = dot_nt(f0, t0) + dot_nt(f0, t1) + dot_nt(f1, t0)
    for i in range(HEAT_N):
        heat_ref[i] = heat[:, HALF * i : HALF * i + HALF]


def home_heat(rows, radial_step, far_weights, flux_weights):
    steps = NT // HEAT_N
    return pl.pallas_call(
        heat_kernel,
        grid=(steps,),
        out_shape=(
            jax.ShapeDtypeStruct((NT, 8, HALF), F32),
            jax.ShapeDtypeStruct((256, 256), BF16),
        ),
        in_specs=[
            pl.BlockSpec((HEAT_N, HALF, 128), lambda d: (d, 0, 0)),
            pl.BlockSpec((HEAT_N, 8, 128), lambda d: (d, HALF // 8, 0)),
            pl.BlockSpec((PTS, PTS), lambda d: (0, 0)),
            pl.BlockSpec((1, PTS), lambda d: (0, 0)),
            pl.BlockSpec((1, PTS), lambda d: (0, 0)),
        ],
        out_specs=(
            pl.BlockSpec((HEAT_N, 8, HALF), lambda d: (d, 0, 0)),
            pl.BlockSpec((256, 256), lambda d: (0, 0)),
        ),
        compiler_params=pltpu.CompilerParams(vmem_limit_bytes=ROOM),
        cost_estimate=pl.CostEstimate(
            flops=25 * 10**8 * steps, bytes_accessed=steps << 20, transcendentals=steps << 21
        ),
        name="home_heat",
    )(rows, rows, radial_step, far_weights[None], flux_weights[None])


DEP_N = GROUP


def deposit_kernel(
    lanes_ref, heat_ref, cells_ref, vel_ref, dif_ref, flux_ref, below_ref, above_ref,
    out_ref, acc,
):
    d = pl.program_id(0)

    @pl.when(d == 0)
    def _():
        acc[...] = jnp.zeros_like(acc)

    one, nil = jnp.ones((), F32), jnp.zeros((), F32)
    width = DEP_N * MSG
    cols, rows, heats = [], [], []
    for i in range(DEP_N):
        nums = lanes_ref[i]
        heat = jnp.concatenate([heat_ref[i, 0:1], heat_ref[i, 1:2]], axis=1)
        cols.append(nums[0:1])
        rows.append(nums[1:2])
        heats.append(jnp.where(nums[3:4] > 0.5, 0.5 * heat, nil))
    col = jnp.concatenate(cols, axis=1).astype(I32)
    row = jnp.concatenate(rows, axis=1).astype(I32)
    heat = jnp.concatenate(heats, axis=1)
    high = heat.astype(BF16).astype(F32)
    here = col == iota((128, width), 0)
    spread = jnp.concatenate(
        [jnp.where(here, high, nil).astype(BF16), jnp.where(here, heat - high, nil).astype(BF16)], axis=0
    )
    hot = jnp.where(row == iota((ROWS, width), 0), one, nil).astype(BF16)
    acc[...] += dot_nt(hot, spread)

    @pl.when(d == NT // DEP_N - 1)
    def _():
        layers = ROWS // 64
        wall, lane = iota((64, 128), 0), iota((64, 128), 1)
        for x in range(layers):
            at = 64 * x
            h = cells_ref[at : at + 64]
            x_lower = cells_ref[at - 64 : at] if x else below_ref[...]
            x_upper = cells_ref[at + 64 : at + 128] if x < layers - 1 else above_ref[...]
            w_lower = jnp.where(wall == 0, h, pltpu.roll(h, 1, 0))
            w_upper = jnp.where(wall == 63, h, pltpu.roll(h, 63, 0))
            s_lower = jnp.where(lane == 0, nil, pltpu.roll(h, 1, 1))
            s_upper = jnp.where(lane == 127, nil, pltpu.roll(h, 127, 1))
            laplace = (x_lower + x_upper) + (w_lower + w_upper) + (s_lower + s_upper) - 6.0 * h
            new = h + dif_ref[at : at + 64] * laplace - vel_ref[at : at + 64] * (h - x_lower)
            new = new + jnp.where(wall == 0, flux_ref[x : x + 1], nil)
            out_ref[at : at + 64] = new + (acc[at : at + 64, :128] + acc[at : at + 64, 128:])


def deposit(lanes, heat, cells, velocity, diffusivity, wall_flux, below, above):
    def whole(shape):
        return pl.BlockSpec(shape, lambda d: (0, 0))

    field = whole((ROWS, 128))
    return pl.pallas_call(
        deposit_kernel,
        grid=(NT // DEP_N,),
        out_shape=jax.ShapeDtypeStruct((ROWS, 128), F32),
        in_specs=[
            pl.BlockSpec((DEP_N, 8, MSG), lambda d: (d, 0, 0)),
            pl.BlockSpec((DEP_N, 8, HALF), lambda d: (d, 0, 0)),
            field,
            field,
            field,
            whole((ROWS // 64, 128)),
            whole((64, 128)),
            whole((64, 128)),
        ],
        out_specs=field,
        scratch_shapes=[pltpu.VMEM((ROWS, 256), F32)],
        compiler_params=pltpu.CompilerParams(vmem_limit_bytes=40 * 2**20),
        cost_estimate=pl.CostEstimate(flops=10**10, bytes_accessed=4 << 20, transcendentals=0),
        name="deposit",
    )(lanes, heat, cells, velocity, diffusivity, wall_flux, below, above)


def span_term(ends):
    row8, lane = iota((8, ROWS), 0), iota((8, 128), 1)
    terms = jnp.zeros((8, ROWS), F32)
    for i, rest in enumerate(ends):
        for k in range(3):
            high = rest.astype(BF16).astype(F32)
            terms = jnp.where(row8 == 3 * i + k, high, terms)
            rest = rest - high
    row = iota((8, 128), 0)
    first, last = (row < 3) & (lane == 0), (row >= 3) & (row < 6) & (lane == 127)
    pick = jnp.where(first | last, 1.0, 0.0).astype(BF16)
    return lax.dot_general(
        terms.astype(BF16), pick, (((0,), (0,)), ((), ())), preferred_element_type=F32
    )


SETTLE = 1024


def settle_kernel(
    rows_ref, fw_ref, weights_ref, new_ref, dif_ref, left_ref, right_ref, out_ref, field_ref,
    stage, comb, got, got_sem, side, side_sem, slot_v, slot_s, slot_sem, amount_v, amount_s, amount_sem,
    out_v, out_sem,
):
    fetch_side = pltpu.make_async_copy(rows_ref.at[:, pl.ds(HALF, 8)], side, side_sem)
    fetch_side.start()

    def fetch(g):
        part = pl.ds(g * GROUP, GROUP)
        return pltpu.make_async_copy(rows_ref.at[part, pl.ds(0, HALF)], got.at[part], got_sem.at[g])

    for g in range(NT // GROUP):
        fetch(g).start()
    field_ref[...] = new_ref[...] + dif_ref[...] * span_term((left_ref[...], right_ref[...]))
    fetch_side.wait()
    for t in range(NT):
        slot_v[4 * t : 4 * t + 4] = side[t, 0:4].astype(I32)
    valid = jnp.where(slot_v[...] < OWN, 1.0, 0.0).astype(BF16)
    by_row = dot(valid, jnp.ones((128, 128), BF16)).astype(BF16)
    of_sender = jnp.where(iota((NT, 128), 1) >> 2 == iota((NT, 128), 0), 1.0, 0.0).astype(BF16)
    amount_v[...] = dot(of_sender, by_row).astype(I32)
    copies = (
        pltpu.make_async_copy(slot_v, slot_s, slot_sem),
        pltpu.make_async_copy(amount_v, amount_s, amount_sem),
    )
    for copy in copies:
        copy.start()

    low_lanes = iota((HALF, 128), 1) < 64

    for g in range(NT // GROUP):
        fetch(g).wait()

    @pl.loop(0, NT // GROUP, unroll=4)
    def _(g):
        for k in range(GROUP):
            t = GROUP * g + k
            rows = got[t]
            col = far_columns(side[t])
            at = pl.multiple_of(t * MSG, MSG)
            comb[pl.ds(at, HALF)] = jnp.where(low_lanes, rows, col[:HALF])
            comb[pl.ds(pl.multiple_of(at + HALF, HALF), HALF)] = jnp.where(
                low_lanes, pltpu.roll(rows, 64, 1), col[HALF:]
            )

    for copy in copies:
        copy.wait()

    @pl.loop(0, NT)
    def _(t):
        amount = amount_s[t, 0]

        def move(r, lanes):
            row = 4 * t + r
            for lane in lanes:
                stage[pl.ds(slot_s[row, lane], 1)] = comb[pl.ds(row * 128 + lane, 1)]

        @pl.loop(0, amount >> 7)
        def _(r):
            move(r, range(128))

        last = amount >> 7
        for lane in range(0, 128, 32):

            @pl.when((amount & 127) > lane)
            def _():
                move(last, range(lane, lane + 32))

    weights = weights_ref[...]
    fw = twice(fw_ref[...])
    low_lanes = iota((SETTLE, 128), 1) < 64

    def send(c, h):
        part = pl.ds(c * SETTLE + h * OWN2, SETTLE)
        return pltpu.make_async_copy(out_v.at[:, part], out_ref.at[:, part], out_sem.at[2 * c + h])

    for c in range(OWN2 // SETTLE):
        at = c * SETTLE
        a = stage[at : at + SETTLE]
        b = stage[at + OWN2 : at + OWN2 + SETTLE]
        state = jnp.where(low_lanes, a, pltpu.roll(b, 64, 1))
        add = fw * jnp.where(low_lanes, pltpu.roll(a, 64, 1), b)
        for _ in range(SUB):
            state = substep(state, add, weights)
        for k in range(SETTLE // 128):
            turned = state[128 * k : 128 * k + 128].T
            out_v[:, at + 128 * k : at + 128 * k + 128] = turned[:64]
            out_v[:, at + OWN2 + 128 * k : at + OWN2 + 128 * k + 128] = turned[64:]
        for h in range(2):
            send(c, h).start()
    for c in range(OWN2 // SETTLE):
        for h in range(2):
            send(c, h).wait()


def settle(rows, far_weights, weights, new, diffusivity, left, right):
    vmem = pl.BlockSpec(memory_space=pltpu.VMEM)
    return pl.pallas_call(
        settle_kernel,
        out_shape=(jax.ShapeDtypeStruct((PTS, OWN), F32), jax.ShapeDtypeStruct((ROWS, 128), F32)),
        in_specs=[pl.BlockSpec(memory_space=pl.ANY)] + [vmem] * 6,
        out_specs=(pl.BlockSpec(memory_space=pl.ANY), vmem),
        scratch_shapes=[
            pltpu.VMEM((OWN + 8, 128), F32),
            pltpu.VMEM((NT * MSG, 128), F32),
            pltpu.VMEM((NT, HALF, 128), F32),
            pltpu.SemaphoreType.DMA((NT // GROUP,)),
            pltpu.VMEM((NT, 8, 128), F32),
            pltpu.SemaphoreType.DMA,
            pltpu.VMEM((128, 128), I32),
            pltpu.SMEM((128, 128), I32),
            pltpu.SemaphoreType.DMA,
            pltpu.VMEM((NT, 128), I32),
            pltpu.SMEM((NT, 128), I32),
            pltpu.SemaphoreType.DMA,
            pltpu.VMEM((PTS, OWN), F32),
            pltpu.SemaphoreType.DMA((2 * OWN2 // SETTLE,)),
        ],
        compiler_params=pltpu.CompilerParams(vmem_limit_bytes=ROOM),
        name="settle",
    )(rows, far_weights[None], weights, new, diffusivity, left, right)


def edges_of(cells, first, last):
    n_x, n_s = lax.axis_size("stream"), lax.axis_size("tile")
    up_x = [(i, i + 1) for i in range(n_x - 1)]
    down_x = [(i + 1, i) for i in range(n_x - 1)]
    up_s = [(i, (i + 1) % n_s) for i in range(n_s)]
    down_s = [((i + 1) % n_s, i) for i in range(n_s)]
    below = lax.ppermute(cells[-1], "stream", up_x)
    above = lax.ppermute(cells[0], "stream", down_x)
    left = lax.ppermute(last, "tile", up_s)
    right = lax.ppermute(first, "tile", down_s)
    return below, above, left, right


def on_device(
    enthalpy, velocity, diffusivity, wall_flux, profiles, counts, owners, cells,
    radial_step, far_weights, flux_weights,
):
    table = enthalpy.reshape(ROWS, 128)
    rows, lanes, first, last = route(counts, owners, cells, table, profiles)
    rows, radial_step, far_weights, flux_weights = lax.optimization_barrier(
        (rows, radial_step, far_weights, flux_weights)
    )
    got = lax.all_to_all(rows, "tile", split_axis=0, concat_axis=0, tiled=True)
    layers, first, last = lax.optimization_barrier((enthalpy, first, last))
    heat, weights = home_heat(rows, radial_step, far_weights, flux_weights)
    below, above, left, right = edges_of(layers, first, last)
    spread = diffusivity.reshape(ROWS, 128)
    new = deposit(lanes, heat, table, velocity.reshape(ROWS, 128), spread, wall_flux, below, above)
    new_profiles, field = settle(got, far_weights, weights, new, spread, left, right)
    new_enthalpy = field.reshape(enthalpy.shape)
    return new_enthalpy, new_profiles


def solution(mesh):
    return jax.shard_map(
        on_device,
        mesh=mesh,
        in_specs=(
            P("stream", None, "tile"),
            P("stream", None, "tile"),
            P("stream", None, "tile"),
            P("stream", "tile"),
            P(None, ("stream", "tile")),
            P(("stream", "tile")),
            P(("stream", "tile")),
            P(("stream", "tile")),
            P(),
            P(),
            P(),
        ),
        out_specs=(P("stream", None, "tile"), P(None, ("stream", "tile"))),
        check_vma=False,
    )
```

```python
import jax
import jax.numpy as jnp
from jax import lax
from jax.experimental import pallas as pl
from jax.experimental.pallas import tpu as pltpu
from jax.sharding import PartitionSpec as P

SUB = 16
PTS = 64
NT = 32
CAP = 16384
OWN = 6144
MSG = 512
HALF = MSG // 2
LOAD = HALF + 8
BLK = 256
NBLK = CAP // BLK
STRIDE = MSG + 16
ROWS = 1024
OWN2 = OWN // 2

GROUP = 4
ROOM = 60 * 2**20

F32, BF16, I32 = jnp.float32, jnp.bfloat16, jnp.int32
NTD = (((1,), (1,)), ((), ()))


def iota(shape, dim):
    return lax.broadcasted_iota(I32, shape, dim)


def split(x):
    high = x.astype(BF16)
    return high, (x - high.astype(F32)).astype(BF16)


def dot(a, b):
    return jnp.dot(a, b, preferred_element_type=F32)


def dot_nt(a, b):
    return lax.dot_general(a, b, NTD, preferred_element_type=F32)


def route_kernel(
    count_ref, owners_ref, cells_ref, field_ref, prof_ref,
    rows_ref, lanes_ref, first_ref, last_ref,
    pos_s, m0_s, m1_s, m2_s, m3_s, m4_s, sorted_a, sorted_b, sorted_c, sorted_d,
    bucket, tab_v, tab_s, sem, prof_v, prof_sem, pack_v, pack_sem, meta_v, table,
):
    count = count_ref[0]
    fetch = pltpu.make_async_copy(prof_ref, prof_v, prof_sem)
    fetch.start()

    def blocks(ref):
        x = ref[...].reshape(NBLK, 2, 128)
        return jnp.concatenate([x[:, 0], x[:, 1]], axis=1)

    slot = iota((NBLK, BLK), 0) * BLK + iota((NBLK, BLK), 1)
    owners = blocks(owners_ref)
    dest = jnp.floor((owners.astype(F32) + 0.5) * (1.0 / OWN)).astype(I32)
    within = owners - dest * OWN
    live = slot < count
    dest = jnp.where(live, dest, NT)
    cells = blocks(cells_ref)
    m0_s[...] = (cells & 127).astype(F32)
    m1_s[...] = ((cells >> 7) & 3).astype(F32)
    m2_s[...] = (cells >> 9).astype(F32)
    m3_s[...] = (within & 255).astype(F32)
    m4_s[...] = (within >> 8).astype(F32)

    sub, lane = iota((BLK, BLK), 0), iota((BLK, BLK), 1)
    one, nil = jnp.ones((), F32), jnp.zeros((), F32)
    before = jnp.where(sub < lane, one, nil).astype(BF16)
    same_block = (sub >> 5) == (lane >> 5)
    same_dest = (sub & 31) == (lane & 31)
    seg_left = jnp.where(same_block & (lane < sub), one, nil).astype(BF16)
    seg_right = jnp.where(same_block & (sub < lane), one, nil).astype(BF16)
    base_right = jnp.where(same_dest & ((sub >> 5) < (lane >> 5)), one, nil).astype(BF16)
    all_right = jnp.where(same_dest, one, nil).astype(BF16)
    ones_a = jnp.ones((8, BLK), BF16)
    ones_b = jnp.ones((BLK, 128), BF16)
    run = jnp.zeros((8, BLK), F32)
    longest = jnp.zeros((8, BLK), F32)
    for c in range(8):
        part = dest[8 * c : 8 * c + 8]
        hot = jnp.where(part[:, None, :] == iota((8, NT, BLK), 1), one, nil).reshape(BLK, BLK)
        hot_b = hot.astype(BF16)
        prefix = dot(hot_b, before)
        amount = dot(hot_b, ones_b)
        seg = dot(seg_left, amount.astype(BF16))
        seg2 = jnp.concatenate([seg, seg], axis=1)
        pos = jnp.sum((hot * (prefix + seg2)).reshape(8, NT, BLK), axis=1)
        pos_s[8 * c : 8 * c + 8] = jnp.where(live[8 * c : 8 * c + 8], pos, 511.0)
        amount_l = dot_nt(ones_a, hot_b)
        amount_lb = amount_l.astype(BF16)
        src = dot(amount_lb, seg_right)
        base = dot(amount_lb, base_right) + run
        run = run + dot(amount_lb, all_right)
        longest = jnp.maximum(longest, amount_l)
        most = amount_l
        for shift in (1, 2, 4, 8, 16):
            most = jnp.maximum(most, pltpu.roll(most, BLK - shift, 1))
        first = iota((8, BLK), 1) & 31
        row8 = iota((8, BLK), 0)
        packed = jnp.where(row8 == 0, src, nil)
        packed = jnp.where(row8 == 1, base + (first * STRIDE).astype(F32), packed)
        packed = jnp.where(row8 == 2, amount_l, packed)
        packed = jnp.where(row8 == 3, most, packed)
        packed = packed.astype(I32)
        tab_v[16 * c : 16 * c + 8] = packed[:, :128]
        tab_v[16 * c + 8 : 16 * c + 16] = packed[:, 128:]
    copy = pltpu.make_async_copy(tab_v, tab_s, sem)
    copy.start()
    short = jnp.max(longest) <= 8.0
    total = run

    zero8 = jnp.zeros((STRIDE, 128), F32)

    @pl.loop(0, NT)
    def _(d):
        bucket[pl.ds(pl.multiple_of(d * STRIDE, 8), STRIDE)] = zero8

    copy.wait()
    fetch.wait()

    meta_rest = jnp.zeros((56, BLK), BF16)
    low_rest = jnp.zeros((64, BLK), BF16)
    row8 = iota((8, BLK), 0)

    def sort_block(j, out):
        x = prof_v[:, pl.ds(pl.multiple_of(j * BLK, BLK), BLK)]
        high, low = split(x)
        meta = jnp.zeros((8, BLK), F32)
        for k, ref in enumerate((m0_s, m1_s, m2_s, m3_s, m4_s)):
            meta = jnp.where(row8 == k, ref[pl.ds(j, 1), :], meta)
        data = jnp.concatenate([high, meta.astype(BF16), meta_rest, low, low_rest], axis=0)
        place = pos_s[pl.ds(j, 1), :].astype(I32)
        perm = jnp.where(place == sub, one, nil).astype(BF16)
        got = dot_nt(perm, data)
        out[0:BLK] = got[:, :128] + got[:, 128:]

    def copy_block(p, c, inp):
        chunk, at = p * 8, c * NT
        most = tab_s[chunk + 3, at]

        @pl.when(most <= 8)
        def _():
            for d in range(NT):
                src = tab_s[chunk, at + d]
                dst = tab_s[chunk + 1, at + d]
                bucket[pl.ds(dst, 8)] = inp[pl.ds(src, 8)]

        @pl.when((most > 8) & (most <= 16))
        def _():
            for d in range(NT):
                src = tab_s[chunk, at + d]
                dst = tab_s[chunk + 1, at + d]
                bucket[pl.ds(dst, 16)] = inp[pl.ds(src, 16)]

        @pl.when(most > 16)
        def _():
            @pl.loop(0, NT)
            def _(d):
                src = tab_s[chunk, at + d]
                dst = tab_s[chunk + 1, at + d]

                @pl.loop(0, (tab_s[chunk + 2, at + d] + 7) >> 3)
                def _(k):
                    bucket[pl.ds(dst + 8 * k, 8)] = inp[pl.ds(src + 8 * k, 8)]

    def copy_short(p, c, inp):
        chunk, at = p * 8, c * NT
        for d in range(NT):
            src = tab_s[chunk, at + d]
            dst = tab_s[chunk + 1, at + d]
            bucket[pl.ds(dst, 8)] = inp[pl.ds(src, 8)]

    for ref in (sorted_a, sorted_b, sorted_c, sorted_d):
        ref[BLK:] = jnp.zeros((16, 128), F32)
    quads = (count + 4 * BLK - 1) // (4 * BLK)
    sort_block(0, sorted_a)
    sort_block(1, sorted_b)

    def quad(copy_any):
        @pl.loop(0, quads)
        def _(p):
            sort_block(4 * p + 2, sorted_c)
            copy_any(p, 0, sorted_a)
            sort_block(4 * p + 3, sorted_d)
            copy_any(p, 1, sorted_b)
            sort_block(jnp.minimum(4 * p + 4, NBLK - 1), sorted_a)
            copy_any(p, 2, sorted_c)
            sort_block(jnp.minimum(4 * p + 5, NBLK - 1), sorted_b)
            copy_any(p, 3, sorted_d)

    pl.when(short)(lambda: quad(copy_short))
    pl.when(jnp.logical_not(short))(lambda: quad(copy_block))

    low_lanes = iota((HALF, 128), 1) < 64
    r8, l8 = iota((8, 128), 0), iota((8, 128), 1)
    pick = jnp.where((r8 == 0) & (l8 == 64), one, nil)
    pick = jnp.where((r8 == 1) & (l8 == 65), one, pick)
    pick = jnp.where((r8 == 1) & (l8 == 66), 4.0 * one, pick)
    pick = jnp.where((r8 == 2) & (l8 == 67), one, pick)
    pick = jnp.where((r8 == 2) & (l8 == 68), 256.0 * one, pick)
    pick = pick.astype(BF16)
    rank = iota((8, MSG), 1)
    rank_row = iota((8, MSG), 0)
    lane_dest = iota((8, BLK), 1)

    def send(g):
        part = pl.ds(g * GROUP, GROUP)
        return pltpu.make_async_copy(pack_v.at[part], rows_ref.at[part], pack_sem.at[g])

    def pack(g):
        for k in range(GROUP):
            d = GROUP * g + k
            at = pl.multiple_of(d * STRIDE, 8)
            lo = bucket[pl.ds(at, HALF)]
            hi = bucket[pl.ds(pl.multiple_of(at + HALF, 8), HALF)]
            pack_v[d, 0:HALF] = jnp.where(low_lanes, lo, pltpu.roll(hi, 64, 1))
            meta_v[d] = jnp.where(low_lanes, pltpu.roll(lo, 64, 1), hi).astype(BF16)
            both = jnp.concatenate([lo, hi], axis=0).astype(BF16)
            nums = dot_nt(pick, both)
            mine = jnp.max(jnp.where(lane_dest == d, total, nil), axis=1, keepdims=True)
            valid = rank.astype(F32) < mine
            nums = jnp.where((rank_row == 2) & ~valid, float(OWN), nums)
            nums = jnp.where(rank_row == 3, jnp.where(valid, one, nil), nums)
            lanes_ref[d] = nums
            pack_v[d, HALF : HALF + 4] = jnp.concatenate(
                [nums[2:3, 128 * q : 128 * q + 128] for q in range(4)], axis=0
            )

    cells = field_ref[...].reshape(ROWS // 4, 4, 128)
    parts = [split(cells[:, q]) for q in range(4)]
    table[...] = jnp.concatenate([p[0] for p in parts] + [p[1] for p in parts], axis=1)
    m_rows = GROUP * HALF
    ones8 = jnp.ones((8, 256), BF16)
    place = iota((m_rows, 128), 1).astype(F32)

    def far(g):
        meta = meta_v[pl.ds(g * GROUP, GROUP)].reshape(m_rows, 128).astype(F32)
        for h in range(2):
            first = 0 if h == 0 else 64
            col = meta[:, first : first + 1] + 128.0 * meta[:, first + 1 : first + 2]
            col = jnp.broadcast_to(col, (m_rows, 128))
            row = jnp.broadcast_to(meta[:, first + 2 : first + 3], (m_rows, 128))
            hot = jnp.concatenate(
                [jnp.where(row == place + 128.0 * q, one, nil).astype(BF16) for q in range(2)], axis=1
            )
            val = dot(hot, table[...])
            got = jnp.zeros((m_rows, 128), F32)
            for q in range(4):
                both = val[:, 128 * q : 128 * q + 128] + val[:, 512 + 128 * q : 640 + 128 * q]
                got = jnp.where(col == place + 128.0 * q, both, got)
            v0, v1 = split(got)
            far_l = dot_nt(ones8, jnp.concatenate([v0, v1], axis=1))
            for i in range(GROUP):
                for q in range(2):
                    at = HALF * i + 128 * q
                    row_at = HALF + 4 + 2 * h + q
                    pack_v[GROUP * g + i, row_at : row_at + 1] = far_l[0:1, at : at + 128]

    pack(0)

    @pl.loop(0, NT // GROUP - 1)
    def _(g):
        far(g)
        pack(g + 1)
        send(g).start()

    far(NT // GROUP - 1)
    send(NT // GROUP - 1).start()
    pick = jnp.where((r8 == 0) & (l8 == 0), one, nil) + jnp.where((r8 == 1) & (l8 == 127), one, nil)
    pick = pick.astype(BF16)
    f0, f1 = split(field_ref[...])
    f2 = (field_ref[...] - f0.astype(F32) - f1.astype(F32)).astype(BF16)
    ends = dot_nt(pick, f0) + dot_nt(pick, f1) + dot_nt(pick, f2)
    first_ref[...] = ends[0:1]
    last_ref[...] = ends[1:2]
    for g in range(NT // GROUP):
        send(g).wait()


def route(counts, owners, cells, field, profiles):
    vmem = pl.BlockSpec(memory_space=pltpu.VMEM)
    anywhere = pl.BlockSpec(memory_space=pl.ANY)
    return pl.pallas_call(
        route_kernel,
        out_shape=(
            jax.ShapeDtypeStruct((NT, LOAD, 128), F32),
            jax.ShapeDtypeStruct((NT, 8, MSG), F32),
            jax.ShapeDtypeStruct((1, ROWS), F32),
            jax.ShapeDtypeStruct((1, ROWS), F32),
        ),
        in_specs=[pl.BlockSpec(memory_space=pltpu.SMEM), vmem, vmem, vmem, anywhere],
        out_specs=(anywhere, vmem, vmem, vmem),
        scratch_shapes=[pltpu.VMEM((NBLK, BLK), F32)] * 6
        + [pltpu.VMEM((BLK + 16, 128), F32)] * 4
        + [
            pltpu.VMEM((NT * STRIDE, 128), F32),
            pltpu.VMEM((128, 128), I32),
            pltpu.SMEM((128, 128), I32),
            pltpu.SemaphoreType.DMA,
            pltpu.VMEM((PTS, CAP), F32),
            pltpu.SemaphoreType.DMA,
            pltpu.VMEM((NT, LOAD, 128), F32),
            pltpu.SemaphoreType.DMA((NT // GROUP,)),
            pltpu.VMEM((NT, HALF, 128), BF16),
            pltpu.VMEM((ROWS // 4, 1024), BF16),
        ],
        compiler_params=pltpu.CompilerParams(vmem_limit_bytes=ROOM),
        name="route",
    )(counts, owners.reshape(128, 128), cells.reshape(128, 128), field, profiles)


def twice(row):
    return jnp.concatenate([row, row], axis=1)


def step_weights(radial_step):
    w0, w1 = split(radial_step.T)
    w0, w1 = w0.astype(F32), w1.astype(F32)
    nil = jnp.zeros((PTS, PTS), F32)
    half = jnp.concatenate(
        [
            jnp.concatenate([w0, nil, w1, nil], axis=1),
            jnp.concatenate([nil, w0, nil, w1], axis=1),
        ],
        axis=0,
    ).astype(BF16)
    return jnp.concatenate([half, half], axis=0)


def flux_rows(flux_weights):
    row, low = iota((8, 128), 0), iota((8, 128), 1) < 64
    mine = ((row == 0) & low) | ((row == 1) & jnp.logical_not(low))
    return jnp.where(mine, twice(flux_weights) / SUB, 0.0)


def substep(state, add, weights):
    s0, s1 = split(state)
    got = dot(jnp.concatenate([s0, s1], axis=1), weights)
    return (got[:, :128] + got[:, 128:]) + (add + 0.25 * jnp.tanh(state))


HEAT_N = 8


def far_columns(side):
    far = jnp.concatenate([side[4 + q : 5 + q] for q in range(4)], axis=1)
    rest = far - far.astype(BF16).astype(F32)
    row8 = iota((8, MSG), 0)
    terms = jnp.where(row8 == 0, far, jnp.where(row8 == 1, rest, 0.0)).astype(BF16)
    pick = jnp.where(iota((8, 128), 0) < 2, 1.0, 0.0).astype(BF16)
    return lax.dot_general(terms, pick, (((0,), (0,)), ((), ())), preferred_element_type=F32)


def heat_kernel(rows_ref, side_ref, radial_ref, fw_ref, flux_ref, heat_ref, weights_ref):
    @pl.when(pl.program_id(0) == 0)
    def _():
        weights_ref[...] = step_weights(radial_ref[...])

    weights = weights_ref[...]
    fw = twice(fw_ref[...])
    state = rows_ref[...].reshape(HEAT_N * HALF, 128)
    low_lanes = iota((HALF, 128), 1) < 64
    adds = []
    for i in range(HEAT_N):
        far = far_columns(side_ref[i])
        adds.append(fw * jnp.where(low_lanes, far[:HALF], far[HALF:]))
    add = jnp.concatenate(adds, axis=0)
    total = jnp.zeros_like(state)
    for _ in range(SUB):
        state = substep(state, add, weights)
        total = total + state
    t0, t1 = split(total)
    f0, f1 = split(flux_rows(flux_ref[...]))
    heat = dot_nt(f0, t0) + dot_nt(f0, t1) + dot_nt(f1, t0)
    for i in range(HEAT_N):
        heat_ref[i] = heat[:, HALF * i : HALF * i + HALF]


def home_heat(rows, radial_step, far_weights, flux_weights):
    steps = NT // HEAT_N
    return pl.pallas_call(
        heat_kernel,
        grid=(steps,),
        out_shape=(
            jax.ShapeDtypeStruct((NT, 8, HALF), F32),
            jax.ShapeDtypeStruct((256, 256), BF16),
        ),
        in_specs=[
            pl.BlockSpec((HEAT_N, HALF, 128), lambda d: (d, 0, 0)),
            pl.BlockSpec((HEAT_N, 8, 128), lambda d: (d, HALF // 8, 0)),
            pl.BlockSpec((PTS, PTS), lambda d: (0, 0)),
            pl.BlockSpec((1, PTS), lambda d: (0, 0)),
            pl.BlockSpec((1, PTS), lambda d: (0, 0)),
        ],
        out_specs=(
            pl.BlockSpec((HEAT_N, 8, HALF), lambda d: (d, 0, 0)),
            pl.BlockSpec((256, 256), lambda d: (0, 0)),
        ),
        compiler_params=pltpu.CompilerParams(vmem_limit_bytes=ROOM),
        cost_estimate=pl.CostEstimate(
            flops=25 * 10**8 * steps, bytes_accessed=steps << 20, transcendentals=steps << 21
        ),
        name="home_heat",
    )(rows, rows, radial_step, far_weights[None], flux_weights[None])


DEP_N = GROUP


def deposit_kernel(
    lanes_ref, heat_ref, cells_ref, vel_ref, dif_ref, flux_ref, below_ref, above_ref,
    out_ref, acc,
):
    d = pl.program_id(0)

    @pl.when(d == 0)
    def _():
        acc[...] = jnp.zeros_like(acc)

    one, nil = jnp.ones((), F32), jnp.zeros((), F32)
    width = DEP_N * MSG
    cols, rows, heats = [], [], []
    for i in range(DEP_N):
        nums = lanes_ref[i]
        heat = jnp.concatenate([heat_ref[i, 0:1], heat_ref[i, 1:2]], axis=1)
        cols.append(nums[0:1])
        rows.append(nums[1:2])
        heats.append(jnp.where(nums[3:4] > 0.5, 0.5 * heat, nil))
    col = jnp.concatenate(cols, axis=1).astype(I32)
    row = jnp.concatenate(rows, axis=1).astype(I32)
    heat = jnp.concatenate(heats, axis=1)
    high = heat.astype(BF16).astype(F32)
    here = col == iota((128, width), 0)
    spread = jnp.concatenate(
        [jnp.where(here, high, nil).astype(BF16), jnp.where(here, heat - high, nil).astype(BF16)], axis=0
    )
    hot = jnp.where(row == iota((ROWS, width), 0), one, nil).astype(BF16)
    acc[...] += dot_nt(hot, spread)

    @pl.when(d == NT // DEP_N - 1)
    def _():
        layers = ROWS // 64
        wall, lane = iota((64, 128), 0), iota((64, 128), 1)
        for x in range(layers):
            at = 64 * x
            h = cells_ref[at : at + 64]
            x_lower = cells_ref[at - 64 : at] if x else below_ref[...]
            x_upper = cells_ref[at + 64 : at + 128] if x < layers - 1 else above_ref[...]
            w_lower = jnp.where(wall == 0, h, pltpu.roll(h, 1, 0))
            w_upper = jnp.where(wall == 63, h, pltpu.roll(h, 63, 0))
            s_lower = jnp.where(lane == 0, nil, pltpu.roll(h, 1, 1))
            s_upper = jnp.where(lane == 127, nil, pltpu.roll(h, 127, 1))
            laplace = (x_lower + x_upper) + (w_lower + w_upper) + (s_lower + s_upper) - 6.0 * h
            new = h + dif_ref[at : at + 64] * laplace - vel_ref[at : at + 64] * (h - x_lower)
            new = new + jnp.where(wall == 0, flux_ref[x : x + 1], nil)
            out_ref[at : at + 64] = new + (acc[at : at + 64, :128] + acc[at : at + 64, 128:])


def deposit(lanes, heat, cells, velocity, diffusivity, wall_flux, below, above):
    def whole(shape):
        return pl.BlockSpec(shape, lambda d: (0, 0))

    field = whole((ROWS, 128))
    return pl.pallas_call(
        deposit_kernel,
        grid=(NT // DEP_N,),
        out_shape=jax.ShapeDtypeStruct((ROWS, 128), F32),
        in_specs=[
            pl.BlockSpec((DEP_N, 8, MSG), lambda d: (d, 0, 0)),
            pl.BlockSpec((DEP_N, 8, HALF), lambda d: (d, 0, 0)),
            field,
            field,
            field,
            whole((ROWS // 64, 128)),
            whole((64, 128)),
            whole((64, 128)),
        ],
        out_specs=field,
        scratch_shapes=[pltpu.VMEM((ROWS, 256), F32)],
        compiler_params=pltpu.CompilerParams(vmem_limit_bytes=40 * 2**20),
        cost_estimate=pl.CostEstimate(flops=10**10, bytes_accessed=4 << 20, transcendentals=0),
        name="deposit",
    )(lanes, heat, cells, velocity, diffusivity, wall_flux, below, above)


def span_term(ends):
    row8, lane = iota((8, ROWS), 0), iota((8, 128), 1)
    terms = jnp.zeros((8, ROWS), F32)
    for i, rest in enumerate(ends):
        for k in range(3):
            high = rest.astype(BF16).astype(F32)
            terms = jnp.where(row8 == 3 * i + k, high, terms)
            rest = rest - high
    row = iota((8, 128), 0)
    first, last = (row < 3) & (lane == 0), (row >= 3) & (row < 6) & (lane == 127)
    pick = jnp.where(first | last, 1.0, 0.0).astype(BF16)
    return lax.dot_general(
        terms.astype(BF16), pick, (((0,), (0,)), ((), ())), preferred_element_type=F32
    )


SETTLE = 1536


def settle_kernel(
    rows_ref, fw_ref, weights_ref, new_ref, dif_ref, left_ref, right_ref, out_ref, field_ref,
    stage, comb, got, got_sem, side, side_sem, slot_v, slot_s, slot_sem, amount_v, amount_s, amount_sem,
    out_v, out_sem,
):
    fetch_side = pltpu.make_async_copy(rows_ref.at[:, pl.ds(HALF, 8)], side, side_sem)
    fetch_side.start()

    def fetch(g):
        part = pl.ds(g * GROUP, GROUP)
        return pltpu.make_async_copy(rows_ref.at[part, pl.ds(0, HALF)], got.at[part], got_sem.at[g])

    for g in range(NT // GROUP):
        fetch(g).start()
    field_ref[...] = new_ref[...] + dif_ref[...] * span_term((left_ref[...], right_ref[...]))
    fetch_side.wait()
    for t in range(NT):
        slot_v[4 * t : 4 * t + 4] = side[t, 0:4].astype(I32)
    valid = jnp.where(slot_v[...] < OWN, 1.0, 0.0).astype(BF16)
    by_row = dot(valid, jnp.ones((128, 128), BF16)).astype(BF16)
    of_sender = jnp.where(iota((NT, 128), 1) >> 2 == iota((NT, 128), 0), 1.0, 0.0).astype(BF16)
    amount_v[...] = dot(of_sender, by_row).astype(I32)
    copies = (
        pltpu.make_async_copy(slot_v, slot_s, slot_sem),
        pltpu.make_async_copy(amount_v, amount_s, amount_sem),
    )
    for copy in copies:
        copy.start()

    low_lanes = iota((HALF, 128), 1) < 64

    for g in range(NT // GROUP):
        fetch(g).wait()

    @pl.loop(0, NT // GROUP, unroll=4)
    def _(g):
        for k in range(GROUP):
            t = GROUP * g + k
            rows = got[t]
            col = far_columns(side[t])
            at = pl.multiple_of(t * MSG, MSG)
            comb[pl.ds(at, HALF)] = jnp.where(low_lanes, rows, col[:HALF])
            comb[pl.ds(pl.multiple_of(at + HALF, HALF), HALF)] = jnp.where(
                low_lanes, pltpu.roll(rows, 64, 1), col[HALF:]
            )

    for copy in copies:
        copy.wait()

    @pl.loop(0, NT)
    def _(t):
        amount = amount_s[t, 0]

        def move(r, lanes):
            row = 4 * t + r
            for lane in lanes:
                stage[pl.ds(slot_s[row, lane], 1)] = comb[pl.ds(row * 128 + lane, 1)]

        @pl.loop(0, amount >> 7)
        def _(r):
            move(r, range(128))

        last = amount >> 7
        for lane in range(0, 128, 32):

            @pl.when((amount & 127) > lane)
            def _():
                move(last, range(lane, lane + 32))

    weights = weights_ref[...]
    fw = twice(fw_ref[...])
    low_lanes = iota((SETTLE, 128), 1) < 64

    def send(c, h):
        part = pl.ds(c * SETTLE + h * OWN2, SETTLE)
        return pltpu.make_async_copy(out_v.at[:, part], out_ref.at[:, part], out_sem.at[2 * c + h])

    for c in range(OWN2 // SETTLE):
        at = c * SETTLE
        a = stage[at : at + SETTLE]
        b = stage[at + OWN2 : at + OWN2 + SETTLE]
        state = jnp.where(low_lanes, a, pltpu.roll(b, 64, 1))
        add = fw * jnp.where(low_lanes, pltpu.roll(a, 64, 1), b)
        for _ in range(SUB):
            state = substep(state, add, weights)
        for k in range(SETTLE // 128):
            turned = state[128 * k : 128 * k + 128].T
            out_v[:, at + 128 * k : at + 128 * k + 128] = turned[:64]
            out_v[:, at + OWN2 + 128 * k : at + OWN2 + 128 * k + 128] = turned[64:]
        for h in range(2):
            send(c, h).start()
    for c in range(OWN2 // SETTLE):
        for h in range(2):
            send(c, h).wait()


def settle(rows, far_weights, weights, new, diffusivity, left, right):
    vmem = pl.BlockSpec(memory_space=pltpu.VMEM)
    return pl.pallas_call(
        settle_kernel,
        out_shape=(jax.ShapeDtypeStruct((PTS, OWN), F32), jax.ShapeDtypeStruct((ROWS, 128), F32)),
        in_specs=[pl.BlockSpec(memory_space=pl.ANY)] + [vmem] * 6,
        out_specs=(pl.BlockSpec(memory_space=pl.ANY), vmem),
        scratch_shapes=[
            pltpu.VMEM((OWN + 8, 128), F32),
            pltpu.VMEM((NT * MSG, 128), F32),
            pltpu.VMEM((NT, HALF, 128), F32),
            pltpu.SemaphoreType.DMA((NT // GROUP,)),
            pltpu.VMEM((NT, 8, 128), F32),
            pltpu.SemaphoreType.DMA,
            pltpu.VMEM((128, 128), I32),
            pltpu.SMEM((128, 128), I32),
            pltpu.SemaphoreType.DMA,
            pltpu.VMEM((NT, 128), I32),
            pltpu.SMEM((NT, 128), I32),
            pltpu.SemaphoreType.DMA,
            pltpu.VMEM((PTS, OWN), F32),
            pltpu.SemaphoreType.DMA((2 * OWN2 // SETTLE,)),
        ],
        compiler_params=pltpu.CompilerParams(vmem_limit_bytes=ROOM),
        name="settle",
    )(rows, far_weights[None], weights, new, diffusivity, left, right)


def edges_of(cells, first, last):
    n_x, n_s = lax.axis_size("stream"), lax.axis_size("tile")
    up_x = [(i, i + 1) for i in range(n_x - 1)]
    down_x = [(i + 1, i) for i in range(n_x - 1)]
    up_s = [(i, (i + 1) % n_s) for i in range(n_s)]
    down_s = [((i + 1) % n_s, i) for i in range(n_s)]
    below = lax.ppermute(cells[-1], "stream", up_x)
    above = lax.ppermute(cells[0], "stream", down_x)
    left = lax.ppermute(last, "tile", up_s)
    right = lax.ppermute(first, "tile", down_s)
    return below, above, left, right


def on_device(
    enthalpy, velocity, diffusivity, wall_flux, profiles, counts, owners, cells,
    radial_step, far_weights, flux_weights,
):
    table = enthalpy.reshape(ROWS, 128)
    rows, lanes, first, last = route(counts, owners, cells, table, profiles)
    rows, radial_step, far_weights, flux_weights = lax.optimization_barrier(
        (rows, radial_step, far_weights, flux_weights)
    )
    got = lax.all_to_all(rows, "tile", split_axis=0, concat_axis=0, tiled=True)
    layers, first, last = lax.optimization_barrier((enthalpy, first, last))
    heat, weights = home_heat(rows, radial_step, far_weights, flux_weights)
    below, above, left, right = edges_of(layers, first, last)
    spread = diffusivity.reshape(ROWS, 128)
    new = deposit(lanes, heat, table, velocity.reshape(ROWS, 128), spread, wall_flux, below, above)
    new_profiles, field = settle(got, far_weights, weights, new, spread, left, right)
    new_enthalpy = field.reshape(enthalpy.shape)
    return new_enthalpy, new_profiles


def solution(mesh):
    return jax.shard_map(
        on_device,
        mesh=mesh,
        in_specs=(
            P("stream", None, "tile"),
            P("stream", None, "tile"),
            P("stream", None, "tile"),
            P("stream", "tile"),
            P(None, ("stream", "tile")),
            P(("stream", "tile")),
            P(("stream", "tile")),
            P(("stream", "tile")),
            P(),
            P(),
            P(),
        ),
        out_specs=(P("stream", None, "tile"), P(None, ("stream", "tile"))),
        check_vma=False,
    )
```
